32 devices in a mesh: row: 4 (over y, x), col: 8 (over z, core).
Axes of the slice: x: 2, y: 2, z: 4, core: 2. Of those that a mesh axis runs over, the one named last changes fastest.
Arguments:
- inputs: bfloat16 [2048, 2048], P('row', 'col'), may hold values from -6 to 6
- query_weight: bfloat16 [2048, 2048], P('row', 'col'), may hold values from -4 to 4
- key_weight: bfloat16 [2048, 2048], P('row', 'col'), may hold values from -4 to 4
- value_weight: bfloat16 [2048, 2048], P('row', 'col'), may hold values from -0.125 to 0.125
- output_weight: bfloat16 [2048, 2048], P('row', 'col'), may hold values from -4 to 4
- gate_weight: bfloat16 [2048, 8192], P('row', 'col'), may hold values from -0.125 to 0.125
- up_weight: bfloat16 [2048, 8192], P('row', 'col'), may hold values from -0.125 to 0.125
- down_weight: bfloat16 [2048, 8192], P('row', 'col'), may hold values from -4 to 4
- query_gain: float32 [2048], replicated, may hold values from 0.5 to 4.5
- key_gain: float32 [2048], replicated, may hold values from 0.5 to 4.5
- attn_gain: float32 [2048], replicated, may hold values from 0.25 to 1.75
- mlp_gain: float32 [2048], replicated, may hold values from 0.25 to 1.75
- positions: int32 [2048], P('row'), may hold values from 0 to 511, as said below
- segments: int32 [2048], P('row'), may hold values from 0 to 2047, as said below
- cotangent: bfloat16 [2048, 2048], P('row', 'col'), may hold values from -18 to 18
Outputs:
- layer_out: bfloat16 [2048, 2048], P('row', 'col')
- grad_inputs: float32 [2048, 2048], P('row', 'col')
- grad_query: float32 [2048, 2048], P('row', 'col')
- grad_key: float32 [2048, 2048], P('row', 'col')
- grad_value: float32 [2048, 2048], P('row', 'col')
- grad_output: float32 [2048, 2048], P('row', 'col')
- grad_gate: float32 [2048, 8192], P('row', 'col')
- grad_up: float32 [2048, 8192], P('row', 'col')
- grad_down: float32 [2048, 8192], P('row', 'col')
- grad_query_gain: float32 [2048], P('col')
- grad_key_gain: float32 [2048], P('col')
- grad_attn_gain: float32 [2048], P('col')
- grad_mlp_gain: float32 [2048], P('col')
The draws below stay inside these ranges and needn't reach their ends.
Inputs may be any that keep to these rules, and one draw needn't show every extreme that they name: `segments`: A token's segment number is the index of its segment's first token, so numbers never fall; every sequence of 512 tokens begins a new segment; the first sequence is one segment; the last token is a segment of its own. `positions`: A token's position is the number of earlier tokens of its segment.
All inputs are finite; a program needn't handle non-finite values.
Results may differ from the reference program's by a relative error of at most 0.015.
Values may be sent and summed in bfloat16 or wider, within the bound.
A program may use at most 192 MiB of HBM per device.

```python
import math
import jax
import jax.numpy as jnp
from jax import lax

D = 2048
H = 16
HD = 128
FF = 8192
LENGTH = 512
TOK_DEV = 512
TOKENS = 2048
N_ROW = 4


def column_ramp(count, spread):
    return spread ** (jnp.arange(count, dtype=jnp.float32) / max(count - 1, 1) - 0.5)


def clipped_normal(key, shape):
    return jnp.clip(jax.random.normal(key, shape, jnp.float32), -6.0, 6.0)


def shared_query(key):
    return clipped_normal(jax.random.fold_in(key, 101), (D, D)) * D ** (-0.5)


def draw_query_weight(key, part):
    spread = 3.0
    return (shared_query(key) * column_ramp(D, spread)[None, :]).astype(jnp.bfloat16)


def draw_key_weight(key, part):
    own = clipped_normal(jax.random.fold_in(key, 102), (D, D)) * D ** (-0.5)
    mixed = own
    spread = 3.0
    return (mixed * column_ramp(D, spread)[None, :]).astype(jnp.bfloat16)


def draw_output_weight(key, part):
    spread = 3.0
    values = clipped_normal(jax.random.fold_in(key, 103), (D, D)) * D ** (-0.5)
    return (values * column_ramp(D, spread)[:, None]).astype(jnp.bfloat16)


def draw_down_weight(key, part):
    spread = 3.0
    values = clipped_normal(jax.random.fold_in(key, 104), (D, FF)) * FF ** (-0.5)
    return (values * column_ramp(D, spread)[:, None]).astype(jnp.bfloat16)


def draw_query_gain(key, part):
    values = jax.random.uniform(jax.random.fold_in(key, 105), (D,), jnp.float32, 0.5, 1.5)
    return values


def draw_key_gain(key, part):
    values = jax.random.uniform(jax.random.fold_in(key, 106), (D,), jnp.float32, 0.5, 1.5)
    return values


def document_layout(key):
    places = jnp.arange(TOKENS, dtype=jnp.int32)
    starts = jax.random.randint(jax.random.fold_in(key, 107), (TOKENS,), 0, max(LENGTH // 4, 2)) == 0
    starts = jnp.where(places < LENGTH, False, starts)
    starts = jnp.where(places % LENGTH == 0, True, starts)
    starts = jnp.where(places == TOKENS - 1, True, starts)
    starts = starts.astype(jnp.int32)
    first = lax.cummax(starts * places, axis=0)
    return (first.astype(jnp.int32), (places - first).astype(jnp.int32))


def draw_segments(key, part):
    return document_layout(key)[0]


def draw_positions(key, part):
    return document_layout(key)[1]


def draw_cotangent(key, part):
    spread = 3.0
    noise = clipped_normal(jax.random.fold_in(key, 108), (TOKENS, D))
    return (noise * column_ramp(TOKENS, spread)[:, None]).astype(jnp.bfloat16)


def shard_levels(own_key, shape, pieces, least, top_value):
    gain, own = 1.0, jax.random.fold_in(own_key, 6)
    for axis_at, parts in pieces:
        draws = jnp.exp(jax.random.uniform(jax.random.fold_in(own, axis_at), (parts,), jnp.float32, least / len(pieces), top_value / len(pieces)))
        gain = gain * jnp.repeat(draws, shape[axis_at] // parts).reshape([-1 if axis == axis_at else 1 for axis in range(len(shape))])
    return gain


def normal_values(stream_key, shape, scale, bound, split=(), kind=jnp.bfloat16):
    drawn = jax.random.normal(stream_key, shape, jnp.float32) * scale
    if len(split) > 0:
        drawn = shard_levels(stream_key, shape, split, -0.22, 0.18) * drawn
    return jnp.clip(drawn, min=-bound, max=bound).astype(kind)


def setup_inputs(seed: int = 0) -> dict:
    keys = jax.random.split(jax.random.key(seed), 16)
    inputs = normal_values(keys[0], (TOKENS, D), 1.0, 6.0, ((0, 4), (1, 8)))
    query_weight = draw_query_weight(jax.random.fold_in(keys[15], 71), 0)
    key_weight = draw_key_weight(jax.random.fold_in(keys[15], 71), 0)
    value_weight = normal_values(keys[3], (D, D), D ** -0.5, 0.125, ((0, 4), (1, 8)))
    output_weight = draw_output_weight(jax.random.fold_in(keys[15], 71), 0)
    gate_weight = normal_values(keys[5], (D, FF), D ** -0.5, 0.125, ((0, 4), (1, 8)))
    up_weight = normal_values(keys[6], (D, FF), D ** -0.5, 0.125, ((0, 4), (1, 8)))
    down_weight = draw_down_weight(jax.random.fold_in(keys[15], 71), 0)
    query_gain = draw_query_gain(jax.random.fold_in(keys[15], 71), 0)
    key_gain = draw_key_gain(jax.random.fold_in(keys[15], 71), 0)
    attn_gain = jnp.clip(1.0 + 0.15 * jax.random.normal(keys[10], (D,), jnp.float32), 0.25, 1.75)
    mlp_gain = jnp.clip(1.0 + 0.15 * jax.random.normal(keys[11], (D,), jnp.float32), 0.25, 1.75)
    positions = draw_positions(jax.random.fold_in(keys[15], 71), 0)
    segments = draw_segments(jax.random.fold_in(keys[15], 71), 0)
    cotangent = draw_cotangent(jax.random.fold_in(keys[15], 71), 0)
    return {"inputs": inputs, "query_weight": query_weight, "key_weight": key_weight, "value_weight": value_weight, "output_weight": output_weight, "gate_weight": gate_weight, "up_weight": up_weight, "down_weight": down_weight, "query_gain": query_gain, "key_gain": key_gain, "attn_gain": attn_gain, "mlp_gain": mlp_gain, "positions": positions, "segments": segments, "cotangent": cotangent}


@jax.custom_vjp
def low(v):
    return lax.optimization_barrier(v.astype(jnp.bfloat16)).astype(jnp.float32)

@jax.custom_vjp
def low_back(v):
    return v

def low_keep(v):
    return (low(v), None)

def low_pass(kept, grad):
    return (grad,)

def back_keep(v):
    return (v, None)

def back_low(kept, grad):
    return (low(grad),)
low.defvjp(low_keep, low_pass)
low_back.defvjp(back_keep, back_low)
EPS = 1e-06
THETA = 500000.0
MASKED = -1e+30

def matmul(left, right):
    return jnp.dot(left, right, precision=lax.Precision.HIGHEST, preferred_element_type=jnp.float32)

def inverse_rms(values):
    return lax.rsqrt(lax.optimization_barrier(jnp.mean(values * values, axis=-1, keepdims=True)) + EPS)

def rope_tables(positions):
    halfway = HD // 2
    frequency = jnp.exp(jnp.arange(halfway, dtype=jnp.float32) * (-2.0 * math.log(THETA) / HD))
    angles = positions.astype(jnp.float32)[:, None] * frequency[None, :]
    return (jnp.cos(angles)[:, None, :], jnp.sin(angles)[:, None, :])

def rotate(values, cosine, sine):
    halfway = values.shape[-1] // 2
    first_half = values[..., :halfway]
    second_half = values[..., halfway:]
    return jnp.concatenate([first_half * cosine - second_half * sine, second_half * cosine + first_half * sine], axis=-1)

def attend(block):
    queries, keys_part, values_part, segment_part = block
    scores = jnp.einsum('qhd,khd->hqk', queries, keys_part, precision=lax.Precision.HIGHEST, preferred_element_type=jnp.float32)
    scores = low_back(scores)
    places = jnp.arange(LENGTH)
    allowed = (segment_part[:, None] == segment_part[None, :]) & (places[:, None] >= places[None, :])
    scores = jnp.where(allowed[None], scores, MASKED)
    probs = low(jax.nn.softmax(scores, axis=-1))
    return jnp.einsum('hqk,khd->qhd', probs, values_part, precision=lax.Precision.HIGHEST, preferred_element_type=jnp.float32)

def layer(inputs, query_w, key_w, value_w, output_w, gate_w, up_w, down_w, query_g, key_g, attn_g, mlp_g, cosine, sine, segment):
    rows = inputs.shape[0]
    sequences = rows // LENGTH
    scale = HD ** (-0.5)
    query = low_back(matmul(inputs, query_w))
    key_raw = low_back(matmul(inputs, key_w))
    value = low(low_back(matmul(inputs, value_w)))
    query_norm = query * inverse_rms(query) * query_g
    key_norm = key_raw * inverse_rms(key_raw) * key_g
    query_rot = low(rotate(query_norm.reshape(rows, H, HD), cosine, sine) * scale)
    key_rot = low(rotate(key_norm.reshape(rows, H, HD), cosine, sine))
    shape_seq = (sequences, LENGTH, H, HD)
    attended = lax.map(jax.checkpoint(attend), (query_rot.reshape(shape_seq), key_rot.reshape(shape_seq), value.reshape(shape_seq), segment.reshape(sequences, LENGTH)))
    attended = low(low_back(attended.reshape(rows, D)))
    branch = low_back(matmul(attended, output_w.T))
    middle = inputs + branch * inverse_rms(branch) * attn_g
    middle_low = low(middle)
    gate = low_back(matmul(middle_low, gate_w))
    upper = low_back(matmul(middle_low, up_w))
    mixed = low(jax.nn.silu(gate) * upper)
    ffn = low_back(matmul(mixed, down_w.T))
    return middle + ffn * inverse_rms(ffn) * mlp_g

def reference(inputs, query_weight, key_weight, value_weight, output_weight, gate_weight, up_weight, down_weight, query_gain, key_gain, attn_gain, mlp_gain, positions, segments, cotangent):
    cosine, sine = rope_tables(positions)
    halfway = HD // 2

    def whole(xvals, query_w, key_w, value_w, output_w, gate_w, up_w, down_w, query_g, key_g, attn_g, mlp_g):

        def group(carry, block):
            xpart, cos_part, sin_part, seg_part = block
            result = jax.checkpoint(layer)(xpart, query_w, key_w, value_w, output_w, gate_w, up_w, down_w, query_g, key_g, attn_g, mlp_g, cos_part, sin_part, seg_part)
            return (carry, result)
        blocks = (xvals.reshape(N_ROW, TOK_DEV, D), cosine.reshape(N_ROW, TOK_DEV, 1, halfway), sine.reshape(N_ROW, TOK_DEV, 1, halfway), segments.reshape(N_ROW, TOK_DEV))
        _, outcome = lax.scan(group, jnp.zeros((), jnp.float32), blocks)
        return outcome.reshape(TOKENS, D)
    primals = (inputs.astype(jnp.float32), query_weight.astype(jnp.float32), key_weight.astype(jnp.float32), value_weight.astype(jnp.float32), output_weight.astype(jnp.float32), gate_weight.astype(jnp.float32), up_weight.astype(jnp.float32), down_weight.astype(jnp.float32), query_gain.astype(jnp.float32), key_gain.astype(jnp.float32), attn_gain.astype(jnp.float32), mlp_gain.astype(jnp.float32))
    outcome, pullback = jax.vjp(whole, *primals)
    grads = pullback(cotangent.astype(jnp.float32))
    return (outcome.astype(jnp.bfloat16), grads[0], grads[1], grads[2], grads[3], grads[4], grads[5], grads[6], grads[7], grads[8], grads[9], grads[10], grads[11])
```

```python
import math

import jax
import jax.numpy as jnp
from jax import lax
from jax.experimental import pallas as pl
from jax.experimental.pallas import tpu as pltpu
from jax.sharding import PartitionSpec as P

HD = 128
LENGTH = 512


EPS = 1e-06
THETA = 500000.0
MASKED = -1e30


def rope_tables(positions, head_size):
    halfway = head_size // 2
    frequency = jnp.exp(
        jnp.arange(halfway, dtype=jnp.float32) * (-2.0 * math.log(THETA) / head_size)
    )
    angles = positions.astype(jnp.float32)[:, None] * frequency[None, :]
    return (jnp.cos(angles)[:, None, :], jnp.sin(angles)[:, None, :])


def rotate(values, cosine, sine):
    halfway = values.shape[-1] // 2
    first_half = values[..., :halfway]
    second_half = values[..., halfway:]
    return jnp.concatenate(
        [first_half * cosine - second_half * sine, second_half * cosine + first_half * sine],
        axis=-1,
    )


def matmul(left, right):
    return jnp.dot(left, right, preferred_element_type=jnp.float32)


def cross_rows(left, right):
    return lax.dot_general(
        left, right, (((0,), (0,)), ((), ())), preferred_element_type=jnp.float32
    )


def cross_cols(left, right):
    return lax.dot_general(
        left, right, (((1,), (1,)), ((), ())), preferred_element_type=jnp.float32
    )


def visible_pairs(segment_part):
    places = jnp.arange(segment_part.shape[0])
    return (segment_part[:, None] == segment_part[None, :]) & (places[:, None] >= places[None, :])


def on_device(
    inputs,
    query_weight,
    key_weight,
    value_weight,
    output_weight,
    gate_weight,
    up_weight,
    down_weight,
    query_gain,
    key_gain,
    attn_gain,
    mlp_gain,
    positions,
    segments,
    cotangent,
):
    bfloat = jnp.bfloat16
    floats = jnp.float32
    rows = inputs.shape[0]
    local_width = inputs.shape[1]
    width = local_width * lax.axis_size("col")
    offset = lax.axis_index("col") * local_width
    head_size = HD
    heads_here = local_width // head_size
    sequences = rows // LENGTH
    scale = head_size ** (-0.5)
    shape_seq = (sequences, LENGTH, heads_here, head_size)

    def mine(values):
        return lax.dynamic_slice_in_dim(values, offset, local_width, values.ndim - 1)

    query_gain_here = mine(query_gain)
    key_gain_here = mine(key_gain)
    cot_here = cotangent.astype(floats)
    gathered = (
        lax.all_gather(query_weight, "row", axis=0, tiled=True),
        lax.all_gather(key_weight, "row", axis=0, tiled=True),
        lax.all_gather(value_weight, "row", axis=0, tiled=True),
        lax.all_gather(gate_weight, "row", axis=0, tiled=True),
        lax.all_gather(up_weight, "row", axis=0, tiled=True),
        lax.all_gather(output_weight, "row", axis=0, tiled=True),
        lax.all_gather(down_weight, "row", axis=0, tiled=True),
    )
    query_full, key_full, value_full, gate_full, up_full, output_full, down_full = gathered
    whole_in = lax.all_gather(inputs, "col", axis=1, tiled=True)
    query_raw = matmul(whole_in, query_full)
    key_raw = matmul(whole_in, key_full)
    value_raw = matmul(whole_in, value_full)
    query_total, key_total = lax.psum(
        (jnp.sum(query_raw * query_raw, axis=1), jnp.sum(key_raw * key_raw, axis=1)), "col"
    )
    query_scale = lax.rsqrt(query_total / width + EPS)[:, None]
    key_scale = lax.rsqrt(key_total / width + EPS)[:, None]
    query_hat = query_raw * query_scale
    key_hat = key_raw * key_scale
    cosine, sine = rope_tables(positions, head_size)
    query_low = (
        rotate((query_hat * query_gain_here).reshape(rows, heads_here, head_size), cosine, sine)
        * scale
    ).astype(bfloat)
    key_low = rotate(
        (key_hat * key_gain_here).reshape(rows, heads_here, head_size), cosine, sine
    ).astype(bfloat)
    value_low = value_raw.astype(bfloat).reshape(rows, heads_here, head_size)
    query_blocks = query_low.reshape(shape_seq)
    key_blocks = key_low.reshape(shape_seq)
    value_blocks = value_low.reshape(shape_seq)
    segment_blocks = segments.reshape(sequences, LENGTH)

    def attend(block):
        queries, keys_part, values_part, segment_part = block
        scores = jnp.einsum("qhd,khd->hqk", queries, keys_part, preferred_element_type=floats)
        scores = jnp.where(visible_pairs(segment_part)[None], scores, MASKED)
        largest = jnp.max(scores, axis=-1, keepdims=True)
        exponent = jnp.exp(scores - largest)
        totals = jnp.sum(exponent, axis=-1, keepdims=True)
        weights_low = (exponent / totals).astype(bfloat)
        attended_part = jnp.einsum(
            "hqk,khd->qhd", weights_low, values_part, preferred_element_type=floats
        )
        return (attended_part, (largest + jnp.log(totals))[..., 0])

    attended, log_totals = lax.map(attend, (query_blocks, key_blocks, value_blocks, segment_blocks))
    attended_low = attended.reshape(rows, local_width).astype(bfloat)
    branch = lax.psum(cross_cols(attended_low, output_full), "col")
    branch_scale = lax.rsqrt(jnp.mean(branch * branch, axis=1, keepdims=True) + EPS)
    branch_hat = branch * branch_scale
    middle = whole_in.astype(floats) + branch_hat * attn_gain
    middle_low = middle.astype(bfloat)
    middle_here = mine(middle)
    branch_hat_here = mine(branch_hat)
    gate_pre = matmul(middle_low, gate_full)
    up_pre = matmul(middle_low, up_full)
    sigma = jax.nn.sigmoid(gate_pre)
    silu_gate = gate_pre * sigma
    mixed_low = (silu_gate * up_pre).astype(bfloat)
    ffn = lax.psum(cross_cols(mixed_low, down_full), "col")
    ffn_scale = lax.rsqrt(jnp.mean(ffn * ffn, axis=1, keepdims=True) + EPS)
    ffn_hat = ffn * ffn_scale
    ffn_hat_here = mine(ffn_hat)
    grad_top = lax.all_gather(cotangent, "col", axis=1, tiled=True).astype(floats)
    normed_top = grad_top * mlp_gain
    inner_top = jnp.sum(normed_top * ffn_hat, axis=1, keepdims=True)
    grad_ffn_low = (ffn_scale * (normed_top - ffn_hat * inner_top / width)).astype(bfloat)
    layer_out = (middle_here + ffn_hat_here * mine(mlp_gain)).astype(bfloat)
    grad_mlp_gain = jnp.sum(cot_here * ffn_hat_here, axis=0)
    grad_down = cross_rows(grad_ffn_low, mixed_low)
    grad_mixed = matmul(grad_ffn_low, down_full)
    grad_gate_low = (grad_mixed * up_pre * sigma * (1.0 + gate_pre * (1.0 - sigma))).astype(bfloat)
    grad_up_low = (grad_mixed * silu_gate).astype(bfloat)
    grad_middle_part = cross_cols(grad_gate_low, gate_full) + cross_cols(grad_up_low, up_full)
    grad_gate = cross_rows(middle_low, grad_gate_low)
    grad_up = cross_rows(middle_low, grad_up_low)
    grad_middle = grad_top + lax.psum(grad_middle_part, "col")
    grad_middle_here = mine(grad_middle)
    grad_attn_gain = jnp.sum(grad_middle_here * branch_hat_here, axis=0)
    normed_mid = grad_middle * attn_gain
    inner_mid = jnp.sum(normed_mid * branch_hat, axis=1, keepdims=True)
    grad_branch_low = (branch_scale * (normed_mid - branch_hat * inner_mid / width)).astype(bfloat)
    grad_output = cross_rows(grad_branch_low, attended_low)
    grad_attended_low = matmul(grad_branch_low, output_full).astype(bfloat)

    def attend_back(block):
        queries, keys_part, values_part, segment_part, log_part, grad_part = block
        scores = jnp.einsum("qhd,khd->hqk", queries, keys_part, preferred_element_type=floats)
        scores = jnp.where(visible_pairs(segment_part)[None], scores, MASKED)
        probs = jnp.exp(scores - log_part[..., None])
        grad_values = jnp.einsum(
            "hqk,qhd->khd", probs.astype(bfloat), grad_part, preferred_element_type=floats
        )
        grad_probs = jnp.einsum(
            "qhd,khd->hqk", grad_part, values_part, preferred_element_type=floats
        )
        grad_scores = probs * (grad_probs - jnp.sum(probs * grad_probs, axis=-1, keepdims=True))
        scores_low = grad_scores.astype(bfloat)
        grad_queries = jnp.einsum(
            "hqk,khd->qhd", scores_low, keys_part, preferred_element_type=floats
        )
        grad_keys = jnp.einsum("hqk,qhd->khd", scores_low, queries, preferred_element_type=floats)
        return (grad_queries, grad_keys, grad_values.astype(bfloat))

    grad_queries, grad_keys, grad_values = lax.map(
        attend_back,
        (
            query_blocks,
            key_blocks,
            value_blocks,
            segment_blocks,
            log_totals,
            grad_attended_low.reshape(shape_seq),
        ),
    )
    grad_query_norm = rotate(
        grad_queries.reshape(rows, heads_here, head_size) * scale, cosine, -sine
    ).reshape(rows, local_width)
    grad_key_norm = rotate(grad_keys.reshape(rows, heads_here, head_size), cosine, -sine).reshape(
        rows, local_width
    )
    grad_query_gain = jnp.sum(grad_query_norm * query_hat, axis=0)
    grad_key_gain = jnp.sum(grad_key_norm * key_hat, axis=0)
    normed_query = grad_query_norm * query_gain_here
    normed_key = grad_key_norm * key_gain_here
    inner_query, inner_key = lax.psum(
        (jnp.sum(normed_query * query_hat, axis=1), jnp.sum(normed_key * key_hat, axis=1)), "col"
    )
    grad_query_low = (
        query_scale * (normed_query - query_hat * inner_query[:, None] / width)
    ).astype(bfloat)
    grad_key_low = (key_scale * (normed_key - key_hat * inner_key[:, None] / width)).astype(bfloat)
    grad_value_low = grad_values.reshape(rows, local_width)
    grad_in_part = (
        cross_cols(grad_query_low, query_full)
        + cross_cols(grad_key_low, key_full)
        + cross_cols(grad_value_low, value_full)
    )
    grad_inputs = grad_middle_here + lax.psum_scatter(
        grad_in_part, "col", scatter_dimension=1, tiled=True
    )
    grad_query = cross_rows(whole_in, grad_query_low)
    grad_key = cross_rows(whole_in, grad_key_low)
    grad_value = cross_rows(whole_in, grad_value_low)
    summed = (
        lax.psum_scatter(grad_query, "row", scatter_dimension=0, tiled=True),
        lax.psum_scatter(grad_key, "row", scatter_dimension=0, tiled=True),
        lax.psum_scatter(grad_value, "row", scatter_dimension=0, tiled=True),
        lax.psum_scatter(grad_output, "row", scatter_dimension=0, tiled=True),
        lax.psum_scatter(grad_gate, "row", scatter_dimension=0, tiled=True),
        lax.psum_scatter(grad_up, "row", scatter_dimension=0, tiled=True),
        lax.psum_scatter(grad_down, "row", scatter_dimension=0, tiled=True),
    )
    gains = lax.psum((grad_query_gain, grad_key_gain, grad_attn_gain, grad_mlp_gain), "row")
    return (
        layer_out,
        grad_inputs,
        summed[0],
        summed[1],
        summed[2],
        summed[3],
        summed[4],
        summed[5],
        summed[6],
        gains[0],
        gains[1],
        gains[2],
        gains[3],
    )


BF = jnp.bfloat16
F32 = jnp.float32
MESH_ID = pl.DeviceIdType.MESH
T = 512
DC = 256
DR = 512
D = 2048
FH = 512
LAYER_STAGES = 5
EXACT = lax.Precision.HIGHEST


def dot_nn(a, b):
    return jnp.dot(a, b, preferred_element_type=F32)


def dot_nt(a, b, precision=None):
    return lax.dot_general(
        a, b, (((1,), (1,)), ((), ())), precision=precision, preferred_element_type=F32
    )


def dot_tn(a, b, precision=None):
    return lax.dot_general(
        a, b, (((0,), (0,)), ((), ())), precision=precision, preferred_element_type=F32
    )


def aligned(start, size):
    return pl.ds(pl.multiple_of(start, size), size)


class Counter:
    def __init__(self):
        self.used = 0

    def take(self, count=1):
        first = self.used
        self.used += count
        return first


def block_kernel(
    x_hbm,
    wq_hbm,
    wk_hbm,
    wv_hbm,
    wo_hbm,
    wg_hbm,
    wu_hbm,
    wd_hbm,
    cot_hbm,
    gains_ref,
    pos_ref,
    layer_out,
    grad_in,
    gains_out,
    land_down,
    land_gu,
    land_o,
    land_qkv,
    wqkv,
    wo,
    wgu,
    wd,
    x_full,
    mid_full,
    gf_full,
    gb_full,
    gu_s,
    mixed_s,
    ggu_s,
    probs_s,
    hat_s,
    low_s,
    cos_s,
    sin_s,
    cot_s,
    middle_s,
    bhat_s,
    work_s,
    att_s,
    ga_s,
    gqkv_s,
    gs_s,
    pl_s,
    gqk_s,
    own_s,
    stage_c,
    land_c,
    stage_y,
    land_y,
    stage_z,
    land_z,
    scal_s,
    gain_s,
    stage_down,
    stage_gu,
    out_lo,
    send_sem,
    recv_sem,
    local_sem,
):
    row = lax.axis_index("row")
    col = lax.axis_index("col")
    x_at = lax.rem(row, 2)
    y_at = lax.div(row, 2)
    core = lax.rem(col, 2)
    z_at = lax.div(col, 2)
    row_x = row + 1 - 2 * x_at
    row_y = lax.rem(row + 2, 4)
    row_d = row_y + 1 - 2 * x_at
    sib = col + 1 - 2 * core
    dev_x = (row_x, col)
    dev_y = (row_y, col)
    dev_d = (row_d, col)
    dev_c = (row, sib)

    def dev_z(step):
        return (row, lax.rem(col + 2 * step, 8))

    def col_from(step):
        return lax.rem(col + 8 - 2 * step, 8)

    def sib_from(step):
        return lax.rem(sib + 8 - 2 * step, 8)

    counter = Counter()
    locals_used = Counter()
    pending = []

    def copy_of(index, src, dst, device):
        return pltpu.make_async_remote_copy(
            src_ref=src,
            dst_ref=dst,
            send_sem=send_sem.at[index],
            recv_sem=recv_sem.at[index],
            device_id=device,
            device_id_type=MESH_ID,
        )

    def send(index, src, dst, device):
        copy = copy_of(index, src, dst, device)
        copy.start()
        pending.append(copy)
        return copy

    def arrived(index, dst):
        copy_of(index, dst, dst, dev_c).wait_recv()

    def sent(copy):
        copy.wait_send()
        pending[:] = [other for other in pending if other is not copy]

    def local(src, dst):
        copy = pltpu.make_async_copy(src, dst, local_sem.at[locals_used.take()])
        copy.start()
        return copy

    barrier = pltpu.get_barrier_semaphore()
    partners = [dev_x, dev_y, dev_d] + [(row, lax.rem(col + step, 8)) for step in range(1, 8)]
    for device in partners:
        pl.semaphore_signal(barrier, inc=1, device_id=device, device_id_type=MESH_ID)
    local_copies = []
    for index, ref in enumerate((wq_hbm, wk_hbm, wv_hbm)):
        local_copies.append(local(ref, wqkv.at[aligned(row * DR, DR), pl.ds(index * DC, DC)]))
    local_copies.append(local(wo_hbm, wo.at[aligned(row * DR, DR), :]))
    half_mine = aligned(y_at * FH, FH)
    half_other = aligned((1 - y_at) * FH, FH)
    local_copies.append(local(wg_hbm.at[:, half_mine], wgu.at[aligned(row * DR, DR), pl.ds(0, FH)]))
    local_copies.append(local(wu_hbm.at[:, half_mine], wgu.at[aligned(row * DR, DR), pl.ds(FH, FH)]))
    local_copies.append(local(wd_hbm.at[:, half_mine], wd.at[aligned(row * DR, DR), :]))
    local_copies.append(local(x_hbm, x_full.at[:, aligned(col * DC, DC)]))
    local_copies.append(local(cot_hbm, cot_s))
    pl.semaphore_wait(barrier, len(partners))

    def gather_block(buf, rows, at):
        return buf.at[rows, aligned(at * DC, DC)]

    class Gather:
        def __init__(self, buf, plane):
            self.buf = buf
            self.plane = plane
            self.base_z = counter.take(3)
            self.base_c = counter.take(4)
            if plane:
                self.base_y = counter.take(4)
                self.base_cy = counter.take(4)
                self.rows = aligned(y_at * T, T)
                self.rows_other = aligned((1 - y_at) * T, T)
            else:
                self.rows = pl.ds(0, T)

        def start(self, source=None):
            own = gather_block(self.buf, self.rows, col)
            src = own if source is None else source
            for step in (1, 2, 3):
                send(self.base_z + step - 1, src, own, dev_z(step))
            if self.plane:
                send(self.base_y, src, own, dev_y)
            send(self.base_c, src, own, dev_c)

        def finish(self):
            for step in (1, 2, 3):
                block = gather_block(self.buf, self.rows, col_from(step))
                arrived(self.base_z + step - 1, block)
                if self.plane:
                    send(self.base_y + step, block, block, dev_y)
                send(self.base_c + step, block, block, dev_c)
            if self.plane:
                for step in range(4):
                    block = gather_block(self.buf, self.rows_other, col_from(step))
                    arrived(self.base_y + step, block)
                    send(self.base_cy + step, block, block, dev_c)
            for step in range(4):
                arrived(self.base_c + step, gather_block(self.buf, self.rows, sib_from(step)))
                if self.plane:
                    arrived(
                        self.base_cy + step, gather_block(self.buf, self.rows_other, sib_from(step))
                    )

    class Reduce:
        ORDER = (1, 2, 3, 0)

        def __init__(self, partial, plane):
            self.partial = partial
            self.plane = plane
            self.count = 2 * T if plane else T
            self.base_c = counter.take(4)
            self.base_z = counter.take(3)
            if plane:
                self.base_y = counter.take(4)
                self.rows = aligned(y_at * T, T)
                self.rows_other = aligned((1 - y_at) * T, T)
            else:
                self.rows = pl.ds(0, T)
            self.sent = []

        def start(self):
            count = self.count
            for slot, step in enumerate(self.ORDER):
                target = lax.rem(z_at + step, 4)
                start = pl.multiple_of((2 * target + 1 - core) * DC, DC)
                stage_c[slot, :count, :] = self.partial(start).astype(BF)
                self.sent.append(
                    send(
                        self.base_c + slot,
                        stage_c.at[slot, pl.ds(0, count), :],
                        land_c.at[slot, pl.ds(0, count), :],
                        dev_c,
                    )
                )
                start = pl.multiple_of((2 * target + core) * DC, DC)
                own_s[slot, :count, :] = self.partial(start)

        def cores(self):
            count = self.count
            for slot, step in enumerate(self.ORDER):
                arrived(self.base_c + slot, land_c.at[slot, pl.ds(0, count), :])
                if self.plane:
                    rows = self.rows_other
                    stage_y[slot] = (
                        own_s[slot, rows, :] + land_c[slot, rows, :].astype(F32)
                    ).astype(BF)
                    self.sent.append(
                        send(self.base_y + slot, stage_y.at[slot], land_y.at[slot], dev_y)
                    )
                    rows = self.rows
                    own_s[slot, rows, :] = own_s[slot, rows, :] + land_c[slot, rows, :].astype(F32)
                else:
                    self.pass_on(slot, step, land_c.at[slot, pl.ds(0, T), :])

        def pass_on(self, slot, step, landed):
            total = own_s[slot, self.rows, :] + landed[...].astype(F32)
            if step == 0:
                own_s[slot, self.rows, :] = total
            else:
                stage_z[slot] = total.astype(BF)
                self.sent.append(
                    send(self.base_z + slot, stage_z.at[slot], land_z.at[slot], dev_z(step))
                )

        def planes(self):
            if self.plane:
                for slot, step in enumerate(self.ORDER):
                    arrived(self.base_y + slot, land_y.at[slot])
                    self.pass_on(slot, step, land_y.at[slot])

        def finish(self):
            for slot in range(3):
                arrived(self.base_z + slot, land_z.at[slot])
            total = own_s[3, self.rows, :]
            for slot in range(3):
                total = total + land_z[slot].astype(F32)
            for copy in self.sent:
                sent(copy)
            return total

    pick = lax.broadcasted_iota(jnp.int32, (8, DC), 0)
    lane = lax.broadcasted_iota(jnp.int32, (8, DC), 1)
    first_row = (pick == 0).astype(F32)
    second_row = (pick == 1).astype(F32)
    spread = ((pick == 0) & (lane < 128)).astype(F32) + ((pick == 1) & (lane >= 128)).astype(F32)

    def sums_over_col(stage, first, second):
        base = counter.take(7)
        mine = dot_nt(first_row, first, EXACT)
        if second is not None:
            mine = mine + dot_nt(second_row, second, EXACT)
        scal_s[stage, col] = mine
        for step in range(1, 8):
            send(
                base + step - 1,
                scal_s.at[stage, col],
                scal_s.at[stage, col],
                (row, lax.rem(col + step, 8)),
            )
        for step in range(1, 8):
            arrived(base + step - 1, scal_s.at[stage, lax.rem(col + 8 - step, 8)])
        total = scal_s[stage, 0]
        for index in range(1, 8):
            total = total + scal_s[stage, index]
        both = dot_tn(total, spread, EXACT)
        return both[:, :128], both[:, 128:]

    def wide(values):
        return jnp.concatenate([values, values], axis=1)

    x_gather = Gather(x_full, False)
    attn_base = counter.take(16)

    def attn_place(index, owner, part=None):
        if part is None:
            rows = aligned(owner * DR, DR)
        else:
            rows = aligned(owner * DR + part * (DR // 2), DR // 2)
        if index < 3:
            return wqkv.at[rows, pl.ds(index * DC, DC)]
        return wo.at[rows, :]

    attn_hbm = (wq_hbm, wk_hbm, wv_hbm, wo_hbm)

    def attn_send(index):
        send(attn_base + index, attn_hbm[index], attn_place(index, row), dev_x)
        send(attn_base + 4 + index, attn_hbm[index], attn_place(index, row), dev_y)

    def attn_relay(index):
        arrived(attn_base + index, attn_place(index, row_x))
        part = attn_place(index, row_x, 0)
        send(attn_base + 8 + index, part, part, dev_y)
        arrived(attn_base + 4 + index, attn_place(index, row_y))
        part = attn_place(index, row_y, 1)
        send(attn_base + 12 + index, part, part, dev_x)

    def attn_ready(index):
        arrived(attn_base + 8 + index, attn_place(index, row_d, 0))
        arrived(attn_base + 12 + index, attn_place(index, row_d, 1))

    mlp_base = counter.take(9)
    mlp_hbm = (wg_hbm, wu_hbm, wd_hbm)

    def mlp_place(index, owner):
        rows = aligned(owner * DR, DR)
        if index < 2:
            return wgu.at[rows, pl.ds(index * FH, FH)]
        return wd.at[rows, :]

    def mlp_send(index):
        send(mlp_base + index, mlp_hbm[index].at[:, half_mine], mlp_place(index, row), dev_x)
        send(mlp_base + 3 + index, mlp_hbm[index].at[:, half_other], mlp_place(index, row), dev_y)

    def mlp_relay(index):
        place = mlp_place(index, row_y)
        arrived(mlp_base + 3 + index, place)
        send(mlp_base + 6 + index, place, place, dev_x)

    def mlp_ready(index):
        arrived(mlp_base + index, mlp_place(index, row_x))
        arrived(mlp_base + 6 + index, mlp_place(index, row_d))

    for index in range(3):
        attn_send(index)
    x_gather.start(x_hbm)

    lane_at = lax.broadcasted_iota(jnp.int32, (1, HD), 1)
    within = lax.rem(lane_at, HD // 2).astype(F32)
    frequency = jnp.exp(within * (-2.0 * math.log(THETA) / HD))
    angles = pos_ref[...].astype(F32) * frequency
    cos_s[...] = jnp.cos(angles)
    sine = jnp.sin(angles)
    sin_s[...] = jnp.where(lane_at < HD // 2, -sine, sine)

    for index in range(3):
        attn_relay(index)
    attn_send(3)
    for copy in local_copies:
        copy.wait()
    x_gather.finish()
    for index in range(3):
        attn_ready(index)

    gains = gains_ref[:, aligned(col * DC, DC)]
    raw = []
    for index in range(3):
        raw.append(dot_nn(x_full[...], wqkv[:, pl.ds(index * DC, DC)]))
    low_s[2] = raw[2].astype(BF)
    hat_s[0] = raw[0]
    hat_s[1] = raw[1]
    attn_relay(3)
    for index in range(3):
        mlp_send(index)
    totals = sums_over_col(0, raw[0] * raw[0], raw[1] * raw[1])
    scales = [lax.rsqrt(total / D + EPS) for total in totals]
    work_s[0] = jnp.concatenate(scales, axis=1)
    for index in range(2):
        hat = hat_s[index] * wide(scales[index])
        hat_s[index] = hat
        normed = hat * gains[index : index + 1, :]
        for head in range(2):
            part = normed[:, head * HD : (head + 1) * HD]
            turned = part * cos_s[...] + pltpu.roll(part, HD // 2, 1) * sin_s[...]
            if index == 0:
                turned = turned * (HD**-0.5)
            low_s[index, :, pl.ds(head * HD, HD)] = turned.astype(BF)

    chunk = 128

    def visible(at):
        query = at * chunk + lax.broadcasted_iota(jnp.int32, (chunk, T), 0)
        key = lax.broadcasted_iota(jnp.int32, (chunk, T), 1)
        oldest = query - pos_ref[aligned(at * chunk, chunk), :]
        return (key <= query) & (key >= oldest)

    def attend_chunk(at, carry):
        rows = aligned(at * chunk, chunk)
        allowed = visible(at)
        for head in range(2):
            lanes = pl.ds(head * HD, HD)
            scores = dot_nt(low_s[0, rows, lanes], low_s[1, :, lanes])
            scores = jnp.where(allowed, scores, MASKED)
            exponent = jnp.exp(scores - jnp.max(scores, axis=1, keepdims=True))
            probs = exponent / jnp.sum(exponent, axis=1, keepdims=True)
            probs_s[head, rows, :] = probs
            att_s[rows, lanes] = dot_nn(probs.astype(BF), low_s[2, :, lanes]).astype(BF)
        return carry

    lax.fori_loop(0, T // chunk, attend_chunk, 0)

    attn_ready(3)
    branch_sum = Reduce(lambda start: dot_nt(att_s[...], wo[pl.ds(start, DC), :]), False)
    branch_sum.start()
    branch_sum.cores()
    mlp_relay(0)
    branch = branch_sum.finish()
    work_s[1] = branch
    mlp_relay(1)
    total, _ = sums_over_col(1, branch * branch, None)
    branch_scale = lax.rsqrt(total / D + EPS)
    work_s[2, :, :128] = branch_scale
    branch_hat = work_s[1] * wide(branch_scale)
    bhat_s[...] = branch_hat
    middle = x_hbm_slice(x_full, col) + branch_hat * gains[2:3, :]
    middle_s[...] = middle
    mid_full[aligned(y_at * T, T), aligned(col * DC, DC)] = middle.astype(BF)
    mid_gather = Gather(mid_full, True)
    mid_gather.start()
    mlp_relay(2)
    mid_gather.finish()
    mlp_ready(0)
    mlp_ready(1)

    tile = 256

    def forward_tile(at, carry):
        rows = aligned(lax.div(at, 2) * T, T)
        lane_start = lax.rem(at, 2) * tile
        lanes = aligned(lane_start, tile)
        lanes_up = aligned(lane_start + FH, tile)
        gate = dot_nn(mid_full[rows, :], wgu[:, lanes])
        up = dot_nn(mid_full[rows, :], wgu[:, lanes_up])
        gu_s[rows, lanes] = gate
        gu_s[rows, lanes_up] = up
        mixed_s[rows, lanes] = (gate * jax.nn.sigmoid(gate) * up).astype(BF)
        return carry

    lax.fori_loop(0, 4, forward_tile, 0)
    mlp_ready(2)
    ffn_sum = Reduce(lambda start: dot_nt(mixed_s[...], wd[pl.ds(start, DC), :]), True)
    ffn_sum.start()
    ffn_sum.cores()
    ffn_sum.planes()
    ffn = ffn_sum.finish()
    work_s[1] = ffn
    cot_gain = cot_s[...].astype(F32) * gains[3:4, :]
    total, inner = sums_over_col(2, ffn * ffn, cot_gain * ffn)
    ffn_scale = lax.rsqrt(total / D + EPS)
    ffn_hat = work_s[1] * wide(ffn_scale)
    cot = cot_s[...].astype(F32)
    out_lo[...] = (middle_s[...] + ffn_hat * gains[3:4, :]).astype(BF)
    lo_copy = local(out_lo, layer_out)
    gain_s[row, 3:4, :] = jnp.sum(cot * ffn_hat, axis=0, keepdims=True)
    inner = wide(inner * ffn_scale / D)
    grad_ffn = wide(ffn_scale) * (cot * gains[3:4, :] - ffn_hat * inner)
    gf_full[aligned(y_at * T, T), aligned(col * DC, DC)] = grad_ffn.astype(BF)
    gf_gather = Gather(gf_full, True)
    gf_gather.start()
    gf_gather.finish()

    def backward_tile(at, carry):
        rows = aligned(lax.div(at, 2) * T, T)
        lane_start = lax.rem(at, 2) * tile
        lanes = aligned(lane_start, tile)
        lanes_up = aligned(lane_start + FH, tile)
        grad_mixed = dot_nn(gf_full[rows, :], wd[:, lanes])
        gate = gu_s[rows, lanes]
        up = gu_s[rows, lanes_up]
        sigma = jax.nn.sigmoid(gate)
        ggu_s[rows, lanes] = (grad_mixed * up * sigma * (1.0 + gate * (1.0 - sigma))).astype(BF)
        ggu_s[rows, lanes_up] = (grad_mixed * gate * sigma).astype(BF)
        return carry

    lax.fori_loop(0, 4, backward_tile, 0)
    mid_sum = Reduce(lambda start: dot_nt(ggu_s[...], wgu[pl.ds(start, DC), :]), True)
    mid_sum.start()
    mid_sum.cores()

    order = ((row_x, dev_x), (row_y, dev_y), (row_d, dev_d), (row, None))

    def push(stage, slot, land, base, device):
        if device is None:
            return local(stage.at[slot], land.at[row])
        return send(base + slot, stage.at[slot], land.at[row], device)

    pushes = []
    down_base = counter.take(3)
    for slot, (owner, device) in enumerate(order):
        lanes = aligned(owner * DR, DR)
        stage_down[slot] = dot_tn(gf_full[:, lanes], mixed_s[...]).astype(BF)
        pushes.append(push(stage_down, slot, land_down, down_base, device))
    mid_sum.planes()
    gu_base = counter.take(3)
    gu_pushes = []
    for slot, (owner, device) in enumerate(order):
        lanes = aligned(owner * DR, DR)
        for part in range(2):
            half = pl.ds(part * FH, FH)
            stage_gu[slot, :, half] = dot_tn(mid_full[:, lanes], ggu_s[:, half]).astype(BF)
        gu_pushes.append(push(stage_gu, slot, land_gu, gu_base, device))
    grad_middle = cot_s[...].astype(F32) + mid_sum.finish()
    middle_s[...] = grad_middle
    gain_s[row, 2:3, :] = jnp.sum(grad_middle * bhat_s[...], axis=0, keepdims=True)
    inner, _ = sums_over_col(3, grad_middle * gains[2:3, :] * bhat_s[...], None)
    branch_scale = wide(work_s[2, :, :128])
    grad_branch = branch_scale * (
        middle_s[...] * gains[2:3, :] - bhat_s[...] * wide(inner / D)
    )
    gb_full[:, aligned(col * DC, DC)] = grad_branch.astype(BF)
    gb_gather = Gather(gb_full, False)
    gb_gather.start()
    gb_gather.finish()

    ga_s[...] = dot_nn(gb_full[...], wo[...]).astype(BF)

    def attend_back_chunk(at, carry):
        rows = aligned(at * chunk, chunk)
        for head in range(2):
            lanes = pl.ds(head * HD, HD)
            grad_probs = dot_nt(ga_s[rows, lanes], low_s[2, :, lanes])
            probs = probs_s[head, rows, :]
            weighted = probs * grad_probs
            inner = jnp.sum(weighted, axis=1, keepdims=True)
            grad_scores = (probs * (grad_probs - inner)).astype(BF)
            gs_s[head, rows, :] = grad_scores
            pl_s[head, rows, :] = probs.astype(BF)
            gqk_s[0, rows, lanes] = dot_nn(grad_scores, low_s[1, :, lanes])
        return carry

    lax.fori_loop(0, T // chunk, attend_back_chunk, 0)
    for head in range(2):
        lanes = pl.ds(head * HD, HD)
        gqk_s[1, :, lanes] = dot_tn(gs_s[head], low_s[0, :, lanes])
        gqkv_s[:, pl.ds(2 * DC + head * HD, HD)] = dot_tn(pl_s[head], ga_s[:, lanes]).astype(BF)
    inners = []
    for index in range(2):
        for head in range(2):
            lanes = pl.ds(head * HD, HD)
            part = gqk_s[index, :, lanes]
            turned = part * cos_s[...] - pltpu.roll(part, HD // 2, 1) * sin_s[...]
            if index == 0:
                turned = turned * (HD**-0.5)
            gqk_s[index, :, lanes] = turned
        weighted = gqk_s[index] * hat_s[index]
        gain_s[row, index : index + 1, :] = jnp.sum(weighted, axis=0, keepdims=True)
        inners.append(weighted * gains[index : index + 1, :])
    gain_base = counter.take(3)
    for slot, (_, device) in enumerate(order[:3]):
        send(gain_base + slot, gain_s.at[row], gain_s.at[row], device)
    totals = sums_over_col(4, inners[0], inners[1])
    for index in range(2):
        scale = wide(work_s[0, :, index * 128 : (index + 1) * 128])
        gqkv_s[:, pl.ds(index * DC, DC)] = (
            scale
            * (
                gqk_s[index] * gains[index : index + 1, :]
                - hat_s[index] * wide(totals[index] / D)
            )
        ).astype(BF)

    for group in (pushes, gu_pushes):
        for copy in group[:3]:
            sent(copy)
        group[3].wait()
    in_sum = Reduce(lambda start: dot_nt(gqkv_s[...], wqkv[pl.ds(start, DC), :]), False)
    in_sum.start()
    in_sum.cores()
    o_base = counter.take(3)
    qkv_base = counter.take(3)
    late = []
    for slot, (owner, device) in enumerate(order):
        lanes = aligned(owner * DR, DR)
        stage_gu[slot, :, pl.ds(0, 3 * DC)] = dot_tn(x_full[:, lanes], gqkv_s[...]).astype(BF)
        source = stage_gu.at[slot, :, pl.ds(0, 3 * DC)]
        if device is None:
            late.append(local(source, land_qkv.at[row]))
        else:
            send(qkv_base + slot, source, land_qkv.at[row], device)
        stage_down[slot, :, pl.ds(0, DC)] = dot_tn(gb_full[:, lanes], att_s[...]).astype(BF)
        source = stage_down.at[slot, :, pl.ds(0, DC)]
        if device is None:
            late.append(local(source, land_o.at[row]))
        else:
            send(o_base + slot, source, land_o.at[row], device)
    work_s[1] = middle_s[...] + in_sum.finish()
    late.append(local(work_s.at[1], grad_in))
    late.append(lo_copy)

    sources = (row_x, row_y, row_d)
    for slot, owner in enumerate(sources):
        arrived(gain_base + slot, gain_s.at[owner])
    gains_out[...] = gain_s[0] + gain_s[1] + gain_s[2] + gain_s[3]
    for slot, owner in enumerate(sources):
        arrived(down_base + slot, land_down.at[owner])
        arrived(gu_base + slot, land_gu.at[owner])
        arrived(o_base + slot, land_o.at[owner])
        arrived(qkv_base + slot, land_qkv.at[owner])
    for copy in late:
        copy.wait()
    for copy in pending:
        copy.wait_send()


def x_hbm_slice(x_full, col):
    return x_full[:, aligned(col * DC, DC)].astype(F32)


MIB = 1 << 20


def on_device_kernel(
    inputs,
    query_weight,
    key_weight,
    value_weight,
    output_weight,
    gate_weight,
    up_weight,
    down_weight,
    query_gain,
    key_gain,
    attn_gain,
    mlp_gain,
    positions,
    segments,
    cotangent,
):
    gains = jnp.stack([query_gain, key_gain, attn_gain, mlp_gain])
    gains = jnp.concatenate([gains, jnp.zeros_like(gains)], axis=0)
    hbm = pl.BlockSpec(memory_space=pl.ANY)
    vmem = pl.BlockSpec(memory_space=pltpu.VMEM)
    sds = jax.ShapeDtypeStruct
    copies = 230
    results = pl.pallas_call(
        block_kernel,
        out_shape=[
            sds((T, DC), BF),
            sds((T, DC), F32),
            sds((8, DC), F32),
            sds((4, DR, FH), BF),
            sds((4, DR, 2 * FH), BF),
            sds((4, DR, DC), BF),
            sds((4, DR, 3 * DC), BF),
        ],
        in_specs=[hbm] * 9 + [vmem, vmem],
        out_specs=[hbm, hbm, vmem, hbm, hbm, hbm, hbm],
        scratch_shapes=[
            pltpu.VMEM((D, 3 * DC), BF),
            pltpu.VMEM((D, DC), BF),
            pltpu.VMEM((D, 2 * FH), BF),
            pltpu.VMEM((D, FH), BF),
            pltpu.VMEM((T, D), BF),
            pltpu.VMEM((2 * T, D), BF),
            pltpu.VMEM((2 * T, D), BF),
            pltpu.VMEM((T, D), BF),
            pltpu.VMEM((2 * T, 2 * FH), F32),
            pltpu.VMEM((2 * T, FH), BF),
            pltpu.VMEM((2 * T, 2 * FH), BF),
            pltpu.VMEM((2, T, T), F32),
            pltpu.VMEM((2, T, DC), F32),
            pltpu.VMEM((3, T, DC), BF),
            pltpu.VMEM((T, HD), F32),
            pltpu.VMEM((T, HD), F32),
            pltpu.VMEM((T, DC), BF),
            pltpu.VMEM((T, DC), F32),
            pltpu.VMEM((T, DC), F32),
            pltpu.VMEM((3, T, DC), F32),
            pltpu.VMEM((T, DC), BF),
            pltpu.VMEM((T, DC), BF),
            pltpu.VMEM((T, 3 * DC), BF),
            pltpu.VMEM((2, T, T), BF),
            pltpu.VMEM((2, T, T), BF),
            pltpu.VMEM((2, T, DC), F32),
            pltpu.VMEM((4, 2 * T, DC), F32),
            pltpu.VMEM((4, 2 * T, DC), BF),
            pltpu.VMEM((4, 2 * T, DC), BF),
            pltpu.VMEM((4, T, DC), BF),
            pltpu.VMEM((4, T, DC), BF),
            pltpu.VMEM((3, T, DC), BF),
            pltpu.VMEM((3, T, DC), BF),
            pltpu.VMEM((LAYER_STAGES, 8, 8, T), F32),
            pltpu.VMEM((4, 8, DC), F32),
            pltpu.VMEM((4, DR, FH), BF),
            pltpu.VMEM((4, DR, 2 * FH), BF),
            pltpu.VMEM((T, DC), BF),
            pltpu.SemaphoreType.DMA((copies,)),
            pltpu.SemaphoreType.DMA((copies,)),
            pltpu.SemaphoreType.DMA((32,)),
        ],
        compiler_params=pltpu.CompilerParams(
            collective_id=0, has_side_effects=True, vmem_limit_bytes=64 * MIB
        ),
        cost_estimate=pl.CostEstimate(
            flops=26_800_000_000, bytes_accessed=16_000_000, transcendentals=2_000_000
        ),
    )(
        inputs,
        query_weight,
        key_weight,
        value_weight,
        output_weight,
        gate_weight,
        up_weight,
        down_weight,
        cotangent,
        gains,
        positions[:, None],
    )
    layer_out, grad_in, gains_out, land_down, land_gu, land_o, land_qkv = results

    def halves(landed):
        landed = landed.astype(F32)
        return jnp.concatenate([landed[0] + landed[1], landed[2] + landed[3]], axis=1)

    def total(landed):
        landed = landed.astype(F32)
        return landed[0] + landed[1] + landed[2] + landed[3]

    return (
        layer_out,
        grad_in,
        total(land_qkv[:, :, :DC]),
        total(land_qkv[:, :, DC : 2 * DC]),
        total(land_qkv[:, :, 2 * DC :]),
        total(land_o),
        halves(land_gu[:, :, :FH]),
        halves(land_gu[:, :, FH:]),
        halves(land_down),
        gains_out[0],
        gains_out[1],
        gains_out[2],
        gains_out[3],
    )


def solution(mesh):
    in_specs = (
        P("row", "col"),
        P("row", "col"),
        P("row", "col"),
        P("row", "col"),
        P("row", "col"),
        P("row", "col"),
        P("row", "col"),
        P("row", "col"),
        P(),
        P(),
        P(),
        P(),
        P("row"),
        P("row"),
        P("row", "col"),
    )
    out_specs = (
        P("row", "col"),
        P("row", "col"),
        P("row", "col"),
        P("row", "col"),
        P("row", "col"),
        P("row", "col"),
        P("row", "col"),
        P("row", "col"),
        P("row", "col"),
        P("col"),
        P("col"),
        P("col"),
        P("col"),
    )
    sizes = (mesh.shape["row"], mesh.shape["col"])
    body = on_device_kernel if sizes == (4, 8) else on_device
    return jax.shard_map(
        body, mesh=mesh, in_specs=in_specs, out_specs=out_specs, check_vma=False
    )
```

```python
import math

import jax
import jax.numpy as jnp
from jax import lax
from jax.experimental import pallas as pl
from jax.experimental.pallas import tpu as pltpu
from jax.sharding import PartitionSpec as P

HD = 128
LENGTH = 512


EPS = 1e-06
THETA = 500000.0
MASKED = -1e30


def rope_tables(positions, head_size):
    halfway = head_size // 2
    frequency = jnp.exp(
        jnp.arange(halfway, dtype=jnp.float32) * (-2.0 * math.log(THETA) / head_size)
    )
    angles = positions.astype(jnp.float32)[:, None] * frequency[None, :]
    return (jnp.cos(angles)[:, None, :], jnp.sin(angles)[:, None, :])


def rotate(values, cosine, sine):
    halfway = values.shape[-1] // 2
    first_half = values[..., :halfway]
    second_half = values[..., halfway:]
    return jnp.concatenate(
        [first_half * cosine - second_half * sine, second_half * cosine + first_half * sine],
        axis=-1,
    )


def matmul(left, right):
    return jnp.dot(left, right, preferred_element_type=jnp.float32)


def cross_rows(left, right):
    return lax.dot_general(
        left, right, (((0,), (0,)), ((), ())), preferred_element_type=jnp.float32
    )


def cross_cols(left, right):
    return lax.dot_general(
        left, right, (((1,), (1,)), ((), ())), preferred_element_type=jnp.float32
    )


def visible_pairs(segment_part):
    places = jnp.arange(segment_part.shape[0])
    return (segment_part[:, None] == segment_part[None, :]) & (places[:, None] >= places[None, :])


def on_device(
    inputs,
    query_weight,
    key_weight,
    value_weight,
    output_weight,
    gate_weight,
    up_weight,
    down_weight,
    query_gain,
    key_gain,
    attn_gain,
    mlp_gain,
    positions,
    segments,
    cotangent,
):
    bfloat = jnp.bfloat16
    floats = jnp.float32
    rows = inputs.shape[0]
    local_width = inputs.shape[1]
    width = local_width * lax.axis_size("col")
    offset = lax.axis_index("col") * local_width
    head_size = HD
    heads_here = local_width // head_size
    sequences = rows // LENGTH
    scale = head_size ** (-0.5)
    shape_seq = (sequences, LENGTH, heads_here, head_size)

    def mine(values):
        return lax.dynamic_slice_in_dim(values, offset, local_width, values.ndim - 1)

    query_gain_here = mine(query_gain)
    key_gain_here = mine(key_gain)
    cot_here = cotangent.astype(floats)
    gathered = (
        lax.all_gather(query_weight, "row", axis=0, tiled=True),
        lax.all_gather(key_weight, "row", axis=0, tiled=True),
        lax.all_gather(value_weight, "row", axis=0, tiled=True),
        lax.all_gather(gate_weight, "row", axis=0, tiled=True),
        lax.all_gather(up_weight, "row", axis=0, tiled=True),
        lax.all_gather(output_weight, "row", axis=0, tiled=True),
        lax.all_gather(down_weight, "row", axis=0, tiled=True),
    )
    query_full, key_full, value_full, gate_full, up_full, output_full, down_full = gathered
    whole_in = lax.all_gather(inputs, "col", axis=1, tiled=True)
    query_raw = matmul(whole_in, query_full)
    key_raw = matmul(whole_in, key_full)
    value_raw = matmul(whole_in, value_full)
    query_total, key_total = lax.psum(
        (jnp.sum(query_raw * query_raw, axis=1), jnp.sum(key_raw * key_raw, axis=1)), "col"
    )
    query_scale = lax.rsqrt(query_total / width + EPS)[:, None]
    key_scale = lax.rsqrt(key_total / width + EPS)[:, None]
    query_hat = query_raw * query_scale
    key_hat = key_raw * key_scale
    cosine, sine = rope_tables(positions, head_size)
    query_low = (
        rotate((query_hat * query_gain_here).reshape(rows, heads_here, head_size), cosine, sine)
        * scale
    ).astype(bfloat)
    key_low = rotate(
        (key_hat * key_gain_here).reshape(rows, heads_here, head_size), cosine, sine
    ).astype(bfloat)
    value_low = value_raw.astype(bfloat).reshape(rows, heads_here, head_size)
    query_blocks = query_low.reshape(shape_seq)
    key_blocks = key_low.reshape(shape_seq)
    value_blocks = value_low.reshape(shape_seq)
    segment_blocks = segments.reshape(sequences, LENGTH)

    def attend(block):
        queries, keys_part, values_part, segment_part = block
        scores = jnp.einsum("qhd,khd->hqk", queries, keys_part, preferred_element_type=floats)
        scores = jnp.where(visible_pairs(segment_part)[None], scores, MASKED)
        largest = jnp.max(scores, axis=-1, keepdims=True)
        exponent = jnp.exp(scores - largest)
        totals = jnp.sum(exponent, axis=-1, keepdims=True)
        weights_low = (exponent / totals).astype(bfloat)
        attended_part = jnp.einsum(
            "hqk,khd->qhd", weights_low, values_part, preferred_element_type=floats
        )
        return (attended_part, (largest + jnp.log(totals))[..., 0])

    attended, log_totals = lax.map(attend, (query_blocks, key_blocks, value_blocks, segment_blocks))
    attended_low = attended.reshape(rows, local_width).astype(bfloat)
    branch = lax.psum(cross_cols(attended_low, output_full), "col")
    branch_scale = lax.rsqrt(jnp.mean(branch * branch, axis=1, keepdims=True) + EPS)
    branch_hat = branch * branch_scale
    middle = whole_in.astype(floats) + branch_hat * attn_gain
    middle_low = middle.astype(bfloat)
    middle_here = mine(middle)
    branch_hat_here = mine(branch_hat)
    gate_pre = matmul(middle_low, gate_full)
    up_pre = matmul(middle_low, up_full)
    sigma = jax.nn.sigmoid(gate_pre)
    silu_gate = gate_pre * sigma
    mixed_low = (silu_gate * up_pre).astype(bfloat)
    ffn = lax.psum(cross_cols(mixed_low, down_full), "col")
    ffn_scale = lax.rsqrt(jnp.mean(ffn * ffn, axis=1, keepdims=True) + EPS)
    ffn_hat = ffn * ffn_scale
    ffn_hat_here = mine(ffn_hat)
    grad_top = lax.all_gather(cotangent, "col", axis=1, tiled=True).astype(floats)
    normed_top = grad_top * mlp_gain
    inner_top = jnp.sum(normed_top * ffn_hat, axis=1, keepdims=True)
    grad_ffn_low = (ffn_scale * (normed_top - ffn_hat * inner_top / width)).astype(bfloat)
    layer_out = (middle_here + ffn_hat_here * mine(mlp_gain)).astype(bfloat)
    grad_mlp_gain = jnp.sum(cot_here * ffn_hat_here, axis=0)
    grad_down = cross_rows(grad_ffn_low, mixed_low)
    grad_mixed = matmul(grad_ffn_low, down_full)
    grad_gate_low = (grad_mixed * up_pre * sigma * (1.0 + gate_pre * (1.0 - sigma))).astype(bfloat)
    grad_up_low = (grad_mixed * silu_gate).astype(bfloat)
    grad_middle_part = cross_cols(grad_gate_low, gate_full) + cross_cols(grad_up_low, up_full)
    grad_gate = cross_rows(middle_low, grad_gate_low)
    grad_up = cross_rows(middle_low, grad_up_low)
    grad_middle = grad_top + lax.psum(grad_middle_part, "col")
    grad_middle_here = mine(grad_middle)
    grad_attn_gain = jnp.sum(grad_middle_here * branch_hat_here, axis=0)
    normed_mid = grad_middle * attn_gain
    inner_mid = jnp.sum(normed_mid * branch_hat, axis=1, keepdims=True)
    grad_branch_low = (branch_scale * (normed_mid - branch_hat * inner_mid / width)).astype(bfloat)
    grad_output = cross_rows(grad_branch_low, attended_low)
    grad_attended_low = matmul(grad_branch_low, output_full).astype(bfloat)

    def attend_back(block):
        queries, keys_part, values_part, segment_part, log_part, grad_part = block
        scores = jnp.einsum("qhd,khd->hqk", queries, keys_part, preferred_element_type=floats)
        scores = jnp.where(visible_pairs(segment_part)[None], scores, MASKED)
        probs = jnp.exp(scores - log_part[..., None])
        grad_values = jnp.einsum(
            "hqk,qhd->khd", probs.astype(bfloat), grad_part, preferred_element_type=floats
        )
        grad_probs = jnp.einsum(
            "qhd,khd->hqk", grad_part, values_part, preferred_element_type=floats
        )
        grad_scores = probs * (grad_probs - jnp.sum(probs * grad_probs, axis=-1, keepdims=True))
        scores_low = grad_scores.astype(bfloat)
        grad_queries = jnp.einsum(
            "hqk,khd->qhd", scores_low, keys_part, preferred_element_type=floats
        )
        grad_keys = jnp.einsum("hqk,qhd->khd", scores_low, queries, preferred_element_type=floats)
        return (grad_queries, grad_keys, grad_values.astype(bfloat))

    grad_queries, grad_keys, grad_values = lax.map(
        attend_back,
        (
            query_blocks,
            key_blocks,
            value_blocks,
            segment_blocks,
            log_totals,
            grad_attended_low.reshape(shape_seq),
        ),
    )
    grad_query_norm = rotate(
        grad_queries.reshape(rows, heads_here, head_size) * scale, cosine, -sine
    ).reshape(rows, local_width)
    grad_key_norm = rotate(grad_keys.reshape(rows, heads_here, head_size), cosine, -sine).reshape(
        rows, local_width
    )
    grad_query_gain = jnp.sum(grad_query_norm * query_hat, axis=0)
    grad_key_gain = jnp.sum(grad_key_norm * key_hat, axis=0)
    normed_query = grad_query_norm * query_gain_here
    normed_key = grad_key_norm * key_gain_here
    inner_query, inner_key = lax.psum(
        (jnp.sum(normed_query * query_hat, axis=1), jnp.sum(normed_key * key_hat, axis=1)), "col"
    )
    grad_query_low = (
        query_scale * (normed_query - query_hat * inner_query[:, None] / width)
    ).astype(bfloat)
    grad_key_low = (key_scale * (normed_key - key_hat * inner_key[:, None] / width)).astype(bfloat)
    grad_value_low = grad_values.reshape(rows, local_width)
    grad_in_part = (
        cross_cols(grad_query_low, query_full)
        + cross_cols(grad_key_low, key_full)
        + cross_cols(grad_value_low, value_full)
    )
    grad_inputs = grad_middle_here + lax.psum_scatter(
        grad_in_part, "col", scatter_dimension=1, tiled=True
    )
    grad_query = cross_rows(whole_in, grad_query_low)
    grad_key = cross_rows(whole_in, grad_key_low)
    grad_value = cross_rows(whole_in, grad_value_low)
    summed = (
        lax.psum_scatter(grad_query, "row", scatter_dimension=0, tiled=True),
        lax.psum_scatter(grad_key, "row", scatter_dimension=0, tiled=True),
        lax.psum_scatter(grad_value, "row", scatter_dimension=0, tiled=True),
        lax.psum_scatter(grad_output, "row", scatter_dimension=0, tiled=True),
        lax.psum_scatter(grad_gate, "row", scatter_dimension=0, tiled=True),
        lax.psum_scatter(grad_up, "row", scatter_dimension=0, tiled=True),
        lax.psum_scatter(grad_down, "row", scatter_dimension=0, tiled=True),
    )
    gains = lax.psum((grad_query_gain, grad_key_gain, grad_attn_gain, grad_mlp_gain), "row")
    return (
        layer_out,
        grad_inputs,
        summed[0],
        summed[1],
        summed[2],
        summed[3],
        summed[4],
        summed[5],
        summed[6],
        gains[0],
        gains[1],
        gains[2],
        gains[3],
    )


BF = jnp.bfloat16
F32 = jnp.float32
MESH_ID = pl.DeviceIdType.MESH
T = 512
DC = 256
DR = 512
D = 2048
FH = 512
LAYER_STAGES = 5
EXACT = lax.Precision.HIGHEST


def dot_nn(a, b):
    return jnp.dot(a, b, preferred_element_type=F32)


def dot_nt(a, b, precision=None):
    return lax.dot_general(
        a, b, (((1,), (1,)), ((), ())), precision=precision, preferred_element_type=F32
    )


def dot_tn(a, b, precision=None):
    return lax.dot_general(
        a, b, (((0,), (0,)), ((), ())), precision=precision, preferred_element_type=F32
    )


def aligned(start, size):
    return pl.ds(pl.multiple_of(start, size), size)


class Counter:
    def __init__(self):
        self.used = 0

    def take(self, count=1):
        first = self.used
        self.used += count
        return first


def block_kernel(
    x_hbm,
    wq_hbm,
    wk_hbm,
    wv_hbm,
    wo_hbm,
    wg_hbm,
    wu_hbm,
    wd_hbm,
    cot_hbm,
    query_gain_ref,
    key_gain_ref,
    attn_gain_ref,
    mlp_gain_ref,
    pos_ref,
    layer_out,
    grad_in,
    gains_out,
    land_mlp,
    land_attn,
    wqkv,
    wo,
    wgu,
    wd,
    x_full,
    mid_full,
    gf_full,
    gb_full,
    gu_s,
    mixed_s,
    probs_s,
    hat_s,
    low_s,
    cos_s,
    sin_s,
    pos_s,
    cot_z,
    braw_s,
    raw_s,
    middle_s,
    bhat_s,
    work_s,
    att_s,
    ga_s,
    gqkv_s,
    gs_s,
    gqk_s,
    own_s,
    stage_c,
    land_c,
    stage_y,
    land_y,
    stage_z,
    land_z,
    scal_s,
    gain_s,
    stage_down,
    stage_gu,
    rel_mlp,
    rel_attn,
    out_lo,
    send_sem,
    recv_sem,
    local_sem,
):
    row = lax.axis_index("row")
    col = lax.axis_index("col")
    x_at = lax.rem(row, 2)
    y_at = lax.div(row, 2)
    core = lax.rem(col, 2)
    z_at = lax.div(col, 2)
    row_x = row + 1 - 2 * x_at
    row_y = lax.rem(row + 2, 4)
    row_d = row_y + 1 - 2 * x_at
    sib = col + 1 - 2 * core
    dev_x = (row_x, col)
    dev_y = (row_y, col)
    dev_d = (row_d, col)
    dev_c = (row, sib)
    z_pair = {
        0: z_at,
        1: z_at + 1 - 2 * lax.rem(z_at, 2),
        2: lax.rem(z_at + 2, 4),
        3: 3 - z_at,
    }
    dev_z = {pair: (row, 2 * z_pair[pair] + core) for pair in (1, 2, 3)}

    counter = Counter()
    locals_used = Counter()
    pending = []

    def copy_of(index, src, dst, device):
        return pltpu.make_async_remote_copy(
            src_ref=src,
            dst_ref=dst,
            send_sem=send_sem.at[index],
            recv_sem=recv_sem.at[index],
            device_id=device,
            device_id_type=MESH_ID,
        )

    def send(index, src, dst, device):
        copy = copy_of(index, src, dst, device)
        copy.start()
        pending.append(copy)
        return copy

    def arrived(index, dst):
        copy_of(index, dst, dst, dev_c).wait_recv()

    def sent(copy):
        copy.wait_send()
        pending[:] = [other for other in pending if other is not copy]

    def local(src, dst):
        copy = pltpu.make_async_copy(src, dst, local_sem.at[locals_used.take()])
        copy.start()
        return copy

    barrier = pltpu.get_barrier_semaphore()
    partners = [dev_x, dev_y, dev_d] + [(row, lax.rem(col + step, 8)) for step in range(1, 8)]
    for device in partners:
        pl.semaphore_signal(barrier, inc=1, device_id=device, device_id_type=MESH_ID)
    half_mine = aligned(y_at * FH, FH)
    half_other = aligned((1 - y_at) * FH, FH)
    rows_mine = aligned(row * DR, DR)
    local_copies = [local(x_hbm, x_full.at[:, aligned(col * DC, DC)]), local(cot_hbm, cot_z.at[z_at])]
    for index, ref in enumerate((wq_hbm, wk_hbm, wv_hbm)):
        local_copies.append(local(ref, wqkv.at[rows_mine, pl.ds(index * DC, DC)]))
    local_copies.append(local(wo_hbm, wo.at[rows_mine, :]))
    local_copies.append(local(wg_hbm.at[:, half_mine], wgu.at[rows_mine, pl.ds(0, FH)]))
    local_copies.append(local(wu_hbm.at[:, half_mine], wgu.at[rows_mine, pl.ds(FH, FH)]))
    local_copies.append(local(wd_hbm.at[:, half_mine], wd.at[rows_mine, :]))
    pl.semaphore_wait(barrier, len(partners))

    class Gather:
        def __init__(self, buf, plane, raw, process):
            self.buf = buf
            self.plane = plane
            self.raw = raw
            self.process = process
            self.base_z = counter.take(3)
            self.base_c = counter.take(4)
            self.rows = pl.ds(0, T)
            if plane:
                self.base_y = counter.take(4)
                self.base_cy = counter.take(4)
                self.rows = aligned(y_at * T, T)
                self.rows_other = aligned((1 - y_at) * T, T)

        def block(self, rows, place, parity=None):
            at = 2 * place + (core if parity is None else parity)
            return rows, aligned(at * DC, DC)

        def start(self):
            self.raw_sends = []
            for pair in (2, 3, 1):
                own = self.raw.at[z_at]
                self.raw_sends.append(send(self.base_z + pair - 1, own, own, dev_z[pair]))

        def finish_own(self):
            for pair in (0, 1, 2, 3):
                place = z_pair[pair]
                if pair:
                    arrived(self.base_z + pair - 1, self.raw.at[place])
                where = self.block(self.rows, place)
                self.buf[where] = self.process(pair, place)
                block = self.buf.at[where]
                if self.plane:
                    send(self.base_y + pair, block, block, dev_y)
                send(self.base_c + pair, block, block, dev_c)
            for pair in range(4):
                arrived(
                    self.base_c + pair, self.buf.at[self.block(self.rows, z_pair[pair], 1 - core)]
                )

        def finish_other(self):
            for pair in range(4):
                block = self.buf.at[self.block(self.rows_other, z_pair[pair])]
                arrived(self.base_y + pair, block)
                send(self.base_cy + pair, block, block, dev_c)
            for pair in range(4):
                arrived(
                    self.base_cy + pair,
                    self.buf.at[self.block(self.rows_other, z_pair[pair], 1 - core)],
                )

    stage_sends = []

    class Reduce:
        ORDER = (2, 3, 1, 0)

        def __init__(self, partial, plane):
            self.partial = partial
            self.plane = plane
            self.count = 2 * T if plane else T
            self.base_c = counter.take(4)
            self.base_z = counter.take(3)
            self.rows = pl.ds(0, T)
            if plane:
                self.base_y = counter.take(4)
                self.rows = aligned(y_at * T, T)
                self.rows_other = aligned((1 - y_at) * T, T)

        def start(self):
            for copy in stage_sends:
                sent(copy)
            stage_sends.clear()
            count = self.count
            for slot, pair in enumerate(self.ORDER):
                target = z_pair[pair]
                start = pl.multiple_of((2 * target + 1 - core) * DC, DC)
                stage_c[slot, :count, :] = self.partial(start).astype(BF)
                stage_sends.append(
                    send(
                        self.base_c + slot,
                        stage_c.at[slot, pl.ds(0, count), :],
                        land_c.at[slot, pl.ds(0, count), :],
                        dev_c,
                    )
                )
                start = pl.multiple_of((2 * target + core) * DC, DC)
                own_s[slot, :count, :] = self.partial(start)
                if slot:
                    self.cores(slot - 1)
            self.cores(3)

        def cores(self, slot):
            count = self.count
            arrived(self.base_c + slot, land_c.at[slot, pl.ds(0, count), :])
            if self.plane:
                rows = self.rows_other
                stage_y[slot] = (own_s[slot, rows, :] + land_c[slot, rows, :].astype(F32)).astype(BF)
                stage_sends.append(
                    send(self.base_y + slot, stage_y.at[slot], land_y.at[slot], dev_y)
                )
                rows = self.rows
                own_s[slot, rows, :] = own_s[slot, rows, :] + land_c[slot, rows, :].astype(F32)
            else:
                self.pass_on(slot, land_c.at[slot, pl.ds(0, T), :])

        def pass_on(self, slot, landed):
            pair = self.ORDER[slot]
            total = own_s[slot, self.rows, :] + landed[...].astype(F32)
            if pair == 0:
                own_s[slot, self.rows, :] = total
            else:
                stage_z[slot] = total.astype(BF)
                stage_sends.append(
                    send(self.base_z + slot, stage_z.at[slot], land_z.at[slot], dev_z[pair])
                )

        def planes(self):
            for slot in range(4):
                arrived(self.base_y + slot, land_y.at[slot])
                self.pass_on(slot, land_y.at[slot])

        def finish(self):
            for slot in range(3):
                arrived(self.base_z + slot, land_z.at[slot])
            total = own_s[3, self.rows, :]
            for slot in range(3):
                total = total + land_z[slot].astype(F32)
            return total

    pick = lax.broadcasted_iota(jnp.int32, (8, DC), 0)
    lane = lax.broadcasted_iota(jnp.int32, (8, DC), 1)
    first_row = (pick == 0).astype(F32)
    second_row = (pick == 1).astype(F32)
    spread = ((pick == 0) & (lane < 128)).astype(F32) + ((pick == 1) & (lane >= 128)).astype(F32)
    scal_base = counter.take(7 * LAYER_STAGES)

    def scal_send(stage, first, second=None):
        mine = dot_nt(first_row, first, EXACT)
        if second is not None:
            mine = mine + dot_nt(second_row, second, EXACT)
        scal_s[stage, col] = mine
        for step in range(1, 8):
            send(
                scal_base + 7 * stage + step - 1,
                scal_s.at[stage, col],
                scal_s.at[stage, col],
                (row, lax.rem(col + step, 8)),
            )

    def scal_get(stage):
        for step in range(1, 8):
            arrived(
                scal_base + 7 * stage + step - 1, scal_s.at[stage, lax.rem(col + 8 - step, 8)]
            )
        total = scal_s[stage, 0]
        for index in range(1, 8):
            total = total + scal_s[stage, index]
        both = dot_tn(total, spread, EXACT)
        return both[:, :128], both[:, 128:]

    def wide(values):
        return jnp.concatenate([values, values], axis=1)

    attn_base = counter.take(16)
    attn_hbm = (wq_hbm, wk_hbm, wv_hbm, wo_hbm)

    def attn_place(index, owner, part=None):
        if part is None:
            rows = aligned(owner * DR, DR)
        else:
            rows = aligned(owner * DR + part * (DR // 2), DR // 2)
        if index < 3:
            return wqkv.at[rows, pl.ds(index * DC, DC)]
        return wo.at[rows, :]

    def attn_send(index):
        send(attn_base + index, attn_hbm[index], attn_place(index, row), dev_x)
        send(attn_base + 4 + index, attn_hbm[index], attn_place(index, row), dev_y)

    def attn_relay(index):
        arrived(attn_base + index, attn_place(index, row_x))
        part = attn_place(index, row_x, 0)
        send(attn_base + 8 + index, part, part, dev_y)
        arrived(attn_base + 4 + index, attn_place(index, row_y))
        part = attn_place(index, row_y, 1)
        send(attn_base + 12 + index, part, part, dev_x)

    def attn_ready(index):
        arrived(attn_base + 8 + index, attn_place(index, row_d, 0))
        arrived(attn_base + 12 + index, attn_place(index, row_d, 1))

    mlp_base = counter.take(9)
    mlp_hbm = (wg_hbm, wu_hbm, wd_hbm)

    def mlp_place(index, owner):
        rows = aligned(owner * DR, DR)
        if index < 2:
            return wgu.at[rows, pl.ds(index * FH, FH)]
        return wd.at[rows, :]

    def mlp_send(index):
        send(mlp_base + index, mlp_hbm[index].at[:, half_mine], mlp_place(index, row), dev_x)
        send(mlp_base + 3 + index, mlp_hbm[index].at[:, half_other], mlp_place(index, row), dev_y)

    def mlp_relay(index):
        place = mlp_place(index, row_y)
        arrived(mlp_base + 3 + index, place)
        send(mlp_base + 6 + index, place, place, dev_x)

    def mlp_ready(index):
        arrived(mlp_base + index, mlp_place(index, row_x))
        arrived(mlp_base + 6 + index, mlp_place(index, row_d))

    for index in range(3):
        attn_send(index)

    x_base = counter.take(7)
    cot_base = counter.take(3)

    def x_block(place, parity):
        return x_full.at[:, aligned((2 * place + parity) * DC, DC)]

    for pair in (2, 3, 1):
        send(x_base + pair - 1, x_hbm, x_block(z_at, core), dev_z[pair])
    send(x_base + 3, x_hbm, x_block(z_at, core), dev_c)

    position_rows = jnp.broadcast_to(pos_ref[...].astype(F32), (8, T))
    position = dot_tn(position_rows, first_row[:, :HD], EXACT)
    pos_s[...] = position.astype(jnp.int32)
    lane_at = lax.broadcasted_iota(jnp.int32, (1, HD), 1)
    within = lax.rem(lane_at, HD // 2).astype(F32)
    frequency = jnp.exp(within * (-2.0 * math.log(THETA) / HD))
    angles = position * frequency
    cos_s[...] = jnp.cos(angles)
    sine = jnp.sin(angles)
    sin_s[...] = jnp.where(lane_at < HD // 2, -sine, sine)

    for index in range(3):
        attn_relay(index)
    attn_send(3)
    for pair in (1, 2, 3):
        block = x_block(z_pair[pair], core)
        arrived(x_base + pair - 1, block)
        send(x_base + 3 + pair, block, block, dev_c)
    for copy in local_copies:
        copy.wait()
    for pair in (2, 3, 1):
        send(cot_base + pair - 1, cot_z.at[z_at], cot_z.at[z_at], dev_z[pair])
    for pair in range(4):
        arrived(x_base + 3 + pair, x_block(z_pair[pair], 1 - core))
    attn_ready(0)
    attn_ready(1)

    def gain_at(ref, at):
        return ref[:, aligned(at * DC, DC)]

    qk_gain = (gain_at(query_gain_ref, col), gain_at(key_gain_ref, col))
    for index in range(2):
        hat_s[index] = dot_nn(x_full[...], wqkv[:, pl.ds(index * DC, DC)])
    scal_send(0, hat_s[0] * hat_s[0], hat_s[1] * hat_s[1])
    attn_relay(3)
    for index in range(3):
        mlp_send(index)
    attn_ready(2)
    low_s[2] = dot_nn(x_full[...], wqkv[:, pl.ds(2 * DC, DC)]).astype(BF)
    scales = [lax.rsqrt(total / D + EPS) for total in scal_get(0)]
    work_s[0] = jnp.concatenate(scales, axis=1)
    for index in range(2):
        hat = hat_s[index] * wide(scales[index])
        hat_s[index] = hat
        normed = hat * qk_gain[index]
        for head in range(2):
            part = normed[:, head * HD : (head + 1) * HD]
            turned = part * cos_s[...] + pltpu.roll(part, HD // 2, 1) * sin_s[...]
            if index == 0:
                turned = turned * (HD**-0.5)
            low_s[index, :, pl.ds(head * HD, HD)] = turned.astype(BF)

    chunk = 128

    def visible(at):
        query = at * chunk + lax.broadcasted_iota(jnp.int32, (chunk, T), 0)
        key = lax.broadcasted_iota(jnp.int32, (chunk, T), 1)
        oldest = query - pos_s[aligned(at * chunk, chunk), :1]
        return (key <= query) & (key >= oldest)

    def attend_chunk(at, carry):
        rows = aligned(at * chunk, chunk)
        allowed = visible(at)
        for head in range(2):
            lanes = pl.ds(head * HD, HD)
            scores = dot_nt(low_s[0, rows, lanes], low_s[1, :, lanes])
            scores = jnp.where(allowed, scores, MASKED)
            exponent = jnp.exp(scores - jnp.max(scores, axis=1, keepdims=True))
            probs = exponent / jnp.sum(exponent, axis=1, keepdims=True)
            probs_s[head, rows, :] = probs
            att_s[rows, lanes] = dot_nn(probs.astype(BF), low_s[2, :, lanes]).astype(BF)
        return carry

    lax.fori_loop(0, T // chunk, attend_chunk, 0)

    attn_ready(3)
    branch_sum = Reduce(lambda start: dot_nt(att_s[...], wo[pl.ds(start, DC), :]), False)
    branch_sum.start()
    mlp_relay(0)
    branch = branch_sum.finish()
    scal_send(1, branch * branch)
    work_s[1] = branch
    braw_s[z_at] = branch.astype(BF)

    def middle_block(pair, place):
        at = 2 * place + core
        raw = work_s[1] if pair == 0 else braw_s[place].astype(F32)
        hat = raw * wide(work_s[2, :, :128])
        inputs = x_full[:, aligned(at * DC, DC)].astype(F32)
        middle = inputs + hat * gain_at(attn_gain_ref, at)
        if pair == 0:
            bhat_s[...] = hat
            middle_s[...] = middle
        return middle.astype(BF)

    mid_gather = Gather(mid_full, True, braw_s, middle_block)
    mid_gather.start()
    total, _ = scal_get(1)
    work_s[2, :, :128] = lax.rsqrt(total / D + EPS)
    mlp_relay(1)
    mlp_relay(2)
    mid_gather.finish_own()
    mlp_ready(0)
    mlp_ready(1)

    tile = 256

    def forward_tiles(rows):
        def forward_tile(at, carry):
            lanes = aligned(at * tile, tile)
            lanes_up = aligned(at * tile + FH, tile)
            gate = dot_nn(mid_full[rows, :], wgu[:, lanes])
            up = dot_nn(mid_full[rows, :], wgu[:, lanes_up])
            gu_s[rows, lanes] = gate.astype(BF)
            gu_s[rows, lanes_up] = up.astype(BF)
            mixed_s[rows, lanes] = (gate * jax.nn.sigmoid(gate) * up).astype(BF)
            return carry

        lax.fori_loop(0, FH // tile, forward_tile, 0)

    forward_tiles(mid_gather.rows)
    mid_gather.finish_other()
    forward_tiles(mid_gather.rows_other)
    mlp_ready(2)
    ffn_sum = Reduce(lambda start: dot_nt(mixed_s[...], wd[pl.ds(start, DC), :]), True)
    ffn_sum.start()
    ffn_sum.planes()
    ffn = ffn_sum.finish()
    cot = cot_z[z_at].astype(F32)
    mlp_gain = gain_at(mlp_gain_ref, col)
    scal_send(2, ffn * ffn, cot * mlp_gain * ffn)
    work_s[1] = ffn
    raw_s[z_at] = ffn.astype(BF)

    def grad_ffn_block(pair, place):
        at = 2 * place + core
        raw = work_s[1] if pair == 0 else raw_s[place].astype(F32)
        scale = wide(work_s[2, :, 128:])
        grad = cot_z[place].astype(F32) * gain_at(mlp_gain_ref, at)
        return (scale * (grad - raw * scale * wide(own_s[0, pl.ds(0, T), :128]))).astype(BF)

    gf_gather = Gather(gf_full, True, raw_s, grad_ffn_block)
    gf_gather.start()
    for pair in (1, 2, 3):
        arrived(cot_base + pair - 1, cot_z.at[z_pair[pair]])
    total, inner = scal_get(2)
    ffn_scale = lax.rsqrt(total / D + EPS)
    work_s[2, :, 128:] = ffn_scale
    own_s[0, pl.ds(0, T), :128] = inner * ffn_scale / D
    ffn_hat = work_s[1] * wide(ffn_scale)
    out_lo[...] = (middle_s[...] + ffn_hat * mlp_gain).astype(BF)
    lo_copy = local(out_lo, layer_out)
    gain_s[row, 3:4, :] = jnp.sum(cot * ffn_hat, axis=0, keepdims=True)
    gf_gather.finish_own()

    def backward_tiles(rows):
        def backward_tile(at, carry):
            lanes = aligned(at * tile, tile)
            lanes_up = aligned(at * tile + FH, tile)
            grad_mixed = dot_nn(gf_full[rows, :], wd[:, lanes])
            gate = gu_s[rows, lanes].astype(F32)
            up = gu_s[rows, lanes_up].astype(F32)
            sigma = jax.nn.sigmoid(gate)
            gu_s[rows, lanes] = (grad_mixed * up * sigma * (1.0 + gate * (1.0 - sigma))).astype(BF)
            gu_s[rows, lanes_up] = (grad_mixed * gate * sigma).astype(BF)
            return carry

        lax.fori_loop(0, FH // tile, backward_tile, 0)

    backward_tiles(gf_gather.rows)
    gf_gather.finish_other()
    backward_tiles(gf_gather.rows_other)

    def lanes_of(owner):
        return aligned(owner * DR, DR)

    GU = pl.ds(0, 2 * FH)
    DOWN = pl.ds(2 * FH, FH)

    def down_piece(owner):
        return dot_tn(gf_full[:, lanes_of(owner)], mixed_s[...])

    def gu_piece(owner, part):
        return dot_tn(mid_full[:, lanes_of(owner)], gu_s[:, pl.ds(part * FH, FH)])

    def gu_stage(slot, owner):
        for part in range(2):
            stage_gu[slot, :, pl.ds(part * FH, FH)] = gu_piece(owner, part).astype(BF)

    grad_base = counter.take(6)
    stage_down[0] = down_piece(row_d).astype(BF)
    down_sends = [send(grad_base, stage_down.at[0], rel_mlp.at[:, DOWN], dev_x)]
    mid_sum = Reduce(lambda start: dot_nt(gu_s[...], wgu[pl.ds(start, DC), :]), True)
    mid_sum.start()
    gu_stage(0, row_d)
    gu_sends = [send(grad_base + 1, stage_gu.at[0], rel_mlp.at[:, GU], dev_x)]
    stage_down[1] = down_piece(row_x).astype(BF)
    down_sends.append(send(grad_base + 2, stage_down.at[1], land_mlp.at[1, :, DOWN], dev_x))
    mid_sum.planes()
    arrived(grad_base, rel_mlp.at[:, DOWN])
    stage_down[2] = (down_piece(row_y) + rel_mlp[:, DOWN].astype(F32)).astype(BF)
    down_sends.append(send(grad_base + 4, stage_down.at[2], land_mlp.at[2, :, DOWN], dev_y))
    gu_stage(1, row_x)
    gu_sends.append(send(grad_base + 3, stage_gu.at[1], land_mlp.at[1, :, GU], dev_x))
    grad_middle = cot_z[z_at].astype(F32) + mid_sum.finish()
    attn_gain = gain_at(attn_gain_ref, col)
    scal_send(3, grad_middle * attn_gain * bhat_s[...])
    middle_s[...] = grad_middle
    for copy in gf_gather.raw_sends:
        sent(copy)
    raw_s[z_at] = grad_middle.astype(BF)

    def grad_branch_block(pair, place):
        at = 2 * place + core
        scale = wide(work_s[2, :, :128])
        raw = middle_s[...] if pair == 0 else raw_s[place].astype(F32)
        hat = bhat_s[...] if pair == 0 else braw_s[place].astype(F32) * scale
        inner = wide(own_s[0, pl.ds(0, T), :128])
        return (scale * (raw * gain_at(attn_gain_ref, at) - hat * inner)).astype(BF)

    gb_gather = Gather(gb_full, False, raw_s, grad_branch_block)
    gb_gather.start()
    gain_s[row, 2:3, :] = jnp.sum(middle_s[...] * bhat_s[...], axis=0, keepdims=True)
    inner, _ = scal_get(3)
    own_s[0, pl.ds(0, T), :128] = inner / D
    arrived(grad_base + 1, rel_mlp.at[:, GU])
    for part in range(2):
        half = pl.ds(part * FH, FH)
        stage_gu[2, :, half] = (gu_piece(row_y, part) + rel_mlp[:, half].astype(F32)).astype(BF)
    gu_sends.append(send(grad_base + 5, stage_gu.at[2], land_mlp.at[2, :, GU], dev_y))
    gb_gather.finish_own()

    ga_s[...] = dot_nn(gb_full[...], wo[...]).astype(BF)

    upper = pl.ds(0, DR // 2)
    lower = pl.ds(DR // 2, DR // 2)
    attn_grad_base = counter.take(3 * 6)
    late = []

    class AttnGrad:
        def __init__(self, order, left, right, stage, stage_lanes, lanes):
            self.base = attn_grad_base + 6 * order
            self.left, self.right = left, right
            self.stage, self.stage_lanes, self.lanes = stage, stage_lanes, lanes

        def at(self, slot, rows):
            return self.stage.at[slot, rows, self.stage_lanes]

        def start(self):
            for slot, owner in enumerate((row_d, row_x, row_y, row)):
                self.stage[slot, :, self.stage_lanes] = dot_tn(
                    self.left[:, lanes_of(owner)], self.right()
                ).astype(BF)
                if slot == 0:
                    send(self.base, self.at(0, upper), rel_attn.at[upper, self.lanes], dev_x)
                    send(self.base + 1, self.at(0, lower), rel_attn.at[lower, self.lanes], dev_y)
                elif slot == 1:
                    landing = land_attn.at[1, upper, self.lanes]
                    send(self.base + 2, self.at(1, upper), landing, dev_x)
                elif slot == 2:
                    landing = land_attn.at[2, lower, self.lanes]
                    send(self.base + 3, self.at(2, lower), landing, dev_y)
                else:
                    whole = self.at(3, pl.ds(0, DR))
                    late.append(local(whole, land_attn.at[0, :, self.lanes]))

        def relay(self):
            for step, (slot, rows, device) in enumerate(((2, upper, dev_y), (1, lower, dev_x))):
                arrived(self.base + step, rel_attn.at[rows, self.lanes])
                self.stage[slot, rows, self.stage_lanes] = (
                    self.stage[slot, rows, self.stage_lanes].astype(F32)
                    + rel_attn[rows, self.lanes].astype(F32)
                ).astype(BF)
                send(
                    self.base + 4 + step,
                    self.at(slot, rows),
                    land_attn.at[slot, rows, self.lanes],
                    device,
                )

        def finish(self):
            arrived(self.base + 2, land_attn.at[1, upper, self.lanes])
            arrived(self.base + 3, land_attn.at[2, lower, self.lanes])
            arrived(self.base + 4, land_attn.at[2, upper, self.lanes])
            arrived(self.base + 5, land_attn.at[1, lower, self.lanes])

    stage_down[3] = down_piece(row).astype(BF)
    own_copies = [local(stage_down.at[3], land_mlp.at[0, :, DOWN])]
    for copy in down_sends:
        sent(copy)
    own_copies[0].wait()
    first_lanes = pl.ds(0, DC)
    o_grad = AttnGrad(
        0, gb_full, lambda: att_s[...], stage_down, first_lanes, pl.ds(3 * DC, DC)
    )
    o_grad.start()

    def attend_back_chunk(at, carry):
        rows = aligned(at * chunk, chunk)
        for head in range(2):
            lanes = pl.ds(head * HD, HD)
            grad_probs = dot_nt(ga_s[rows, lanes], low_s[2, :, lanes])
            probs = probs_s[head, rows, :]
            inner = jnp.sum(probs * grad_probs, axis=1, keepdims=True)
            grad_scores = (probs * (grad_probs - inner)).astype(BF)
            gs_s[head, rows, :] = grad_scores
            gqk_s[0, rows, lanes] = dot_nn(grad_scores, low_s[1, :, lanes])
        return carry

    lax.fori_loop(0, T // chunk, attend_back_chunk, 0)
    for head in range(2):
        lanes = pl.ds(head * HD, HD)
        gqk_s[1, :, lanes] = dot_tn(gs_s[head], low_s[0, :, lanes])
    inners = []
    for index in range(2):
        for head in range(2):
            lanes = pl.ds(head * HD, HD)
            part = gqk_s[index, :, lanes]
            turned = part * cos_s[...] - pltpu.roll(part, HD // 2, 1) * sin_s[...]
            if index == 0:
                turned = turned * (HD**-0.5)
            gqk_s[index, :, lanes] = turned
        weighted = gqk_s[index] * hat_s[index]
        gain_s[row, index : index + 1, :] = jnp.sum(weighted, axis=0, keepdims=True)
        inners.append(weighted * qk_gain[index])
    scal_send(4, inners[0], inners[1])
    gain_base = counter.take(3)
    for slot, device in enumerate((dev_x, dev_y, dev_d)):
        send(gain_base + slot, gain_s.at[row], gain_s.at[row], device)
    for head in range(2):
        lanes = pl.ds(head * HD, HD)
        gqkv_s[:, pl.ds(2 * DC + head * HD, HD)] = dot_tn(
            probs_s[head].astype(BF), ga_s[:, lanes]
        ).astype(BF)
    v_grad = AttnGrad(
        1,
        x_full,
        lambda: gqkv_s[:, 2 * DC :],
        stage_down,
        pl.ds(DC, DC),
        pl.ds(2 * DC, DC),
    )
    v_grad.start()
    totals = scal_get(4)
    for index in range(2):
        scale = wide(work_s[0, :, index * 128 : (index + 1) * 128])
        gqkv_s[:, pl.ds(index * DC, DC)] = (
            scale * (gqk_s[index] * qk_gain[index] - hat_s[index] * wide(totals[index] / D))
        ).astype(BF)
    in_sum = Reduce(lambda start: dot_nt(gqkv_s[...], wqkv[pl.ds(start, DC), :]), False)
    in_sum.start()
    o_grad.relay()
    gu_stage(3, row)
    own_copies.append(local(stage_gu.at[3], land_mlp.at[0, :, GU]))
    for copy in gu_sends:
        sent(copy)
    own_copies[1].wait()
    both_lanes = pl.ds(0, 2 * DC)
    qk_grad = AttnGrad(
        2, x_full, lambda: gqkv_s[:, : 2 * DC], stage_gu, both_lanes, both_lanes
    )
    qk_grad.start()
    v_grad.relay()
    work_s[1] = middle_s[...] + in_sum.finish()
    late.append(local(work_s.at[1], grad_in))
    late.append(lo_copy)
    qk_grad.relay()

    for slot, owner in enumerate((row_x, row_y, row_d)):
        arrived(gain_base + slot, gain_s.at[owner])
    gains_out[...] = gain_s[0] + gain_s[1] + gain_s[2] + gain_s[3]
    for index, (slot, lanes) in enumerate(((1, DOWN), (1, GU), (2, DOWN), (2, GU))):
        arrived(grad_base + 2 + index, land_mlp.at[slot, :, lanes])
    for grad in (o_grad, v_grad, qk_grad):
        grad.finish()
    for copy in late:
        copy.wait()
    for copy in pending:
        copy.wait_send()


def total_kernel(
    lo_ref, gin_ref, gains_ref, mlp_ref, attn_ref, lo_out, gin_out, *outs
):
    y_at = lax.div(lax.axis_index("row"), 2)
    lo_out[...] = lo_ref[...]
    gin_out[...] = gin_ref[...]
    attn = attn_ref[0].astype(F32) + attn_ref[1].astype(F32) + attn_ref[2].astype(F32)
    for index in range(4):
        outs[index][...] = attn[:, index * DC : (index + 1) * DC]
    mine = mlp_ref[0].astype(F32) + mlp_ref[1].astype(F32)
    other = mlp_ref[2].astype(F32)
    for index in range(3):
        lanes = slice(index * FH, (index + 1) * FH)
        outs[4 + index][:, aligned(y_at * FH, FH)] = mine[:, lanes]
        outs[4 + index][:, aligned((1 - y_at) * FH, FH)] = other[:, lanes]
    for index in range(4):
        outs[7 + index][...] = gains_ref[index : index + 1, :]


MIB = 1 << 20


def on_device_kernel(
    inputs,
    query_weight,
    key_weight,
    value_weight,
    output_weight,
    gate_weight,
    up_weight,
    down_weight,
    query_gain,
    key_gain,
    attn_gain,
    mlp_gain,
    positions,
    segments,
    cotangent,
):
    hbm = pl.BlockSpec(memory_space=pl.ANY)
    vmem = pl.BlockSpec(memory_space=pltpu.VMEM)
    sds = jax.ShapeDtypeStruct
    copies = 240
    landed = pl.pallas_call(
        block_kernel,
        out_shape=[
            sds((T, DC), BF),
            sds((T, DC), F32),
            sds((8, DC), F32),
            sds((3, DR, 3 * FH), BF),
            sds((3, DR, 4 * DC), BF),
        ],
        in_specs=[hbm] * 9 + [vmem] * 5,
        out_specs=[hbm, hbm, vmem, hbm, hbm],
        scratch_shapes=[
            pltpu.VMEM((D, 3 * DC), BF),
            pltpu.VMEM((D, DC), BF),
            pltpu.VMEM((D, 2 * FH), BF),
            pltpu.VMEM((D, FH), BF),
            pltpu.VMEM((T, D), BF),
            pltpu.VMEM((2 * T, D), BF),
            pltpu.VMEM((2 * T, D), BF),
            pltpu.VMEM((T, D), BF),
            pltpu.VMEM((2 * T, 2 * FH), BF),
            pltpu.VMEM((2 * T, FH), BF),
            pltpu.VMEM((2, T, T), F32),
            pltpu.VMEM((2, T, DC), F32),
            pltpu.VMEM((3, T, DC), BF),
            pltpu.VMEM((T, HD), F32),
            pltpu.VMEM((T, HD), F32),
            pltpu.VMEM((T, HD), jnp.int32),
            pltpu.VMEM((4, T, DC), BF),
            pltpu.VMEM((4, T, DC), BF),
            pltpu.VMEM((4, T, DC), BF),
            pltpu.VMEM((T, DC), F32),
            pltpu.VMEM((T, DC), F32),
            pltpu.VMEM((3, T, DC), F32),
            pltpu.VMEM((T, DC), BF),
            pltpu.VMEM((T, DC), BF),
            pltpu.VMEM((T, 3 * DC), BF),
            pltpu.VMEM((2, T, T), BF),
            pltpu.VMEM((2, T, DC), F32),
            pltpu.VMEM((4, 2 * T, DC), F32),
            pltpu.VMEM((4, 2 * T, DC), BF),
            pltpu.VMEM((4, 2 * T, DC), BF),
            pltpu.VMEM((4, T, DC), BF),
            pltpu.VMEM((4, T, DC), BF),
            pltpu.VMEM((3, T, DC), BF),
            pltpu.VMEM((3, T, DC), BF),
            pltpu.VMEM((LAYER_STAGES, 8, 8, T), F32),
            pltpu.VMEM((4, 8, DC), F32),
            pltpu.VMEM((4, DR, FH), BF),
            pltpu.VMEM((4, DR, 2 * FH), BF),
            pltpu.VMEM((DR, 3 * FH), BF),
            pltpu.VMEM((DR, 4 * DC), BF),
            pltpu.VMEM((T, DC), BF),
            pltpu.SemaphoreType.DMA((copies,)),
            pltpu.SemaphoreType.DMA((copies,)),
            pltpu.SemaphoreType.DMA((32,)),
        ],
        compiler_params=pltpu.CompilerParams(
            collective_id=0, has_side_effects=True, vmem_limit_bytes=64 * MIB
        ),
        cost_estimate=pl.CostEstimate(
            flops=26_800_000_000, bytes_accessed=16_000_000, transcendentals=2_000_000
        ),
    )(
        inputs,
        query_weight,
        key_weight,
        value_weight,
        output_weight,
        gate_weight,
        up_weight,
        down_weight,
        cotangent,
        query_gain[None, :],
        key_gain[None, :],
        attn_gain[None, :],
        mlp_gain[None, :],
        positions[None, :],
    )
    step = 64

    def rows_of(width):
        return pl.BlockSpec((step, width), lambda at: (at, 0))

    gain_spec = pl.BlockSpec((1, DC), lambda at: (0, 0))
    results = pl.pallas_call(
        total_kernel,
        grid=(DR // step,),
        out_shape=[sds((T, DC), BF), sds((T, DC), F32)]
        + [sds((DR, DC), F32)] * 4
        + [sds((DR, 2 * FH), F32)] * 3
        + [sds((1, DC), F32)] * 4,
        in_specs=[
            rows_of(DC),
            rows_of(DC),
            pl.BlockSpec((8, DC), lambda at: (0, 0)),
            pl.BlockSpec((3, step, 3 * FH), lambda at: (0, at, 0)),
            pl.BlockSpec((3, step, 4 * DC), lambda at: (0, at, 0)),
        ],
        out_specs=[rows_of(DC)] * 6 + [rows_of(2 * FH)] * 3 + [gain_spec] * 4,
    )(*landed)
    return (*results[:9], *[gain[0] for gain in results[9:]])


def solution(mesh):
    in_specs = (
        P("row", "col"),
        P("row", "col"),
        P("row", "col"),
        P("row", "col"),
        P("row", "col"),
        P("row", "col"),
        P("row", "col"),
        P("row", "col"),
        P(),
        P(),
        P(),
        P(),
        P("row"),
        P("row"),
        P("row", "col"),
    )
    out_specs = (
        P("row", "col"),
        P("row", "col"),
        P("row", "col"),
        P("row", "col"),
        P("row", "col"),
        P("row", "col"),
        P("row", "col"),
        P("row", "col"),
        P("row", "col"),
        P("col"),
        P("col"),
        P("col"),
        P("col"),
    )
    sizes = (mesh.shape["row"], mesh.shape["col"])
    body = on_device_kernel if sizes == (4, 8) else on_device
    return jax.shard_map(
        body, mesh=mesh, in_specs=in_specs, out_specs=out_specs, check_vma=False
    )
```

```python
import math

import jax
import jax.numpy as jnp
from jax import lax
from jax.experimental import pallas as pl
from jax.experimental.pallas import tpu as pltpu
from jax.sharding import PartitionSpec as P

HD = 128
LENGTH = 512


EPS = 1e-06
THETA = 500000.0
MASKED = -1e30


def rope_tables(positions, head_size):
    halfway = head_size // 2
    frequency = jnp.exp(
        jnp.arange(halfway, dtype=jnp.float32) * (-2.0 * math.log(THETA) / head_size)
    )
    angles = positions.astype(jnp.float32)[:, None] * frequency[None, :]
    return (jnp.cos(angles)[:, None, :], jnp.sin(angles)[:, None, :])


def rotate(values, cosine, sine):
    halfway = values.shape[-1] // 2
    first_half = values[..., :halfway]
    second_half = values[..., halfway:]
    return jnp.concatenate(
        [first_half * cosine - second_half * sine, second_half * cosine + first_half * sine],
        axis=-1,
    )


def matmul(left, right):
    return jnp.dot(left, right, preferred_element_type=jnp.float32)


def cross_rows(left, right):
    return lax.dot_general(
        left, right, (((0,), (0,)), ((), ())), preferred_element_type=jnp.float32
    )


def cross_cols(left, right):
    return lax.dot_general(
        left, right, (((1,), (1,)), ((), ())), preferred_element_type=jnp.float32
    )


def visible_pairs(segment_part):
    places = jnp.arange(segment_part.shape[0])
    return (segment_part[:, None] == segment_part[None, :]) & (places[:, None] >= places[None, :])


def on_device(
    inputs,
    query_weight,
    key_weight,
    value_weight,
    output_weight,
    gate_weight,
    up_weight,
    down_weight,
    query_gain,
    key_gain,
    attn_gain,
    mlp_gain,
    positions,
    segments,
    cotangent,
):
    bfloat = jnp.bfloat16
    floats = jnp.float32
    rows = inputs.shape[0]
    local_width = inputs.shape[1]
    width = local_width * lax.axis_size("col")
    offset = lax.axis_index("col") * local_width
    head_size = HD
    heads_here = local_width // head_size
    sequences = rows // LENGTH
    scale = head_size ** (-0.5)
    shape_seq = (sequences, LENGTH, heads_here, head_size)

    def mine(values):
        return lax.dynamic_slice_in_dim(values, offset, local_width, values.ndim - 1)

    query_gain_here = mine(query_gain)
    key_gain_here = mine(key_gain)
    cot_here = cotangent.astype(floats)
    gathered = (
        lax.all_gather(query_weight, "row", axis=0, tiled=True),
        lax.all_gather(key_weight, "row", axis=0, tiled=True),
        lax.all_gather(value_weight, "row", axis=0, tiled=True),
        lax.all_gather(gate_weight, "row", axis=0, tiled=True),
        lax.all_gather(up_weight, "row", axis=0, tiled=True),
        lax.all_gather(output_weight, "row", axis=0, tiled=True),
        lax.all_gather(down_weight, "row", axis=0, tiled=True),
    )
    query_full, key_full, value_full, gate_full, up_full, output_full, down_full = gathered
    whole_in = lax.all_gather(inputs, "col", axis=1, tiled=True)
    query_raw = matmul(whole_in, query_full)
    key_raw = matmul(whole_in, key_full)
    value_raw = matmul(whole_in, value_full)
    query_total, key_total = lax.psum(
        (jnp.sum(query_raw * query_raw, axis=1), jnp.sum(key_raw * key_raw, axis=1)), "col"
    )
    query_scale = lax.rsqrt(query_total / width + EPS)[:, None]
    key_scale = lax.rsqrt(key_total / width + EPS)[:, None]
    query_hat = query_raw * query_scale
    key_hat = key_raw * key_scale
    cosine, sine = rope_tables(positions, head_size)
    query_low = (
        rotate((query_hat * query_gain_here).reshape(rows, heads_here, head_size), cosine, sine)
        * scale
    ).astype(bfloat)
    key_low = rotate(
        (key_hat * key_gain_here).reshape(rows, heads_here, head_size), cosine, sine
    ).astype(bfloat)
    value_low = value_raw.astype(bfloat).reshape(rows, heads_here, head_size)
    query_blocks = query_low.reshape(shape_seq)
    key_blocks = key_low.reshape(shape_seq)
    value_blocks = value_low.reshape(shape_seq)
    segment_blocks = segments.reshape(sequences, LENGTH)

    def attend(block):
        queries, keys_part, values_part, segment_part = block
        scores = jnp.einsum("qhd,khd->hqk", queries, keys_part, preferred_element_type=floats)
        scores = jnp.where(visible_pairs(segment_part)[None], scores, MASKED)
        largest = jnp.max(scores, axis=-1, keepdims=True)
        exponent = jnp.exp(scores - largest)
        totals = jnp.sum(exponent, axis=-1, keepdims=True)
        weights_low = (exponent / totals).astype(bfloat)
        attended_part = jnp.einsum(
            "hqk,khd->qhd", weights_low, values_part, preferred_element_type=floats
        )
        return (attended_part, (largest + jnp.log(totals))[..., 0])

    attended, log_totals = lax.map(attend, (query_blocks, key_blocks, value_blocks, segment_blocks))
    attended_low = attended.reshape(rows, local_width).astype(bfloat)
    branch = lax.psum(cross_cols(attended_low, output_full), "col")
    branch_scale = lax.rsqrt(jnp.mean(branch * branch, axis=1, keepdims=True) + EPS)
    branch_hat = branch * branch_scale
    middle = whole_in.astype(floats) + branch_hat * attn_gain
    middle_low = middle.astype(bfloat)
    middle_here = mine(middle)
    branch_hat_here = mine(branch_hat)
    gate_pre = matmul(middle_low, gate_full)
    up_pre = matmul(middle_low, up_full)
    sigma = jax.nn.sigmoid(gate_pre)
    silu_gate = gate_pre * sigma
    mixed_low = (silu_gate * up_pre).astype(bfloat)
    ffn = lax.psum(cross_cols(mixed_low, down_full), "col")
    ffn_scale = lax.rsqrt(jnp.mean(ffn * ffn, axis=1, keepdims=True) + EPS)
    ffn_hat = ffn * ffn_scale
    ffn_hat_here = mine(ffn_hat)
    grad_top = lax.all_gather(cotangent, "col", axis=1, tiled=True).astype(floats)
    normed_top = grad_top * mlp_gain
    inner_top = jnp.sum(normed_top * ffn_hat, axis=1, keepdims=True)
    grad_ffn_low = (ffn_scale * (normed_top - ffn_hat * inner_top / width)).astype(bfloat)
    layer_out = (middle_here + ffn_hat_here * mine(mlp_gain)).astype(bfloat)
    grad_mlp_gain = jnp.sum(cot_here * ffn_hat_here, axis=0)
    grad_down = cross_rows(grad_ffn_low, mixed_low)
    grad_mixed = matmul(grad_ffn_low, down_full)
    grad_gate_low = (grad_mixed * up_pre * sigma * (1.0 + gate_pre * (1.0 - sigma))).astype(bfloat)
    grad_up_low = (grad_mixed * silu_gate).astype(bfloat)
    grad_middle_part = cross_cols(grad_gate_low, gate_full) + cross_cols(grad_up_low, up_full)
    grad_gate = cross_rows(middle_low, grad_gate_low)
    grad_up = cross_rows(middle_low, grad_up_low)
    grad_middle = grad_top + lax.psum(grad_middle_part, "col")
    grad_middle_here = mine(grad_middle)
    grad_attn_gain = jnp.sum(grad_middle_here * branch_hat_here, axis=0)
    normed_mid = grad_middle * attn_gain
    inner_mid = jnp.sum(normed_mid * branch_hat, axis=1, keepdims=True)
    grad_branch_low = (branch_scale * (normed_mid - branch_hat * inner_mid / width)).astype(bfloat)
    grad_output = cross_rows(grad_branch_low, attended_low)
    grad_attended_low = matmul(grad_branch_low, output_full).astype(bfloat)

    def attend_back(block):
        queries, keys_part, values_part, segment_part, log_part, grad_part = block
        scores = jnp.einsum("qhd,khd->hqk", queries, keys_part, preferred_element_type=floats)
        scores = jnp.where(visible_pairs(segment_part)[None], scores, MASKED)
        probs = jnp.exp(scores - log_part[..., None])
        grad_values = jnp.einsum(
            "hqk,qhd->khd", probs.astype(bfloat), grad_part, preferred_element_type=floats
        )
        grad_probs = jnp.einsum(
            "qhd,khd->hqk", grad_part, values_part, preferred_element_type=floats
        )
        grad_scores = probs * (grad_probs - jnp.sum(probs * grad_probs, axis=-1, keepdims=True))
        scores_low = grad_scores.astype(bfloat)
        grad_queries = jnp.einsum(
            "hqk,khd->qhd", scores_low, keys_part, preferred_element_type=floats
        )
        grad_keys = jnp.einsum("hqk,qhd->khd", scores_low, queries, preferred_element_type=floats)
        return (grad_queries, grad_keys, grad_values.astype(bfloat))

    grad_queries, grad_keys, grad_values = lax.map(
        attend_back,
        (
            query_blocks,
            key_blocks,
            value_blocks,
            segment_blocks,
            log_totals,
            grad_attended_low.reshape(shape_seq),
        ),
    )
    grad_query_norm = rotate(
        grad_queries.reshape(rows, heads_here, head_size) * scale, cosine, -sine
    ).reshape(rows, local_width)
    grad_key_norm = rotate(grad_keys.reshape(rows, heads_here, head_size), cosine, -sine).reshape(
        rows, local_width
    )
    grad_query_gain = jnp.sum(grad_query_norm * query_hat, axis=0)
    grad_key_gain = jnp.sum(grad_key_norm * key_hat, axis=0)
    normed_query = grad_query_norm * query_gain_here
    normed_key = grad_key_norm * key_gain_here
    inner_query, inner_key = lax.psum(
        (jnp.sum(normed_query * query_hat, axis=1), jnp.sum(normed_key * key_hat, axis=1)), "col"
    )
    grad_query_low = (
        query_scale * (normed_query - query_hat * inner_query[:, None] / width)
    ).astype(bfloat)
    grad_key_low = (key_scale * (normed_key - key_hat * inner_key[:, None] / width)).astype(bfloat)
    grad_value_low = grad_values.reshape(rows, local_width)
    grad_in_part = (
        cross_cols(grad_query_low, query_full)
        + cross_cols(grad_key_low, key_full)
        + cross_cols(grad_value_low, value_full)
    )
    grad_inputs = grad_middle_here + lax.psum_scatter(
        grad_in_part, "col", scatter_dimension=1, tiled=True
    )
    grad_query = cross_rows(whole_in, grad_query_low)
    grad_key = cross_rows(whole_in, grad_key_low)
    grad_value = cross_rows(whole_in, grad_value_low)
    summed = (
        lax.psum_scatter(grad_query, "row", scatter_dimension=0, tiled=True),
        lax.psum_scatter(grad_key, "row", scatter_dimension=0, tiled=True),
        lax.psum_scatter(grad_value, "row", scatter_dimension=0, tiled=True),
        lax.psum_scatter(grad_output, "row", scatter_dimension=0, tiled=True),
        lax.psum_scatter(grad_gate, "row", scatter_dimension=0, tiled=True),
        lax.psum_scatter(grad_up, "row", scatter_dimension=0, tiled=True),
        lax.psum_scatter(grad_down, "row", scatter_dimension=0, tiled=True),
    )
    gains = lax.psum((grad_query_gain, grad_key_gain, grad_attn_gain, grad_mlp_gain), "row")
    return (
        layer_out,
        grad_inputs,
        summed[0],
        summed[1],
        summed[2],
        summed[3],
        summed[4],
        summed[5],
        summed[6],
        gains[0],
        gains[1],
        gains[2],
        gains[3],
    )


BF = jnp.bfloat16
F32 = jnp.float32
MESH_ID = pl.DeviceIdType.MESH
T = 512
DC = 256
DR = 512
D = 2048
FH = 512
HT = 256
LAYER_STAGES = 5
EXACT = lax.Precision.HIGHEST


def dot_nn(a, b):
    return jnp.dot(a, b, preferred_element_type=F32)


def dot_nt(a, b, precision=None):
    return lax.dot_general(
        a, b, (((1,), (1,)), ((), ())), precision=precision, preferred_element_type=F32
    )


def dot_tn(a, b, precision=None):
    return lax.dot_general(
        a, b, (((0,), (0,)), ((), ())), precision=precision, preferred_element_type=F32
    )


def aligned(start, size):
    return pl.ds(pl.multiple_of(start, size), size)


class Counter:
    def __init__(self):
        self.used = 0

    def take(self, count=1):
        first = self.used
        self.used += count
        return first


def block_kernel(
    x_hbm,
    wq_hbm,
    wk_hbm,
    wv_hbm,
    wo_hbm,
    wg_hbm,
    wu_hbm,
    wd_hbm,
    cot_hbm,
    query_gain_ref,
    key_gain_ref,
    attn_gain_ref,
    mlp_gain_ref,
    pos_ref,
    layer_out,
    grad_in,
    gains_out,
    land_mlp,
    land_attn,
    wqkv,
    wo,
    wgu,
    wd,
    x_full,
    mid_full,
    gf_full,
    gb_full,
    gu_s,
    mixed_s,
    probs_s,
    hat_s,
    low_s,
    cos_s,
    sin_s,
    pos_s,
    cot_z,
    braw_s,
    raw_s,
    middle_s,
    bhat_s,
    work_s,
    inner_s,
    att_s,
    ga_s,
    gqkv_s,
    gs_s,
    gqk_s,
    own_s,
    stage_c,
    land_c,
    stage_y,
    land_y,
    stage_z,
    land_z,
    land_r,
    scal_s,
    gain_s,
    stage_down,
    stage_gu,
    rel_mlp,
    rel_attn,
    out_lo,
    send_sem,
    recv_sem,
    local_sem,
):
    row = lax.axis_index("row")
    col = lax.axis_index("col")
    x_at = lax.rem(row, 2)
    y_at = lax.div(row, 2)
    core = lax.rem(col, 2)
    z_at = lax.div(col, 2)
    row_x = row + 1 - 2 * x_at
    row_y = lax.rem(row + 2, 4)
    row_d = row_y + 1 - 2 * x_at
    sib = col + 1 - 2 * core
    dev_x = (row_x, col)
    dev_y = (row_y, col)
    dev_d = (row_d, col)
    dev_c = (row, sib)
    z_pair = {
        0: z_at,
        1: z_at + 1 - 2 * lax.rem(z_at, 2),
        2: lax.rem(z_at + 2, 4),
        3: 3 - z_at,
    }
    middle = (z_at == 1) | (z_at == 2)
    at_end = (z_at == 0) | (z_at == 3)
    dev_z = {pair: (row, 2 * z_pair[pair] + core) for pair in (1, 2, 3)}

    counter = Counter()
    locals_used = Counter()
    pending = []

    def copy_of(index, src, dst, device, send_index=None):
        return pltpu.make_async_remote_copy(
            src_ref=src,
            dst_ref=dst,
            send_sem=send_sem.at[index if send_index is None else send_index],
            recv_sem=recv_sem.at[index],
            device_id=device,
            device_id_type=MESH_ID,
        )

    def send(index, src, dst, device, send_index=None, when=None):
        copy = copy_of(index, src, dst, device, send_index)
        if when is None:
            copy.start()
        else:
            pl.when(when)(copy.start)
        pending.append((copy, when))
        return copy, when

    def arrived(index, dst, when=None):
        copy = copy_of(index, dst, dst, dev_c)
        if when is None:
            copy.wait_recv()
        else:
            pl.when(when)(copy.wait_recv)

    def sent(started):
        copy, when = started
        if when is None:
            copy.wait_send()
        else:
            pl.when(when)(copy.wait_send)
        pending[:] = [other for other in pending if other[0] is not copy]

    def local(src, dst):
        copy = pltpu.make_async_copy(src, dst, local_sem.at[locals_used.take()])
        copy.start()
        return copy

    barrier = pltpu.get_barrier_semaphore()
    partners = [dev_x, dev_y, dev_d] + [(row, lax.rem(col + step, 8)) for step in range(1, 8)]
    for device in partners:
        pl.semaphore_signal(barrier, inc=1, device_id=device, device_id_type=MESH_ID)

    @pl.when(at_end)
    def _():
        land_r[...] = jnp.zeros_like(land_r)
        land_z[0] = jnp.zeros_like(land_z[0])

    half_mine = aligned(y_at * FH, FH)
    half_other = aligned((1 - y_at) * FH, FH)
    rows_mine = aligned(row * DR, DR)
    local_copies = [local(x_hbm, x_full.at[:, aligned(col * DC, DC)]), local(cot_hbm, cot_z.at[z_at])]
    for index, ref in enumerate((wq_hbm, wk_hbm, wv_hbm)):
        local_copies.append(local(ref, wqkv.at[rows_mine, pl.ds(index * DC, DC)]))
    local_copies.append(local(wo_hbm, wo.at[rows_mine, :]))
    local_copies.append(local(wg_hbm.at[:, half_mine], wgu.at[rows_mine, pl.ds(0, FH)]))
    local_copies.append(local(wu_hbm.at[:, half_mine], wgu.at[rows_mine, pl.ds(FH, FH)]))
    local_copies.append(local(wd_hbm.at[:, half_mine], wd.at[rows_mine, :]))
    pl.semaphore_wait(barrier, len(partners))

    def own_rows(half, plane):
        if plane:
            return aligned(half * 2 * HT + y_at * HT, HT)
        return pl.ds(half * HT, HT)

    def other_rows(half):
        return aligned(half * 2 * HT + (1 - y_at) * HT, HT)

    def half_rows(half, plane):
        count = 2 * HT if plane else HT
        return pl.ds(half * count, count)

    def tokens(half):
        return pl.ds(half * HT, HT)

    class Gather:
        def __init__(self, buf, plane, raw, process, half):
            self.buf = buf
            self.plane = plane
            self.raw = raw
            self.process = process
            self.half = half
            self.base_z = counter.take(3)
            self.relay = counter.take()
            self.base_c = counter.take(4)
            self.rows = own_rows(half, plane)
            if plane:
                self.base_y = counter.take(4)
                self.base_cy = counter.take(4)
                self.rows_other = other_rows(half)

        def block(self, rows, place, parity=None):
            at = 2 * place + (core if parity is None else parity)
            return rows, aligned(at * DC, DC)

        def start(self):
            self.raw_sends = []
            own = self.raw.at[z_at, tokens(self.half)]
            for pair in (2, 3, 1):
                when = middle if pair == 3 else None
                self.raw_sends.append(
                    send(self.base_z + pair - 1, own, own, dev_z[pair], when=when)
                )

        def finish_own(self):
            for pair in (0, 2, 1, 3):
                place = z_pair[pair]
                if pair:
                    raw = self.raw.at[place, tokens(self.half)]
                    arrived(self.base_z + pair - 1, raw)
                if pair == 2:
                    self.raw_sends.append(
                        send(self.base_z + 2, raw, raw, dev_z[1], self.relay, middle)
                    )
                where = self.block(self.rows, place)
                self.buf[where] = self.process(pair, place, self.half)
                block = self.buf.at[where]
                if self.plane:
                    send(self.base_y + pair, block, block, dev_y)
                send(self.base_c + pair, block, block, dev_c)
            for pair in range(4):
                arrived(
                    self.base_c + pair, self.buf.at[self.block(self.rows, z_pair[pair], 1 - core)]
                )

        def finish_raw(self):
            for copy in self.raw_sends:
                sent(copy)

        def finish_other(self):
            for pair in range(4):
                block = self.buf.at[self.block(self.rows_other, z_pair[pair])]
                arrived(self.base_y + pair, block)
                send(self.base_cy + pair, block, block, dev_c)
            for pair in range(4):
                arrived(
                    self.base_cy + pair,
                    self.buf.at[self.block(self.rows_other, z_pair[pair], 1 - core)],
                )

    stage_sends = ([], [])

    class Reduce:
        ORDER = (3, 1, 2, 0)

        def __init__(self, partial, plane, half):
            self.partial = partial
            self.plane = plane
            self.half = half
            self.base_c = counter.take(4)
            self.base_z = counter.take(3)
            self.relay = counter.take()
            self.left = half_rows(half, plane)
            self.all_rows = pl.ds(half * 2 * HT, 2 * HT if plane else HT)
            self.rows = own_rows(half, True) if plane else self.all_rows
            self.tokens = tokens(half)
            if plane:
                self.base_y = counter.take(4)
                self.rows_other = other_rows(half)

        def start(self):
            for copy in stage_sends[self.half]:
                sent(copy)
            stage_sends[self.half].clear()
            rows = self.all_rows
            for slot, pair in enumerate(self.ORDER):
                target = z_pair[pair]
                start = pl.multiple_of((2 * target + 1 - core) * DC, DC)
                stage_c[slot, rows, :] = self.partial(self.left, start).astype(BF)
                self.send(
                    self.base_c + slot, stage_c.at[slot, rows, :], land_c.at[slot, rows, :], dev_c
                )
                start = pl.multiple_of((2 * target + core) * DC, DC)
                own_s[slot, rows, :] = self.partial(self.left, start)
                if slot:
                    self.cores(slot - 1)
            self.cores(3)

        def send(self, *copy):
            stage_sends[self.half].append(send(*copy))

        def cores(self, slot):
            arrived(self.base_c + slot, land_c.at[slot, self.all_rows, :])
            if self.plane:
                rows = self.rows_other
                stage_y[slot, self.tokens, :] = (
                    own_s[slot, rows, :] + land_c[slot, rows, :].astype(F32)
                ).astype(BF)
                self.send(
                    self.base_y + slot,
                    stage_y.at[slot, self.tokens],
                    land_y.at[slot, self.tokens],
                    dev_y,
                )
                rows = self.rows
                own_s[slot, rows, :] = own_s[slot, rows, :] + land_c[slot, rows, :].astype(F32)
            else:
                self.pass_on(slot, land_c.at[slot, self.rows, :])

        def pass_on(self, slot, landed):
            pair = self.ORDER[slot]
            total = own_s[slot, self.rows, :] + landed[...].astype(F32)
            if pair == 0:
                own_s[slot, self.rows, :] = total
                return
            if pair == 2:
                arrived(self.relay, land_r.at[self.tokens], middle)
                total = total + land_r[self.tokens, :].astype(F32)
            stage_z[slot, self.tokens, :] = total.astype(BF)
            stage, land = stage_z.at[slot, self.tokens], land_z.at[slot, self.tokens]
            if pair == 3:
                index = self.base_z + slot
                self.send(index, stage, land, dev_z[3], None, middle)
                self.send(self.relay, stage, land_r.at[self.tokens], dev_z[1], None, at_end)
            else:
                self.send(self.base_z + slot, stage, land, dev_z[pair])

        def planes(self):
            for slot in range(4):
                landed = land_y.at[slot, self.tokens]
                arrived(self.base_y + slot, landed)
                self.pass_on(slot, landed)

        def finish(self):
            for slot in range(3):
                when = middle if self.ORDER[slot] == 3 else None
                arrived(self.base_z + slot, land_z.at[slot, self.tokens], when)
            total = own_s[3, self.rows, :]
            for slot in range(3):
                total = total + land_z[slot, self.tokens, :].astype(F32)
            return total

    pick = lax.broadcasted_iota(jnp.int32, (8, DC), 0)
    lane = lax.broadcasted_iota(jnp.int32, (8, DC), 1)
    first_row = (pick == 0).astype(F32)
    second_row = (pick == 1).astype(F32)
    spread = ((pick == 0) & (lane < 128)).astype(F32) + ((pick == 1) & (lane >= 128)).astype(F32)
    scal_base = counter.take(7 * 2 * LAYER_STAGES)

    def scal_send(stage, half, first, second=None):
        mine = dot_nt(first_row, first, EXACT)
        if second is not None:
            mine = mine + dot_nt(second_row, second, EXACT)
        place = scal_s.at[stage, half, col]
        place[...] = mine
        for step in range(1, 8):
            index = scal_base + 7 * (2 * stage + half) + step - 1
            send(index, place, place, (row, lax.rem(col + step, 8)))

    def scal_get(stage, half):
        for step in range(1, 8):
            index = scal_base + 7 * (2 * stage + half) + step - 1
            arrived(index, scal_s.at[stage, half, lax.rem(col + 8 - step, 8)])
        total = scal_s[stage, half, 0]
        for index in range(1, 8):
            total = total + scal_s[stage, half, index]
        both = dot_tn(total, spread, EXACT)
        return both[:, :128], both[:, 128:]

    HALVES = (0, 1)

    def wide(values):
        return jnp.concatenate([values, values], axis=1)

    attn_base = counter.take(16)
    attn_hbm = (wq_hbm, wk_hbm, wv_hbm, wo_hbm)

    def attn_place(index, owner, part=None):
        if part is None:
            rows = aligned(owner * DR, DR)
        else:
            rows = aligned(owner * DR + part * (DR // 2), DR // 2)
        if index < 3:
            return wqkv.at[rows, pl.ds(index * DC, DC)]
        return wo.at[rows, :]

    def attn_send(index):
        send(attn_base + index, attn_hbm[index], attn_place(index, row), dev_x)
        send(attn_base + 4 + index, attn_hbm[index], attn_place(index, row), dev_y)

    def attn_relay(index):
        arrived(attn_base + index, attn_place(index, row_x))
        part = attn_place(index, row_x, 0)
        send(attn_base + 8 + index, part, part, dev_y)
        arrived(attn_base + 4 + index, attn_place(index, row_y))
        part = attn_place(index, row_y, 1)
        send(attn_base + 12 + index, part, part, dev_x)

    def attn_ready(index):
        arrived(attn_base + 8 + index, attn_place(index, row_d, 0))
        arrived(attn_base + 12 + index, attn_place(index, row_d, 1))

    mlp_base = counter.take(9)
    mlp_hbm = (wg_hbm, wu_hbm, wd_hbm)

    def mlp_place(index, owner):
        rows = aligned(owner * DR, DR)
        if index < 2:
            return wgu.at[rows, pl.ds(index * FH, FH)]
        return wd.at[rows, :]

    def mlp_send(index):
        send(mlp_base + index, mlp_hbm[index].at[:, half_mine], mlp_place(index, row), dev_x)
        send(mlp_base + 3 + index, mlp_hbm[index].at[:, half_other], mlp_place(index, row), dev_y)

    def mlp_relay(index):
        place = mlp_place(index, row_y)
        arrived(mlp_base + 3 + index, place)
        send(mlp_base + 6 + index, place, place, dev_x)

    def mlp_ready(index):
        arrived(mlp_base + index, mlp_place(index, row_x))
        arrived(mlp_base + 6 + index, mlp_place(index, row_d))

    for index in range(3):
        attn_send(index)

    x_base = counter.take(7)
    cot_base = counter.take(3)

    def x_block(place, parity):
        return x_full.at[:, aligned((2 * place + parity) * DC, DC)]

    for pair in (2, 3, 1):
        send(x_base + pair - 1, x_hbm, x_block(z_at, core), dev_z[pair])
    send(x_base + 3, x_hbm, x_block(z_at, core), dev_c)

    position_rows = jnp.broadcast_to(pos_ref[...].astype(F32), (8, T))
    position = dot_tn(position_rows, first_row[:, :HD], EXACT)
    pos_s[...] = position.astype(jnp.int32)
    lane_at = lax.broadcasted_iota(jnp.int32, (1, HD), 1)
    within = lax.rem(lane_at, HD // 2).astype(F32)
    frequency = jnp.exp(within * (-2.0 * math.log(THETA) / HD))
    angles = position * frequency
    cos_s[...] = jnp.cos(angles)
    sine = jnp.sin(angles)
    sin_s[...] = jnp.where(lane_at < HD // 2, -sine, sine)

    for index in range(3):
        attn_relay(index)
    attn_send(3)
    for pair in (1, 2, 3):
        block = x_block(z_pair[pair], core)
        arrived(x_base + pair - 1, block)
        send(x_base + 3 + pair, block, block, dev_c)
    for copy in local_copies:
        copy.wait()
    for pair in range(4):
        arrived(x_base + 3 + pair, x_block(z_pair[pair], 1 - core))
    attn_ready(0)
    attn_ready(1)

    def gain_at(ref, at):
        return ref[:, aligned(at * DC, DC)]

    qk_gain = (gain_at(query_gain_ref, col), gain_at(key_gain_ref, col))
    for index in range(2):
        hat_s[index] = dot_nn(x_full[...], wqkv[:, pl.ds(index * DC, DC)])
    for half in HALVES:
        query, key = hat_s[0, tokens(half), :], hat_s[1, tokens(half), :]
        scal_send(0, half, query * query, key * key)
    attn_relay(3)
    for index in range(3):
        mlp_send(index)
    attn_ready(2)
    low_s[2] = dot_nn(x_full[...], wqkv[:, pl.ds(2 * DC, DC)]).astype(BF)
    for half in HALVES:
        scales = [lax.rsqrt(total / D + EPS) for total in scal_get(0, half)]
        rows = tokens(half)
        work_s[0, rows, :] = jnp.concatenate(scales, axis=1)
        for index in range(2):
            hat = hat_s[index, rows, :] * wide(scales[index])
            hat_s[index, rows, :] = hat
            normed = hat * qk_gain[index]
            for head in range(2):
                part = normed[:, head * HD : (head + 1) * HD]
                turned = part * cos_s[rows, :] + pltpu.roll(part, HD // 2, 1) * sin_s[rows, :]
                if index == 0:
                    turned = turned * (HD**-0.5)
                low_s[index, rows, pl.ds(head * HD, HD)] = turned.astype(BF)

    chunk = 128

    def attend(half):
        count = (half + 1) * HT
        keys = pl.ds(0, count)

        def attend_chunk(at, carry):
            rows = aligned(at * chunk, chunk)
            query = at * chunk + lax.broadcasted_iota(jnp.int32, (chunk, count), 0)
            key = lax.broadcasted_iota(jnp.int32, (chunk, count), 1)
            oldest = query - pos_s[rows, :1]
            allowed = (key <= query) & (key >= oldest)
            for head in range(2):
                lanes = pl.ds(head * HD, HD)
                scores = dot_nt(low_s[0, rows, lanes], low_s[1, keys, lanes])
                scores = jnp.where(allowed, scores, MASKED)
                exponent = jnp.exp(scores - jnp.max(scores, axis=1, keepdims=True))
                probs = exponent / jnp.sum(exponent, axis=1, keepdims=True)
                probs_s[head, rows, keys] = probs
                att_s[rows, lanes] = dot_nn(probs.astype(BF), low_s[2, keys, lanes]).astype(BF)
            return carry

        first = half * (HT // chunk)
        lax.fori_loop(first, first + HT // chunk, attend_chunk, 0)

    branch_sums = [
        Reduce(
            lambda rows, start: dot_nt(att_s[rows, :], wo[pl.ds(start, DC), :]), False, half
        )
        for half in HALVES
    ]

    def middle_block(pair, place, half):
        rows = tokens(half)
        at = 2 * place + core
        raw = work_s[1, rows, :] if pair == 0 else braw_s[place, rows, :].astype(F32)
        hat = raw * wide(work_s[2, rows, :128])
        inputs = x_full[rows, aligned(at * DC, DC)].astype(F32)
        middle = inputs + hat * gain_at(attn_gain_ref, at)
        if pair == 0:
            bhat_s[rows, :] = hat
            middle_s[rows, :] = middle
        return middle.astype(BF)

    mid_gathers = [Gather(mid_full, True, braw_s, middle_block, half) for half in HALVES]

    def branch_done(half):
        rows = tokens(half)
        branch = branch_sums[half].finish()
        scal_send(1, half, branch * branch)
        work_s[1, rows, :] = branch
        braw_s[z_at, rows, :] = branch.astype(BF)
        mid_gathers[half].start()

    def branch_scaled(half):
        total, _ = scal_get(1, half)
        work_s[2, tokens(half), :128] = lax.rsqrt(total / D + EPS)

    attend(0)
    attn_ready(3)
    branch_sums[0].start()
    attend(1)
    branch_sums[1].start()
    mlp_relay(0)
    branch_done(0)
    mlp_relay(1)
    branch_scaled(0)
    branch_done(1)
    mid_gathers[0].finish_own()
    branch_scaled(1)
    mlp_relay(2)
    mid_gathers[1].finish_own()
    for pair in (2, 3, 1):
        send(cot_base + pair - 1, cot_z.at[z_at], cot_z.at[z_at], dev_z[pair])
    mid_gathers[0].finish_other()
    mlp_ready(0)
    mlp_ready(1)

    tile = 256

    def forward_tiles(half):
        rows = half_rows(half, True)

        def forward_tile(at, carry):
            lanes = aligned(at * tile, tile)
            lanes_up = aligned(at * tile + FH, tile)
            gate = dot_nn(mid_full[rows, :], wgu[:, lanes])
            up = dot_nn(mid_full[rows, :], wgu[:, lanes_up])
            gu_s[rows, lanes] = gate.astype(BF)
            gu_s[rows, lanes_up] = up.astype(BF)
            mixed_s[rows, lanes] = (gate * jax.nn.sigmoid(gate) * up).astype(BF)
            return carry

        lax.fori_loop(0, FH // tile, forward_tile, 0)

    ffn_sums = [
        Reduce(
            lambda rows, start: dot_nt(mixed_s[rows, :], wd[pl.ds(start, DC), :]), True, half
        )
        for half in HALVES
    ]
    mlp_gain = gain_at(mlp_gain_ref, col)

    def grad_ffn_block(pair, place, half):
        rows = tokens(half)
        at = 2 * place + core
        raw = work_s[1, rows, :] if pair == 0 else raw_s[place, rows, :].astype(F32)
        scale = wide(work_s[2, rows, 128:])
        grad = cot_z[place, rows, :].astype(F32) * gain_at(mlp_gain_ref, at)
        return (scale * (grad - raw * scale * wide(inner_s[rows, :]))).astype(BF)

    gf_gathers = [Gather(gf_full, True, raw_s, grad_ffn_block, half) for half in HALVES]

    def ffn_done(half):
        rows = tokens(half)
        ffn = ffn_sums[half].finish()
        cot = cot_z[z_at, rows, :].astype(F32)
        scal_send(2, half, ffn * ffn, cot * mlp_gain * ffn)
        work_s[1, rows, :] = ffn
        raw_s[z_at, rows, :] = ffn.astype(BF)
        gf_gathers[half].start()

    def ffn_scaled(half):
        rows = tokens(half)
        total, inner = scal_get(2, half)
        scale = lax.rsqrt(total / D + EPS)
        work_s[2, rows, 128:] = scale
        inner_s[rows, :] = inner * scale / D
        ffn_hat = work_s[1, rows, :] * wide(scale)
        out_lo[rows, :] = (middle_s[rows, :] + ffn_hat * mlp_gain).astype(BF)
        cot = cot_z[z_at, rows, :].astype(F32)
        return jnp.sum(cot * ffn_hat, axis=0, keepdims=True)

    forward_tiles(0)
    mlp_ready(2)
    ffn_sums[0].start()
    mid_gathers[1].finish_other()
    forward_tiles(1)
    ffn_sums[1].start()
    ffn_sums[0].planes()
    ffn_sums[1].planes()
    ffn_done(0)
    for pair in (1, 2, 3):
        arrived(cot_base + pair - 1, cot_z.at[z_pair[pair]])
    mlp_gain_part = ffn_scaled(0)
    ffn_done(1)
    gf_gathers[0].finish_own()
    gain_s[row, 3:4, :] = mlp_gain_part + ffn_scaled(1)
    lo_copy = local(out_lo, layer_out)
    gf_gathers[1].finish_own()
    gf_gathers[0].finish_other()

    def backward_tiles(half):
        rows = half_rows(half, True)

        def backward_tile(at, carry):
            lanes = aligned(at * tile, tile)
            lanes_up = aligned(at * tile + FH, tile)
            grad_mixed = dot_nn(gf_full[rows, :], wd[:, lanes])
            gate = gu_s[rows, lanes].astype(F32)
            up = gu_s[rows, lanes_up].astype(F32)
            sigma = jax.nn.sigmoid(gate)
            gu_s[rows, lanes] = (grad_mixed * up * sigma * (1.0 + gate * (1.0 - sigma))).astype(BF)
            gu_s[rows, lanes_up] = (grad_mixed * gate * sigma).astype(BF)
            return carry

        lax.fori_loop(0, FH // tile, backward_tile, 0)

    def lanes_of(owner):
        return aligned(owner * DR, DR)

    GU = pl.ds(0, 2 * FH)
    DOWN = pl.ds(2 * FH, FH)

    def down_piece(owner):
        return dot_tn(gf_full[:, lanes_of(owner)], mixed_s[...])

    def gu_piece(owner, part):
        return dot_tn(mid_full[:, lanes_of(owner)], gu_s[:, pl.ds(part * FH, FH)])

    def gu_stage(slot, owner):
        for part in range(2):
            stage_gu[slot, :, pl.ds(part * FH, FH)] = gu_piece(owner, part).astype(BF)

    mid_sums = [
        Reduce(lambda rows, start: dot_nt(gu_s[rows, :], wgu[pl.ds(start, DC), :]), True, half)
        for half in HALVES
    ]
    attn_gain = gain_at(attn_gain_ref, col)

    def grad_branch_block(pair, place, half):
        rows = tokens(half)
        at = 2 * place + core
        scale = wide(work_s[2, rows, :128])
        raw = middle_s[rows, :] if pair == 0 else raw_s[place, rows, :].astype(F32)
        hat = bhat_s[rows, :] if pair == 0 else braw_s[place, rows, :].astype(F32) * scale
        inner = wide(inner_s[rows, :])
        return (scale * (raw * gain_at(attn_gain_ref, at) - hat * inner)).astype(BF)

    gb_gathers = [Gather(gb_full, False, raw_s, grad_branch_block, half) for half in HALVES]

    def mid_done(half):
        rows = tokens(half)
        grad_middle = cot_z[z_at, rows, :].astype(F32) + mid_sums[half].finish()
        scal_send(3, half, grad_middle * attn_gain * bhat_s[rows, :])
        middle_s[rows, :] = grad_middle
        raw_s[z_at, rows, :] = grad_middle.astype(BF)
        gb_gathers[half].start()

    def mid_scaled(half):
        inner, _ = scal_get(3, half)
        inner_s[tokens(half), :] = inner / D

    grad_base = counter.take(6)
    backward_tiles(0)
    gf_gathers[0].finish_raw()
    mid_sums[0].start()
    gf_gathers[1].finish_other()
    stage_down[0] = down_piece(row_d).astype(BF)
    down_sends = [send(grad_base, stage_down.at[0], rel_mlp.at[:, DOWN], dev_x)]
    backward_tiles(1)
    gf_gathers[1].finish_raw()
    mid_sums[1].start()
    gu_stage(0, row_d)
    gu_sends = [send(grad_base + 1, stage_gu.at[0], rel_mlp.at[:, GU], dev_x)]
    mid_sums[0].planes()
    mid_sums[1].planes()
    stage_down[1] = down_piece(row_x).astype(BF)
    down_sends.append(send(grad_base + 2, stage_down.at[1], land_mlp.at[1, :, DOWN], dev_x))
    mid_done(0)
    arrived(grad_base, rel_mlp.at[:, DOWN])
    stage_down[2] = (down_piece(row_y) + rel_mlp[:, DOWN].astype(F32)).astype(BF)
    down_sends.append(send(grad_base + 4, stage_down.at[2], land_mlp.at[2, :, DOWN], dev_y))
    gu_stage(1, row_x)
    gu_sends.append(send(grad_base + 3, stage_gu.at[1], land_mlp.at[1, :, GU], dev_x))
    mid_scaled(0)
    mid_done(1)
    gb_gathers[0].finish_own()
    gain_s[row, 2:3, :] = jnp.sum(middle_s[...] * bhat_s[...], axis=0, keepdims=True)
    mid_scaled(1)
    arrived(grad_base + 1, rel_mlp.at[:, GU])
    for part in range(2):
        half_lanes = pl.ds(part * FH, FH)
        stage_gu[2, :, half_lanes] = (
            gu_piece(row_y, part) + rel_mlp[:, half_lanes].astype(F32)
        ).astype(BF)
    gu_sends.append(send(grad_base + 5, stage_gu.at[2], land_mlp.at[2, :, GU], dev_y))
    gb_gathers[1].finish_own()

    ga_s[...] = dot_nn(gb_full[...], wo[...]).astype(BF)

    upper = pl.ds(0, DR // 2)
    lower = pl.ds(DR // 2, DR // 2)
    attn_grad_base = counter.take(3 * 6)
    late = []

    class AttnGrad:
        def __init__(self, order, left, right, stage, stage_lanes, lanes):
            self.base = attn_grad_base + 6 * order
            self.left, self.right = left, right
            self.stage, self.stage_lanes, self.lanes = stage, stage_lanes, lanes

        def at(self, slot, rows):
            return self.stage.at[slot, rows, self.stage_lanes]

        def start(self):
            for slot, owner in enumerate((row_d, row_x, row_y, row)):
                self.stage[slot, :, self.stage_lanes] = dot_tn(
                    self.left[:, lanes_of(owner)], self.right()
                ).astype(BF)
                if slot == 0:
                    send(self.base, self.at(0, upper), rel_attn.at[upper, self.lanes], dev_x)
                    send(self.base + 1, self.at(0, lower), rel_attn.at[lower, self.lanes], dev_y)
                elif slot == 1:
                    landing = land_attn.at[1, upper, self.lanes]
                    send(self.base + 2, self.at(1, upper), landing, dev_x)
                elif slot == 2:
                    landing = land_attn.at[2, lower, self.lanes]
                    send(self.base + 3, self.at(2, lower), landing, dev_y)
                else:
                    whole = self.at(3, pl.ds(0, DR))
                    late.append(local(whole, land_attn.at[0, :, self.lanes]))

        def relay(self):
            for step, (slot, rows, device) in enumerate(((2, upper, dev_y), (1, lower, dev_x))):
                arrived(self.base + step, rel_attn.at[rows, self.lanes])
                self.stage[slot, rows, self.stage_lanes] = (
                    self.stage[slot, rows, self.stage_lanes].astype(F32)
                    + rel_attn[rows, self.lanes].astype(F32)
                ).astype(BF)
                send(
                    self.base + 4 + step,
                    self.at(slot, rows),
                    land_attn.at[slot, rows, self.lanes],
                    device,
                )

        def finish(self):
            arrived(self.base + 2, land_attn.at[1, upper, self.lanes])
            arrived(self.base + 3, land_attn.at[2, lower, self.lanes])
            arrived(self.base + 4, land_attn.at[2, upper, self.lanes])
            arrived(self.base + 5, land_attn.at[1, lower, self.lanes])

    stage_down[3] = down_piece(row).astype(BF)
    own_copies = [local(stage_down.at[3], land_mlp.at[0, :, DOWN])]
    for copy in down_sends:
        sent(copy)
    own_copies[0].wait()
    first_lanes = pl.ds(0, DC)
    o_grad = AttnGrad(
        0, gb_full, lambda: att_s[...], stage_down, first_lanes, pl.ds(3 * DC, DC)
    )
    o_grad.start()

    def attend_back(half):
        count = (half + 1) * HT
        keys = pl.ds(0, count)

        def attend_back_chunk(at, carry):
            rows = aligned(at * chunk, chunk)
            for head in range(2):
                lanes = pl.ds(head * HD, HD)
                grad_probs = dot_nt(ga_s[rows, lanes], low_s[2, keys, lanes])
                probs = probs_s[head, rows, keys]
                inner = jnp.sum(probs * grad_probs, axis=1, keepdims=True)
                grad_scores = (probs * (grad_probs - inner)).astype(BF)
                gs_s[head, rows, keys] = grad_scores
                gqk_s[0, rows, lanes] = dot_nn(grad_scores, low_s[1, keys, lanes])
            return carry

        first = half * (HT // chunk)
        lax.fori_loop(first, first + HT // chunk, attend_back_chunk, 0)

    for half in HALVES:
        attend_back(half)
    early, last = pl.ds(0, HT), pl.ds(HT, HT)
    for head in range(2):
        lanes = pl.ds(head * HD, HD)
        gqk_s[1, early, lanes] = dot_tn(gs_s[head, :, early], low_s[0, :, lanes])
        gqk_s[1, last, lanes] = dot_tn(gs_s[head, last, last], low_s[0, last, lanes])
    inners = []
    for index in range(2):
        for head in range(2):
            lanes = pl.ds(head * HD, HD)
            part = gqk_s[index, :, lanes]
            turned = part * cos_s[...] - pltpu.roll(part, HD // 2, 1) * sin_s[...]
            if index == 0:
                turned = turned * (HD**-0.5)
            gqk_s[index, :, lanes] = turned
        weighted = gqk_s[index] * hat_s[index]
        gain_s[row, index : index + 1, :] = jnp.sum(weighted, axis=0, keepdims=True)
        inners.append(weighted * qk_gain[index])
    for half in HALVES:
        part = slice(half * HT, (half + 1) * HT)
        scal_send(4, half, inners[0][part], inners[1][part])
    gain_base = counter.take(3)
    for slot, device in enumerate((dev_x, dev_y, dev_d)):
        send(gain_base + slot, gain_s.at[row], gain_s.at[row], device)
    for head in range(2):
        lanes = pl.ds(head * HD, HD)
        out_lanes = pl.ds(2 * DC + head * HD, HD)
        gqkv_s[early, out_lanes] = dot_tn(
            probs_s[head, :, early].astype(BF), ga_s[:, lanes]
        ).astype(BF)
        gqkv_s[last, out_lanes] = dot_tn(
            probs_s[head, last, last].astype(BF), ga_s[last, lanes]
        ).astype(BF)
    v_grad = AttnGrad(
        1,
        x_full,
        lambda: gqkv_s[:, 2 * DC :],
        stage_down,
        pl.ds(DC, DC),
        pl.ds(2 * DC, DC),
    )
    v_grad.start()
    for half in HALVES:
        rows = tokens(half)
        totals = scal_get(4, half)
        for index in range(2):
            scale = wide(work_s[0, rows, index * 128 : (index + 1) * 128])
            gqkv_s[rows, pl.ds(index * DC, DC)] = (
                scale
                * (
                    gqk_s[index, rows, :] * qk_gain[index]
                    - hat_s[index, rows, :] * wide(totals[index] / D)
                )
            ).astype(BF)
    in_sums = [
        Reduce(
            lambda rows, start: dot_nt(gqkv_s[rows, :], wqkv[pl.ds(start, DC), :]), False, half
        )
        for half in HALVES
    ]
    for half in HALVES:
        in_sums[half].start()
    o_grad.relay()
    gu_stage(3, row)
    own_copies.append(local(stage_gu.at[3], land_mlp.at[0, :, GU]))
    for copy in gu_sends:
        sent(copy)
    own_copies[1].wait()
    both_lanes = pl.ds(0, 2 * DC)
    qk_grad = AttnGrad(
        2, x_full, lambda: gqkv_s[:, : 2 * DC], stage_gu, both_lanes, both_lanes
    )
    qk_grad.start()
    v_grad.relay()
    for half in HALVES:
        rows = tokens(half)
        work_s[1, rows, :] = middle_s[rows, :] + in_sums[half].finish()
    late.append(local(work_s.at[1], grad_in))
    late.append(lo_copy)
    qk_grad.relay()

    for slot, owner in enumerate((row_x, row_y, row_d)):
        arrived(gain_base + slot, gain_s.at[owner])
    gains_out[...] = gain_s[0] + gain_s[1] + gain_s[2] + gain_s[3]
    for index, (slot, lanes) in enumerate(((1, DOWN), (1, GU), (2, DOWN), (2, GU))):
        arrived(grad_base + 2 + index, land_mlp.at[slot, :, lanes])
    for grad in (o_grad, v_grad, qk_grad):
        grad.finish()
    for copy in late:
        copy.wait()
    for copy in list(pending):
        sent(copy)


def total_kernel(
    lo_ref, gin_ref, gains_ref, mlp_ref, attn_ref, lo_out, gin_out, *outs
):
    y_at = lax.div(lax.axis_index("row"), 2)
    lo_out[...] = lo_ref[...]
    gin_out[...] = gin_ref[...]
    attn = attn_ref[0].astype(F32) + attn_ref[1].astype(F32) + attn_ref[2].astype(F32)
    for index in range(4):
        outs[index][...] = attn[:, index * DC : (index + 1) * DC]
    mine = mlp_ref[0].astype(F32) + mlp_ref[1].astype(F32)
    other = mlp_ref[2].astype(F32)
    for index in range(3):
        lanes = slice(index * FH, (index + 1) * FH)
        outs[4 + index][:, aligned(y_at * FH, FH)] = mine[:, lanes]
        outs[4 + index][:, aligned((1 - y_at) * FH, FH)] = other[:, lanes]
    for index in range(4):
        outs[7 + index][...] = gains_ref[index : index + 1, :]


MIB = 1 << 20


def on_device_kernel(
    inputs,
    query_weight,
    key_weight,
    value_weight,
    output_weight,
    gate_weight,
    up_weight,
    down_weight,
    query_gain,
    key_gain,
    attn_gain,
    mlp_gain,
    positions,
    segments,
    cotangent,
):
    hbm = pl.BlockSpec(memory_space=pl.ANY)
    vmem = pl.BlockSpec(memory_space=pltpu.VMEM)
    sds = jax.ShapeDtypeStruct
    copies = 320
    landed = pl.pallas_call(
        block_kernel,
        out_shape=[
            sds((T, DC), BF),
            sds((T, DC), F32),
            sds((8, DC), F32),
            sds((3, DR, 3 * FH), BF),
            sds((3, DR, 4 * DC), BF),
        ],
        in_specs=[hbm] * 9 + [vmem] * 5,
        out_specs=[hbm, hbm, vmem, hbm, hbm],
        scratch_shapes=[
            pltpu.VMEM((D, 3 * DC), BF),
            pltpu.VMEM((D, DC), BF),
            pltpu.VMEM((D, 2 * FH), BF),
            pltpu.VMEM((D, FH), BF),
            pltpu.VMEM((T, D), BF),
            pltpu.VMEM((2 * T, D), BF),
            pltpu.VMEM((2 * T, D), BF),
            pltpu.VMEM((T, D), BF),
            pltpu.VMEM((2 * T, 2 * FH), BF),
            pltpu.VMEM((2 * T, FH), BF),
            pltpu.VMEM((2, T, T), F32),
            pltpu.VMEM((2, T, DC), F32),
            pltpu.VMEM((3, T, DC), BF),
            pltpu.VMEM((T, HD), F32),
            pltpu.VMEM((T, HD), F32),
            pltpu.VMEM((T, HD), jnp.int32),
            pltpu.VMEM((4, T, DC), BF),
            pltpu.VMEM((4, T, DC), BF),
            pltpu.VMEM((4, T, DC), BF),
            pltpu.VMEM((T, DC), F32),
            pltpu.VMEM((T, DC), F32),
            pltpu.VMEM((3, T, DC), F32),
            pltpu.VMEM((T, HD), F32),
            pltpu.VMEM((T, DC), BF),
            pltpu.VMEM((T, DC), BF),
            pltpu.VMEM((T, 3 * DC), BF),
            pltpu.VMEM((2, T, T), BF),
            pltpu.VMEM((2, T, DC), F32),
            pltpu.VMEM((4, 2 * T, DC), F32),
            pltpu.VMEM((4, 2 * T, DC), BF),
            pltpu.VMEM((4, 2 * T, DC), BF),
            pltpu.VMEM((4, T, DC), BF),
            pltpu.VMEM((4, T, DC), BF),
            pltpu.VMEM((3, T, DC), BF),
            pltpu.VMEM((3, T, DC), BF),
            pltpu.VMEM((T, DC), BF),
            pltpu.VMEM((LAYER_STAGES, 2, 8, 8, HT), F32),
            pltpu.VMEM((4, 8, DC), F32),
            pltpu.VMEM((4, DR, FH), BF),
            pltpu.VMEM((4, DR, 2 * FH), BF),
            pltpu.VMEM((DR, 3 * FH), BF),
            pltpu.VMEM((DR, 4 * DC), BF),
            pltpu.VMEM((T, DC), BF),
            pltpu.SemaphoreType.DMA((copies,)),
            pltpu.SemaphoreType.DMA((copies,)),
            pltpu.SemaphoreType.DMA((32,)),
        ],
        compiler_params=pltpu.CompilerParams(
            collective_id=0, has_side_effects=True, vmem_limit_bytes=64 * MIB
        ),
        cost_estimate=pl.CostEstimate(
            flops=26_800_000_000, bytes_accessed=16_000_000, transcendentals=2_000_000
        ),
    )(
        inputs,
        query_weight,
        key_weight,
        value_weight,
        output_weight,
        gate_weight,
        up_weight,
        down_weight,
        cotangent,
        query_gain[None, :],
        key_gain[None, :],
        attn_gain[None, :],
        mlp_gain[None, :],
        positions[None, :],
    )
    step = 64

    def rows_of(width):
        return pl.BlockSpec((step, width), lambda at: (at, 0))

    gain_spec = pl.BlockSpec((1, DC), lambda at: (0, 0))
    results = pl.pallas_call(
        total_kernel,
        grid=(DR // step,),
        out_shape=[sds((T, DC), BF), sds((T, DC), F32)]
        + [sds((DR, DC), F32)] * 4
        + [sds((DR, 2 * FH), F32)] * 3
        + [sds((1, DC), F32)] * 4,
        in_specs=[
            rows_of(DC),
            rows_of(DC),
            pl.BlockSpec((8, DC), lambda at: (0, 0)),
            pl.BlockSpec((3, step, 3 * FH), lambda at: (0, at, 0)),
            pl.BlockSpec((3, step, 4 * DC), lambda at: (0, at, 0)),
        ],
        out_specs=[rows_of(DC)] * 6 + [rows_of(2 * FH)] * 3 + [gain_spec] * 4,
    )(*landed)
    return (*results[:9], *[gain[0] for gain in results[9:]])


def solution(mesh):
    in_specs = (
        P("row", "col"),
        P("row", "col"),
        P("row", "col"),
        P("row", "col"),
        P("row", "col"),
        P("row", "col"),
        P("row", "col"),
        P("row", "col"),
        P(),
        P(),
        P(),
        P(),
        P("row"),
        P("row"),
        P("row", "col"),
    )
    out_specs = (
        P("row", "col"),
        P("row", "col"),
        P("row", "col"),
        P("row", "col"),
        P("row", "col"),
        P("row", "col"),
        P("row", "col"),
        P("row", "col"),
        P("row", "col"),
        P("col"),
        P("col"),
        P("col"),
        P("col"),
    )
    sizes = (mesh.shape["row"], mesh.shape["col"])
    body = on_device_kernel if sizes == (4, 8) else on_device
    return jax.shard_map(
        body, mesh=mesh, in_specs=in_specs, out_specs=out_specs, check_vma=False
    )
```

```python
import math

import jax
import jax.numpy as jnp
from jax import lax
from jax.experimental import pallas as pl
from jax.experimental.pallas import tpu as pltpu
from jax.sharding import PartitionSpec as P

HD = 128
LENGTH = 512


EPS = 1e-06
THETA = 500000.0
MASKED = -1e30


def rope_tables(positions, head_size):
    halfway = head_size // 2
    frequency = jnp.exp(
        jnp.arange(halfway, dtype=jnp.float32) * (-2.0 * math.log(THETA) / head_size)
    )
    angles = positions.astype(jnp.float32)[:, None] * frequency[None, :]
    return (jnp.cos(angles)[:, None, :], jnp.sin(angles)[:, None, :])


def rotate(values, cosine, sine):
    halfway = values.shape[-1] // 2
    first_half = values[..., :halfway]
    second_half = values[..., halfway:]
    return jnp.concatenate(
        [first_half * cosine - second_half * sine, second_half * cosine + first_half * sine],
        axis=-1,
    )


def matmul(left, right):
    return jnp.dot(left, right, preferred_element_type=jnp.float32)


def cross_rows(left, right):
    return lax.dot_general(
        left, right, (((0,), (0,)), ((), ())), preferred_element_type=jnp.float32
    )


def cross_cols(left, right):
    return lax.dot_general(
        left, right, (((1,), (1,)), ((), ())), preferred_element_type=jnp.float32
    )


def visible_pairs(segment_part):
    places = jnp.arange(segment_part.shape[0])
    return (segment_part[:, None] == segment_part[None, :]) & (places[:, None] >= places[None, :])


def on_device(
    inputs,
    query_weight,
    key_weight,
    value_weight,
    output_weight,
    gate_weight,
    up_weight,
    down_weight,
    query_gain,
    key_gain,
    attn_gain,
    mlp_gain,
    positions,
    segments,
    cotangent,
):
    bfloat = jnp.bfloat16
    floats = jnp.float32
    rows = inputs.shape[0]
    local_width = inputs.shape[1]
    width = local_width * lax.axis_size("col")
    offset = lax.axis_index("col") * local_width
    head_size = HD
    heads_here = local_width // head_size
    sequences = rows // LENGTH
    scale = head_size ** (-0.5)
    shape_seq = (sequences, LENGTH, heads_here, head_size)

    def mine(values):
        return lax.dynamic_slice_in_dim(values, offset, local_width, values.ndim - 1)

    query_gain_here = mine(query_gain)
    key_gain_here = mine(key_gain)
    cot_here = cotangent.astype(floats)
    gathered = (
        lax.all_gather(query_weight, "row", axis=0, tiled=True),
        lax.all_gather(key_weight, "row", axis=0, tiled=True),
        lax.all_gather(value_weight, "row", axis=0, tiled=True),
        lax.all_gather(gate_weight, "row", axis=0, tiled=True),
        lax.all_gather(up_weight, "row", axis=0, tiled=True),
        lax.all_gather(output_weight, "row", axis=0, tiled=True),
        lax.all_gather(down_weight, "row", axis=0, tiled=True),
    )
    query_full, key_full, value_full, gate_full, up_full, output_full, down_full = gathered
    whole_in = lax.all_gather(inputs, "col", axis=1, tiled=True)
    query_raw = matmul(whole_in, query_full)
    key_raw = matmul(whole_in, key_full)
    value_raw = matmul(whole_in, value_full)
    query_total, key_total = lax.psum(
        (jnp.sum(query_raw * query_raw, axis=1), jnp.sum(key_raw * key_raw, axis=1)), "col"
    )
    query_scale = lax.rsqrt(query_total / width + EPS)[:, None]
    key_scale = lax.rsqrt(key_total / width + EPS)[:, None]
    query_hat = query_raw * query_scale
    key_hat = key_raw * key_scale
    cosine, sine = rope_tables(positions, head_size)
    query_low = (
        rotate((query_hat * query_gain_here).reshape(rows, heads_here, head_size), cosine, sine)
        * scale
    ).astype(bfloat)
    key_low = rotate(
        (key_hat * key_gain_here).reshape(rows, heads_here, head_size), cosine, sine
    ).astype(bfloat)
    value_low = value_raw.astype(bfloat).reshape(rows, heads_here, head_size)
    query_blocks = query_low.reshape(shape_seq)
    key_blocks = key_low.reshape(shape_seq)
    value_blocks = value_low.reshape(shape_seq)
    segment_blocks = segments.reshape(sequences, LENGTH)

    def attend(block):
        queries, keys_part, values_part, segment_part = block
        scores = jnp.einsum("qhd,khd->hqk", queries, keys_part, preferred_element_type=floats)
        scores = jnp.where(visible_pairs(segment_part)[None], scores, MASKED)
        largest = jnp.max(scores, axis=-1, keepdims=True)
        exponent = jnp.exp(scores - largest)
        totals = jnp.sum(exponent, axis=-1, keepdims=True)
        weights_low = (exponent / totals).astype(bfloat)
        attended_part = jnp.einsum(
            "hqk,khd->qhd", weights_low, values_part, preferred_element_type=floats
        )
        return (attended_part, (largest + jnp.log(totals))[..., 0])

    attended, log_totals = lax.map(attend, (query_blocks, key_blocks, value_blocks, segment_blocks))
    attended_low = attended.reshape(rows, local_width).astype(bfloat)
    branch = lax.psum(cross_cols(attended_low, output_full), "col")
    branch_scale = lax.rsqrt(jnp.mean(branch * branch, axis=1, keepdims=True) + EPS)
    branch_hat = branch * branch_scale
    middle = whole_in.astype(floats) + branch_hat * attn_gain
    middle_low = middle.astype(bfloat)
    middle_here = mine(middle)
    branch_hat_here = mine(branch_hat)
    gate_pre = matmul(middle_low, gate_full)
    up_pre = matmul(middle_low, up_full)
    sigma = jax.nn.sigmoid(gate_pre)
    silu_gate = gate_pre * sigma
    mixed_low = (silu_gate * up_pre).astype(bfloat)
    ffn = lax.psum(cross_cols(mixed_low, down_full), "col")
    ffn_scale = lax.rsqrt(jnp.mean(ffn * ffn, axis=1, keepdims=True) + EPS)
    ffn_hat = ffn * ffn_scale
    ffn_hat_here = mine(ffn_hat)
    grad_top = lax.all_gather(cotangent, "col", axis=1, tiled=True).astype(floats)
    normed_top = grad_top * mlp_gain
    inner_top = jnp.sum(normed_top * ffn_hat, axis=1, keepdims=True)
    grad_ffn_low = (ffn_scale * (normed_top - ffn_hat * inner_top / width)).astype(bfloat)
    layer_out = (middle_here + ffn_hat_here * mine(mlp_gain)).astype(bfloat)
    grad_mlp_gain = jnp.sum(cot_here * ffn_hat_here, axis=0)
    grad_down = cross_rows(grad_ffn_low, mixed_low)
    grad_mixed = matmul(grad_ffn_low, down_full)
    grad_gate_low = (grad_mixed * up_pre * sigma * (1.0 + gate_pre * (1.0 - sigma))).astype(bfloat)
    grad_up_low = (grad_mixed * silu_gate).astype(bfloat)
    grad_middle_part = cross_cols(grad_gate_low, gate_full) + cross_cols(grad_up_low, up_full)
    grad_gate = cross_rows(middle_low, grad_gate_low)
    grad_up = cross_rows(middle_low, grad_up_low)
    grad_middle = grad_top + lax.psum(grad_middle_part, "col")
    grad_middle_here = mine(grad_middle)
    grad_attn_gain = jnp.sum(grad_middle_here * branch_hat_here, axis=0)
    normed_mid = grad_middle * attn_gain
    inner_mid = jnp.sum(normed_mid * branch_hat, axis=1, keepdims=True)
    grad_branch_low = (branch_scale * (normed_mid - branch_hat * inner_mid / width)).astype(bfloat)
    grad_output = cross_rows(grad_branch_low, attended_low)
    grad_attended_low = matmul(grad_branch_low, output_full).astype(bfloat)

    def attend_back(block):
        queries, keys_part, values_part, segment_part, log_part, grad_part = block
        scores = jnp.einsum("qhd,khd->hqk", queries, keys_part, preferred_element_type=floats)
        scores = jnp.where(visible_pairs(segment_part)[None], scores, MASKED)
        probs = jnp.exp(scores - log_part[..., None])
        grad_values = jnp.einsum(
            "hqk,qhd->khd", probs.astype(bfloat), grad_part, preferred_element_type=floats
        )
        grad_probs = jnp.einsum(
            "qhd,khd->hqk", grad_part, values_part, preferred_element_type=floats
        )
        grad_scores = probs * (grad_probs - jnp.sum(probs * grad_probs, axis=-1, keepdims=True))
        scores_low = grad_scores.astype(bfloat)
        grad_queries = jnp.einsum(
            "hqk,khd->qhd", scores_low, keys_part, preferred_element_type=floats
        )
        grad_keys = jnp.einsum("hqk,qhd->khd", scores_low, queries, preferred_element_type=floats)
        return (grad_queries, grad_keys, grad_values.astype(bfloat))

    grad_queries, grad_keys, grad_values = lax.map(
        attend_back,
        (
            query_blocks,
            key_blocks,
            value_blocks,
            segment_blocks,
            log_totals,
            grad_attended_low.reshape(shape_seq),
        ),
    )
    grad_query_norm = rotate(
        grad_queries.reshape(rows, heads_here, head_size) * scale, cosine, -sine
    ).reshape(rows, local_width)
    grad_key_norm = rotate(grad_keys.reshape(rows, heads_here, head_size), cosine, -sine).reshape(
        rows, local_width
    )
    grad_query_gain = jnp.sum(grad_query_norm * query_hat, axis=0)
    grad_key_gain = jnp.sum(grad_key_norm * key_hat, axis=0)
    normed_query = grad_query_norm * query_gain_here
    normed_key = grad_key_norm * key_gain_here
    inner_query, inner_key = lax.psum(
        (jnp.sum(normed_query * query_hat, axis=1), jnp.sum(normed_key * key_hat, axis=1)), "col"
    )
    grad_query_low = (
        query_scale * (normed_query - query_hat * inner_query[:, None] / width)
    ).astype(bfloat)
    grad_key_low = (key_scale * (normed_key - key_hat * inner_key[:, None] / width)).astype(bfloat)
    grad_value_low = grad_values.reshape(rows, local_width)
    grad_in_part = (
        cross_cols(grad_query_low, query_full)
        + cross_cols(grad_key_low, key_full)
        + cross_cols(grad_value_low, value_full)
    )
    grad_inputs = grad_middle_here + lax.psum_scatter(
        grad_in_part, "col", scatter_dimension=1, tiled=True
    )
    grad_query = cross_rows(whole_in, grad_query_low)
    grad_key = cross_rows(whole_in, grad_key_low)
    grad_value = cross_rows(whole_in, grad_value_low)
    summed = (
        lax.psum_scatter(grad_query, "row", scatter_dimension=0, tiled=True),
        lax.psum_scatter(grad_key, "row", scatter_dimension=0, tiled=True),
        lax.psum_scatter(grad_value, "row", scatter_dimension=0, tiled=True),
        lax.psum_scatter(grad_output, "row", scatter_dimension=0, tiled=True),
        lax.psum_scatter(grad_gate, "row", scatter_dimension=0, tiled=True),
        lax.psum_scatter(grad_up, "row", scatter_dimension=0, tiled=True),
        lax.psum_scatter(grad_down, "row", scatter_dimension=0, tiled=True),
    )
    gains = lax.psum((grad_query_gain, grad_key_gain, grad_attn_gain, grad_mlp_gain), "row")
    return (
        layer_out,
        grad_inputs,
        summed[0],
        summed[1],
        summed[2],
        summed[3],
        summed[4],
        summed[5],
        summed[6],
        gains[0],
        gains[1],
        gains[2],
        gains[3],
    )


BF = jnp.bfloat16
F32 = jnp.float32
MESH_ID = pl.DeviceIdType.MESH
T = 512
DC = 256
DR = 512
D = 2048
FH = 512
HT = 256
LAYER_STAGES = 5
EXACT = lax.Precision.HIGHEST


def dot_nn(a, b):
    return jnp.dot(a, b, preferred_element_type=F32)


def dot_nt(a, b, precision=None):
    return lax.dot_general(
        a, b, (((1,), (1,)), ((), ())), precision=precision, preferred_element_type=F32
    )


def dot_tn(a, b, precision=None):
    return lax.dot_general(
        a, b, (((0,), (0,)), ((), ())), precision=precision, preferred_element_type=F32
    )


def aligned(start, size):
    return pl.ds(pl.multiple_of(start, size), size)


class Counter:
    def __init__(self):
        self.used = 0

    def take(self, count=1):
        first = self.used
        self.used += count
        return first


def block_kernel(
    x_hbm,
    wq_hbm,
    wk_hbm,
    wv_hbm,
    wo_hbm,
    wg_hbm,
    wu_hbm,
    wd_hbm,
    cot_hbm,
    query_gain_hbm,
    key_gain_hbm,
    attn_gain_hbm,
    mlp_gain_hbm,
    pos_hbm,
    layer_out,
    grad_in,
    gains_out,
    land_mlp,
    land_attn,
    wqkv,
    wo,
    wgu,
    wd,
    x_full,
    mid_full,
    gf_full,
    gb_full,
    gu_s,
    mixed_s,
    probs_s,
    hat_s,
    low_s,
    cos_s,
    sin_s,
    pos_s,
    cot_z,
    braw_s,
    raw_s,
    middle_s,
    bhat_s,
    work_s,
    inner_s,
    att_s,
    ga_s,
    gqkv_s,
    gs_s,
    gqk_s,
    own_s,
    stage_c,
    land_c,
    stage_y,
    land_y,
    stage_z,
    land_z,
    land_r,
    scal_s,
    gain_s,
    stage_down,
    stage_gu,
    rel_mlp,
    rel_attn,
    out_lo,
    query_gain_ref,
    key_gain_ref,
    attn_gain_ref,
    mlp_gain_ref,
    pos_ref,
    send_sem,
    recv_sem,
    local_sem,
):
    row = lax.axis_index("row")
    col = lax.axis_index("col")
    x_at = lax.rem(row, 2)
    y_at = lax.div(row, 2)
    core = lax.rem(col, 2)
    z_at = lax.div(col, 2)
    row_x = row + 1 - 2 * x_at
    row_y = lax.rem(row + 2, 4)
    row_d = row_y + 1 - 2 * x_at
    sib = col + 1 - 2 * core
    dev_x = (row_x, col)
    dev_y = (row_y, col)
    dev_d = (row_d, col)
    dev_c = (row, sib)
    z_pair = {
        0: z_at,
        1: z_at + 1 - 2 * lax.rem(z_at, 2),
        2: lax.rem(z_at + 2, 4),
        3: 3 - z_at,
    }
    middle = (z_at == 1) | (z_at == 2)
    at_end = (z_at == 0) | (z_at == 3)
    dev_z = {pair: (row, 2 * z_pair[pair] + core) for pair in (1, 2, 3)}

    counter = Counter()
    locals_used = Counter()
    pending = []

    def copy_of(index, src, dst, device, send_index=None):
        return pltpu.make_async_remote_copy(
            src_ref=src,
            dst_ref=dst,
            send_sem=send_sem.at[index if send_index is None else send_index],
            recv_sem=recv_sem.at[index],
            device_id=device,
            device_id_type=MESH_ID,
        )

    def send(index, src, dst, device, send_index=None, when=None):
        copy = copy_of(index, src, dst, device, send_index)
        if when is None:
            copy.start()
        else:
            pl.when(when)(copy.start)
        pending.append((copy, when))
        return copy, when

    def arrived(index, dst, when=None):
        copy = copy_of(index, dst, dst, dev_c)
        if when is None:
            copy.wait_recv()
        else:
            pl.when(when)(copy.wait_recv)

    def sent(started):
        copy, when = started
        if when is None:
            copy.wait_send()
        else:
            pl.when(when)(copy.wait_send)
        pending[:] = [other for other in pending if other[0] is not copy]

    def local(src, dst):
        copy = pltpu.make_async_copy(src, dst, local_sem.at[locals_used.take()])
        copy.start()
        return copy

    barrier = pltpu.get_barrier_semaphore()
    partners = [dev_x, dev_y, dev_d] + [(row, lax.rem(col + step, 8)) for step in range(1, 8)]
    for device in partners:
        pl.semaphore_signal(barrier, inc=1, device_id=device, device_id_type=MESH_ID)

    @pl.when(at_end)
    def _():
        land_r[...] = jnp.zeros_like(land_r)
        land_z[0] = jnp.zeros_like(land_z[0])

    small_copies = [
        local(query_gain_hbm, query_gain_ref),
        local(key_gain_hbm, key_gain_ref),
        local(attn_gain_hbm, attn_gain_ref),
        local(mlp_gain_hbm, mlp_gain_ref),
    ]
    pos_copy = local(pos_hbm, pos_ref)
    half_mine = aligned(y_at * FH, FH)
    half_other = aligned((1 - y_at) * FH, FH)
    rows_mine = aligned(row * DR, DR)
    local_copies = [local(x_hbm, x_full.at[:, aligned(col * DC, DC)]), local(cot_hbm, cot_z.at[z_at])]
    for index, ref in enumerate((wq_hbm, wk_hbm, wv_hbm)):
        local_copies.append(local(ref, wqkv.at[rows_mine, pl.ds(index * DC, DC)]))
    local_copies.append(local(wo_hbm, wo.at[rows_mine, :]))
    local_copies.append(local(wg_hbm.at[:, half_mine], wgu.at[rows_mine, pl.ds(0, FH)]))
    local_copies.append(local(wu_hbm.at[:, half_mine], wgu.at[rows_mine, pl.ds(FH, FH)]))
    local_copies.append(local(wd_hbm.at[:, half_mine], wd.at[rows_mine, :]))
    pl.semaphore_wait(barrier, len(partners))

    def own_rows(half, plane):
        if plane:
            return aligned(half * 2 * HT + y_at * HT, HT)
        return pl.ds(half * HT, HT)

    def other_rows(half):
        return aligned(half * 2 * HT + (1 - y_at) * HT, HT)

    def half_rows(half, plane):
        count = 2 * HT if plane else HT
        return pl.ds(half * count, count)

    def tokens(half):
        return pl.ds(half * HT, HT)

    gather_base = counter.take(2 * 16)
    gather_sends = ([], [])

    class Gather:
        def __init__(self, buf, plane, raw, process, half):
            self.buf = buf
            self.plane = plane
            self.raw = raw
            self.process = process
            self.half = half
            self.base_z = gather_base + 16 * half
            self.relay = self.base_z + 3
            self.base_c = self.base_z + 4
            self.base_y = self.base_z + 8
            self.base_cy = self.base_z + 12
            self.rows = own_rows(half, plane)
            if plane:
                self.rows_other = other_rows(half)

        def block(self, rows, place, parity=None):
            at = 2 * place + (core if parity is None else parity)
            return rows, aligned(at * DC, DC)

        def start(self):
            self.finish_sends()
            own = self.raw.at[z_at, tokens(self.half)]
            for pair in (2, 3, 1):
                when = middle if pair == 3 else None
                self.send(self.base_z + pair - 1, own, own, dev_z[pair], None, when)

        def send(self, *copy):
            gather_sends[self.half].append(send(*copy))

        def pass_on(self, *pairs):
            for pair in pairs:
                place = z_pair[pair]
                if pair:
                    raw = self.raw.at[place, tokens(self.half)]
                    arrived(self.base_z + pair - 1, raw)
                if pair == 2:
                    self.send(self.base_z + 2, raw, raw, dev_z[1], self.relay, middle)
                where = self.block(self.rows, place)
                self.buf[where] = self.process(pair, place, self.half)
                block = self.buf.at[where]
                if self.plane:
                    self.send(self.base_y + pair, block, block, dev_y)
                self.send(self.base_c + pair, block, block, dev_c)

        def finish_own(self):
            for pair in range(4):
                arrived(
                    self.base_c + pair, self.buf.at[self.block(self.rows, z_pair[pair], 1 - core)]
                )

        def finish_sends(self):
            for copy in gather_sends[self.half]:
                sent(copy)
            gather_sends[self.half].clear()

        def finish_other(self):
            for pair in range(4):
                block = self.buf.at[self.block(self.rows_other, z_pair[pair])]
                arrived(self.base_y + pair, block)
                self.send(self.base_cy + pair, block, block, dev_c)
            for pair in range(4):
                arrived(
                    self.base_cy + pair,
                    self.buf.at[self.block(self.rows_other, z_pair[pair], 1 - core)],
                )

    reduce_base = counter.take(2 * 12)
    stage_sends = ([], [])

    class Reduce:
        ORDER = (3, 1, 2, 0)

        def __init__(self, partial, plane, half):
            self.partial = partial
            self.plane = plane
            self.half = half
            self.base_c = reduce_base + 12 * half
            self.base_z = self.base_c + 4
            self.relay = self.base_c + 7
            self.base_y = self.base_c + 8
            self.left = half_rows(half, plane)
            self.all_rows = pl.ds(half * 2 * HT, 2 * HT if plane else HT)
            self.rows = own_rows(half, True) if plane else self.all_rows
            self.tokens = tokens(half)
            if plane:
                self.rows_other = other_rows(half)

        def start(self):
            for copy in stage_sends[self.half]:
                sent(copy)
            stage_sends[self.half].clear()
            rows = self.all_rows
            for slot, pair in enumerate(self.ORDER):
                target = z_pair[pair]
                start = pl.multiple_of((2 * target + 1 - core) * DC, DC)
                stage_c[slot, rows, :] = self.partial(self.left, start).astype(BF)
                self.send(
                    self.base_c + slot, stage_c.at[slot, rows, :], land_c.at[slot, rows, :], dev_c
                )
                start = pl.multiple_of((2 * target + core) * DC, DC)
                own_s[slot, rows, :] = self.partial(self.left, start)
                if slot:
                    self.cores(slot - 1)
            self.cores(3)

        def send(self, *copy):
            stage_sends[self.half].append(send(*copy))

        def cores(self, slot):
            arrived(self.base_c + slot, land_c.at[slot, self.all_rows, :])
            if self.plane:
                rows = self.rows_other
                stage_y[slot, self.tokens, :] = (
                    own_s[slot, rows, :] + land_c[slot, rows, :].astype(F32)
                ).astype(BF)
                self.send(
                    self.base_y + slot,
                    stage_y.at[slot, self.tokens],
                    land_y.at[slot, self.tokens],
                    dev_y,
                )
                rows = self.rows
                own_s[slot, rows, :] = own_s[slot, rows, :] + land_c[slot, rows, :].astype(F32)
            else:
                self.pass_on(slot, land_c.at[slot, self.rows, :])

        def pass_on(self, slot, landed):
            pair = self.ORDER[slot]
            total = own_s[slot, self.rows, :] + landed[...].astype(F32)
            if pair == 0:
                own_s[slot, self.rows, :] = total
                return
            if pair == 2:
                arrived(self.relay, land_r.at[self.tokens], middle)
                total = total + land_r[self.tokens, :].astype(F32)
            stage_z[slot, self.tokens, :] = total.astype(BF)
            stage, land = stage_z.at[slot, self.tokens], land_z.at[slot, self.tokens]
            if pair == 3:
                index = self.base_z + slot
                self.send(index, stage, land, dev_z[3], None, middle)
                self.send(self.relay, stage, land_r.at[self.tokens], dev_z[1], None, at_end)
            else:
                self.send(self.base_z + slot, stage, land, dev_z[pair])

        def planes(self, *slots):
            for slot in slots:
                landed = land_y.at[slot, self.tokens]
                arrived(self.base_y + slot, landed)
                self.pass_on(slot, landed)

        def finish(self):
            for slot in range(3):
                when = middle if self.ORDER[slot] == 3 else None
                arrived(self.base_z + slot, land_z.at[slot, self.tokens], when)
            total = own_s[3, self.rows, :]
            for slot in range(3):
                total = total + land_z[slot, self.tokens, :].astype(F32)
            return total

    pick = lax.broadcasted_iota(jnp.int32, (8, DC), 0)
    lane = lax.broadcasted_iota(jnp.int32, (8, DC), 1)
    first_row = (pick == 0).astype(F32)
    second_row = (pick == 1).astype(F32)
    spread = ((pick == 0) & (lane < 128)).astype(F32) + ((pick == 1) & (lane >= 128)).astype(F32)
    scal_base = counter.take(4 * 7)
    scal_sends = ([], [], [], [])

    def scal_send(stage, half, first, second=None):
        mine = dot_nt(first_row, first, EXACT)
        if second is not None:
            mine = mine + dot_nt(second_row, second, EXACT)
        place = scal_s.at[stage, half, col]
        place[...] = mine
        turn = 2 * half + stage % 2
        for copy in scal_sends[turn]:
            sent(copy)
        scal_sends[turn].clear()
        for step in range(1, 8):
            index = scal_base + 7 * turn + step - 1
            scal_sends[turn].append(send(index, place, place, (row, lax.rem(col + step, 8))))

    def scal_get(stage, half):
        for step in range(1, 8):
            index = scal_base + 7 * (2 * half + stage % 2) + step - 1
            arrived(index, scal_s.at[stage, half, lax.rem(col + 8 - step, 8)])
        total = scal_s[stage, half, 0]
        for index in range(1, 8):
            total = total + scal_s[stage, half, index]
        both = dot_tn(total, spread, EXACT)
        return both[:, :128], both[:, 128:]

    HALVES = (0, 1)

    def wide(values):
        return jnp.concatenate([values, values], axis=1)

    attn_base = counter.take(16)
    weight_sends = []
    attn_hbm = (wq_hbm, wk_hbm, wv_hbm, wo_hbm)

    def attn_place(index, owner, part=None):
        if part is None:
            rows = aligned(owner * DR, DR)
        else:
            rows = aligned(owner * DR + part * (DR // 2), DR // 2)
        if index < 3:
            return wqkv.at[rows, pl.ds(index * DC, DC)]
        return wo.at[rows, :]

    def weight_send(*copy):
        weight_sends.append(send(*copy))

    def attn_send(index):
        weight_send(attn_base + index, attn_hbm[index], attn_place(index, row), dev_x)
        weight_send(attn_base + 4 + index, attn_hbm[index], attn_place(index, row), dev_y)

    def attn_relay(index):
        arrived(attn_base + index, attn_place(index, row_x))
        part = attn_place(index, row_x, 0 if index < 3 else None)
        weight_send(attn_base + 8 + index, part, part, dev_y)
        arrived(attn_base + 4 + index, attn_place(index, row_y))
        if index < 3:
            part = attn_place(index, row_y, 1)
            weight_send(attn_base + 12 + index, part, part, dev_x)

    def attn_ready(index):
        arrived(attn_base + 8 + index, attn_place(index, row_d, 0 if index < 3 else None))
        if index < 3:
            arrived(attn_base + 12 + index, attn_place(index, row_d, 1))

    mlp_base = counter.take(9)
    mlp_hbm = (wg_hbm, wu_hbm, wd_hbm)

    def mlp_place(index, owner):
        rows = aligned(owner * DR, DR)
        if index < 2:
            return wgu.at[rows, pl.ds(index * FH, FH)]
        return wd.at[rows, :]

    def mlp_send(index):
        weight_send(mlp_base + index, mlp_hbm[index].at[:, half_mine], mlp_place(index, row), dev_x)
        weight_send(mlp_base + 3 + index, mlp_hbm[index].at[:, half_other], mlp_place(index, row), dev_y)

    def mlp_relay(index):
        place = mlp_place(index, row_y)
        arrived(mlp_base + 3 + index, place)
        weight_send(mlp_base + 6 + index, place, place, dev_x)

    def mlp_ready(index):
        arrived(mlp_base + index, mlp_place(index, row_x))
        arrived(mlp_base + 6 + index, mlp_place(index, row_d))

    for index in range(2):
        attn_send(index)

    x_base = counter.take(7)
    cot_base = counter.take(3)

    def x_block(place, parity):
        return x_full.at[:, aligned((2 * place + parity) * DC, DC)]

    for pair in (2, 3, 1):
        send(x_base + pair - 1, x_hbm, x_block(z_at, core), dev_z[pair])
    send(x_base + 3, x_hbm, x_block(z_at, core), dev_c)

    pos_copy.wait()
    position_rows = jnp.broadcast_to(pos_ref[...].astype(F32), (8, T))
    position = dot_tn(position_rows, first_row[:, :HD], EXACT)
    pos_s[...] = position.astype(jnp.int32)
    lane_at = lax.broadcasted_iota(jnp.int32, (1, HD), 1)
    within = lax.rem(lane_at, HD // 2).astype(F32)
    frequency = jnp.exp(within * (-2.0 * math.log(THETA) / HD))
    angles = position * frequency
    cos_s[...] = jnp.cos(angles)
    sine = jnp.sin(angles)
    sin_s[...] = jnp.where(lane_at < HD // 2, -sine, sine)

    for index in range(2):
        attn_relay(index)
    attn_send(2)
    attn_send(3)
    for pair in (2, 1, 3):
        block = x_block(z_pair[pair], core)
        arrived(x_base + pair - 1, block)
        send(x_base + 3 + pair, block, block, dev_c)
    for copy in local_copies + small_copies:
        copy.wait()
    for pair in range(4):
        arrived(x_base + 3 + pair, x_block(z_pair[pair], 1 - core))
    attn_ready(0)
    attn_ready(1)

    def gain_at(ref, at):
        return ref[:, aligned(at * DC, DC)]

    qk_gain = (gain_at(query_gain_ref, col), gain_at(key_gain_ref, col))
    for index in range(2):
        hat_s[index] = dot_nn(x_full[...], wqkv[:, pl.ds(index * DC, DC)])
    for half in HALVES:
        query, key = hat_s[0, tokens(half), :], hat_s[1, tokens(half), :]
        scal_send(0, half, query * query, key * key)
    attn_relay(2)
    attn_relay(3)
    for index in range(3):
        mlp_send(index)
    attn_ready(2)
    low_s[2] = dot_nn(x_full[...], wqkv[:, pl.ds(2 * DC, DC)]).astype(BF)
    for half in HALVES:
        scales = [lax.rsqrt(total / D + EPS) for total in scal_get(0, half)]
        rows = tokens(half)
        work_s[0, rows, :] = jnp.concatenate(scales, axis=1)
        for index in range(2):
            hat = hat_s[index, rows, :] * wide(scales[index])
            hat_s[index, rows, :] = hat
            normed = hat * qk_gain[index]
            for head in range(2):
                part = normed[:, head * HD : (head + 1) * HD]
                turned = part * cos_s[rows, :] + pltpu.roll(part, HD // 2, 1) * sin_s[rows, :]
                if index == 0:
                    turned = turned * (HD**-0.5)
                low_s[index, rows, pl.ds(head * HD, HD)] = turned.astype(BF)

    chunk = 128

    def attend(half):
        count = (half + 1) * HT
        keys = pl.ds(0, count)

        def attend_chunk(at, carry):
            rows = aligned(at * chunk, chunk)
            query = at * chunk + lax.broadcasted_iota(jnp.int32, (chunk, count), 0)
            key = lax.broadcasted_iota(jnp.int32, (chunk, count), 1)
            oldest = query - pos_s[rows, :1]
            allowed = (key <= query) & (key >= oldest)
            for head in range(2):
                lanes = pl.ds(head * HD, HD)
                scores = dot_nt(low_s[0, rows, lanes], low_s[1, keys, lanes])
                scores = jnp.where(allowed, scores, MASKED)
                exponent = jnp.exp(scores - jnp.max(scores, axis=1, keepdims=True))
                probs = exponent / jnp.sum(exponent, axis=1, keepdims=True)
                probs_s[head, rows, keys] = probs
                att_s[rows, lanes] = dot_nn(probs.astype(BF), low_s[2, keys, lanes]).astype(BF)
            return carry

        first = half * (HT // chunk)
        lax.fori_loop(first, first + HT // chunk, attend_chunk, 0)

    branch_sums = [
        Reduce(
            lambda rows, start: dot_nt(att_s[rows, :], wo[pl.ds(start, DC), :]), False, half
        )
        for half in HALVES
    ]

    def middle_block(pair, place, half):
        rows = tokens(half)
        at = 2 * place + core
        raw = work_s[1, rows, :] if pair == 0 else braw_s[place, rows, :].astype(F32)
        hat = raw * wide(work_s[2, rows, :128])
        inputs = x_full[rows, aligned(at * DC, DC)].astype(F32)
        middle = inputs + hat * gain_at(attn_gain_ref, at)
        if pair == 0:
            bhat_s[rows, :] = hat
            middle_s[rows, :] = middle
        return middle.astype(BF)

    mid_gathers = [Gather(mid_full, True, braw_s, middle_block, half) for half in HALVES]

    def branch_done(half):
        rows = tokens(half)
        branch = branch_sums[half].finish()
        scal_send(1, half, branch * branch)
        work_s[1, rows, :] = branch
        braw_s[z_at, rows, :] = branch.astype(BF)
        mid_gathers[half].start()

    def branch_scaled(half):
        total, _ = scal_get(1, half)
        work_s[2, tokens(half), :128] = lax.rsqrt(total / D + EPS)

    attend(0)
    attn_ready(3)
    branch_sums[0].start()
    attend(1)
    branch_sums[1].start()
    mlp_relay(0)
    branch_done(0)
    mlp_relay(1)
    branch_scaled(0)
    mid_gathers[0].pass_on(0)
    branch_done(1)
    mid_gathers[0].pass_on(2, 1, 3)
    branch_scaled(1)
    mid_gathers[1].pass_on(0)
    mlp_relay(2)
    mid_gathers[1].pass_on(2, 1, 3)
    for pair in (2, 3, 1):
        weight_send(cot_base + pair - 1, cot_z.at[z_at], cot_z.at[z_at], dev_z[pair])
    mid_gathers[0].finish_own()
    mid_gathers[0].finish_other()
    mlp_ready(0)
    mlp_ready(1)

    tile = 256

    def forward_tiles(half):
        rows = half_rows(half, True)

        def forward_tile(at, carry):
            lanes = aligned(at * tile, tile)
            lanes_up = aligned(at * tile + FH, tile)
            gate = dot_nn(mid_full[rows, :], wgu[:, lanes])
            up = dot_nn(mid_full[rows, :], wgu[:, lanes_up])
            gu_s[rows, lanes] = gate.astype(BF)
            gu_s[rows, lanes_up] = up.astype(BF)
            mixed_s[rows, lanes] = (gate * jax.nn.sigmoid(gate) * up).astype(BF)
            return carry

        lax.fori_loop(0, FH // tile, forward_tile, 0)

    ffn_sums = [
        Reduce(
            lambda rows, start: dot_nt(mixed_s[rows, :], wd[pl.ds(start, DC), :]), True, half
        )
        for half in HALVES
    ]
    mlp_gain = gain_at(mlp_gain_ref, col)

    def grad_ffn_block(pair, place, half):
        rows = tokens(half)
        at = 2 * place + core
        raw = work_s[1, rows, :] if pair == 0 else raw_s[place, rows, :].astype(F32)
        scale = wide(work_s[2, rows, 128:])
        grad = cot_z[place, rows, :].astype(F32) * gain_at(mlp_gain_ref, at)
        return (scale * (grad - raw * scale * wide(inner_s[rows, :]))).astype(BF)

    gf_gathers = [Gather(gf_full, True, raw_s, grad_ffn_block, half) for half in HALVES]

    def ffn_done(half):
        rows = tokens(half)
        ffn = ffn_sums[half].finish()
        cot = cot_z[z_at, rows, :].astype(F32)
        scal_send(2, half, ffn * ffn, cot * mlp_gain * ffn)
        work_s[1, rows, :] = ffn
        raw_s[z_at, rows, :] = ffn.astype(BF)
        gf_gathers[half].start()

    def ffn_scaled(half):
        rows = tokens(half)
        total, inner = scal_get(2, half)
        scale = lax.rsqrt(total / D + EPS)
        work_s[2, rows, 128:] = scale
        inner_s[rows, :] = inner * scale / D
        ffn_hat = work_s[1, rows, :] * wide(scale)
        out_lo[rows, :] = (middle_s[rows, :] + ffn_hat * mlp_gain).astype(BF)
        cot = cot_z[z_at, rows, :].astype(F32)
        return jnp.sum(cot * ffn_hat, axis=0, keepdims=True)

    forward_tiles(0)
    mlp_ready(2)
    ffn_sums[0].start()
    mid_gathers[1].finish_own()
    mid_gathers[1].finish_other()
    forward_tiles(1)
    ffn_sums[1].start()
    ffn_sums[0].planes(0, 1, 2, 3)
    ffn_sums[1].planes(0, 1)
    for pair in (1, 2, 3):
        arrived(cot_base + pair - 1, cot_z.at[z_pair[pair]])
    ffn_done(0)
    ffn_sums[1].planes(2, 3)
    mlp_gain_part = ffn_scaled(0)
    gf_gathers[0].pass_on(0)
    ffn_done(1)
    gf_gathers[0].pass_on(2, 1, 3)
    gain_s[row, 3:4, :] = mlp_gain_part + ffn_scaled(1)
    gf_gathers[1].pass_on(0, 2, 1, 3)
    lo_copy = local(out_lo, layer_out)
    gf_gathers[0].finish_own()
    gf_gathers[0].finish_other()

    def backward_tiles(half):
        rows = half_rows(half, True)

        def backward_tile(at, carry):
            lanes = aligned(at * tile, tile)
            lanes_up = aligned(at * tile + FH, tile)
            grad_mixed = dot_nn(gf_full[rows, :], wd[:, lanes])
            gate = gu_s[rows, lanes].astype(F32)
            up = gu_s[rows, lanes_up].astype(F32)
            sigma = jax.nn.sigmoid(gate)
            gu_s[rows, lanes] = (grad_mixed * up * sigma * (1.0 + gate * (1.0 - sigma))).astype(BF)
            gu_s[rows, lanes_up] = (grad_mixed * gate * sigma).astype(BF)
            return carry

        lax.fori_loop(0, FH // tile, backward_tile, 0)

    def lanes_of(owner):
        return aligned(owner * DR, DR)

    def down_piece(owner):
        return dot_tn(gf_full[:, lanes_of(owner)], mixed_s[...])

    def gu_piece(owner, part):
        return dot_tn(mid_full[:, lanes_of(owner)], gu_s[:, pl.ds(part * FH, FH)])

    grad_base = counter.take(9)
    grad_sends = {}

    def grad_lanes(part):
        return pl.ds(part * FH, FH)

    def grad_stage(slot, part):
        if part == 2:
            return stage_down.at[slot]
        return stage_gu.at[slot, :, grad_lanes(part)]

    def grad_piece(slot, part, more=None):
        owner = (row_d, row_x, row_y, row)[slot]
        total = down_piece(owner) if part == 2 else gu_piece(owner, part)
        if more is not None:
            total = total + more
        grad_stage(slot, part)[...] = total.astype(BF)

    def grad_send(slot, part, landing, device):
        index = grad_base + 3 * slot + part
        grad_sends[slot, part] = send(index, grad_stage(slot, part), landing, device)

    def grad_diagonal(part):
        grad_piece(0, part)
        grad_send(0, part, rel_mlp.at[:, grad_lanes(part)], dev_x)

    def grad_near(part):
        grad_piece(1, part)
        grad_send(1, part, land_mlp.at[1, :, grad_lanes(part)], dev_x)

    def grad_relay(part):
        arrived(grad_base + part, rel_mlp.at[:, grad_lanes(part)])
        grad_piece(2, part, rel_mlp[:, grad_lanes(part)].astype(F32))
        grad_send(2, part, land_mlp.at[2, :, grad_lanes(part)], dev_y)

    mid_sums = [
        Reduce(lambda rows, start: dot_nt(gu_s[rows, :], wgu[pl.ds(start, DC), :]), True, half)
        for half in HALVES
    ]
    attn_gain = gain_at(attn_gain_ref, col)

    def grad_branch_block(pair, place, half):
        rows = tokens(half)
        at = 2 * place + core
        scale = wide(work_s[2, rows, :128])
        raw = middle_s[rows, :] if pair == 0 else raw_s[place, rows, :].astype(F32)
        hat = bhat_s[rows, :] if pair == 0 else braw_s[place, rows, :].astype(F32) * scale
        inner = wide(inner_s[rows, :])
        return (scale * (raw * gain_at(attn_gain_ref, at) - hat * inner)).astype(BF)

    gb_gathers = [Gather(gb_full, False, raw_s, grad_branch_block, half) for half in HALVES]

    def mid_done(half):
        rows = tokens(half)
        grad_middle = cot_z[z_at, rows, :].astype(F32) + mid_sums[half].finish()
        scal_send(3, half, grad_middle * attn_gain * bhat_s[rows, :])
        middle_s[rows, :] = grad_middle
        raw_s[z_at, rows, :] = grad_middle.astype(BF)
        gb_gathers[half].start()

    def mid_scaled(half):
        inner, _ = scal_get(3, half)
        inner_s[tokens(half), :] = inner / D

    backward_tiles(0)
    gf_gathers[0].finish_sends()
    mid_sums[0].start()
    gf_gathers[1].finish_own()
    gf_gathers[1].finish_other()
    grad_diagonal(2)
    backward_tiles(1)
    gf_gathers[1].finish_sends()
    mid_sums[1].start()
    grad_diagonal(0)
    grad_diagonal(1)
    mid_sums[0].planes(0, 1, 2, 3)
    mid_sums[1].planes(0, 1)
    mid_done(0)
    mid_sums[1].planes(2, 3)
    grad_relay(2)
    grad_near(2)
    mid_scaled(0)
    gb_gathers[0].pass_on(0)
    mid_done(1)
    grad_near(0)
    gb_gathers[0].pass_on(2, 1, 3)
    mid_scaled(1)
    gb_gathers[1].pass_on(0)
    grad_relay(0)
    grad_near(1)
    gb_gathers[1].pass_on(2, 1, 3)
    grad_relay(1)
    gain_s[row, 2:3, :] = jnp.sum(middle_s[...] * bhat_s[...], axis=0, keepdims=True)
    gb_gathers[0].finish_own()
    gb_gathers[1].finish_own()

    ga_s[...] = dot_nn(gb_full[...], wo[...]).astype(BF)

    whole = pl.ds(0, DR)
    upper = pl.ds(0, DR // 2)
    lower = pl.ds(DR // 2, DR // 2)
    BY_Y = ((whole, 2),)
    BY_BOTH = ((upper, 1), (lower, 2))
    neighbours = {1: dev_x, 2: dev_y}
    attn_grad_base = counter.take(3 * 6)
    late = []

    class AttnGrad:
        def __init__(self, order, routes, left, right, start, size):
            self.base = attn_grad_base + 6 * order
            self.routes = routes
            self.left, self.right = left, right
            self.start_lane, self.size = start, size
            self.lanes = pl.ds(start, size)

        def at(self, slot, rows):
            rows = pl.ds(slot // 2 * DR + rows.start, rows.size)
            return gf_full.at[rows, pl.ds(slot % 2 * 4 * DC + self.start_lane, self.size)]

        def piece(self, slot):
            owner = (row_d, row_x, row_y, row)[slot]
            piece = dot_tn(self.left[:, lanes_of(owner)], self.right())
            self.at(slot, whole)[...] = piece.astype(BF)

        def start(self):
            self.piece(0)
            for step, (rows, first) in enumerate(self.routes):
                landing = rel_attn.at[rows, self.lanes]
                send(self.base + step, self.at(0, rows), landing, neighbours[first])
            self.piece(1)
            self.piece(2)
            for step, (rows, first) in enumerate(self.routes):
                landing = land_attn.at[first, rows, self.lanes]
                send(self.base + 2 + step, self.at(first, rows), landing, neighbours[first])
            self.piece(3)
            late.append(local(self.at(3, whole), land_attn.at[0, :, self.lanes]))

        def relay(self):
            for step, (rows, first) in enumerate(self.routes):
                slot = 3 - first
                arrived(self.base + step, rel_attn.at[rows, self.lanes])
                stage = self.at(slot, rows)
                stage[...] = (
                    stage[...].astype(F32) + rel_attn[rows, self.lanes].astype(F32)
                ).astype(BF)
                landing = land_attn.at[slot, rows, self.lanes]
                send(self.base + 4 + step, stage, landing, neighbours[slot])

        def finish(self):
            for step, (rows, first) in enumerate(self.routes):
                arrived(self.base + 2 + step, land_attn.at[first, rows, self.lanes])
                arrived(self.base + 4 + step, land_attn.at[3 - first, rows, self.lanes])

    grad_piece(3, 2)
    late.append(local(stage_down.at[3], land_mlp.at[0, :, grad_lanes(2)]))
    for gather in gf_gathers:
        gather.finish_sends()
    o_grad = AttnGrad(0, BY_BOTH, gb_full, lambda: att_s[...], 3 * DC, DC)
    o_grad.start()

    def attend_back(half):
        count = (half + 1) * HT
        keys = pl.ds(0, count)

        def attend_back_chunk(at, carry):
            rows = aligned(at * chunk, chunk)
            for head in range(2):
                lanes = pl.ds(head * HD, HD)
                grad_probs = dot_nt(ga_s[rows, lanes], low_s[2, keys, lanes])
                probs = probs_s[head, rows, keys]
                inner = jnp.sum(probs * grad_probs, axis=1, keepdims=True)
                grad_scores = (probs * (grad_probs - inner)).astype(BF)
                gs_s[head, rows, keys] = grad_scores
                gqk_s[0, rows, lanes] = dot_nn(grad_scores, low_s[1, keys, lanes])
            return carry

        first = half * (HT // chunk)
        lax.fori_loop(first, first + HT // chunk, attend_back_chunk, 0)

    for half in HALVES:
        attend_back(half)
    early, last = pl.ds(0, HT), pl.ds(HT, HT)
    for head in range(2):
        lanes = pl.ds(head * HD, HD)
        gqk_s[1, early, lanes] = dot_tn(gs_s[head, :, early], low_s[0, :, lanes])
        gqk_s[1, last, lanes] = dot_tn(gs_s[head, last, last], low_s[0, last, lanes])
    inners = []
    for index in range(2):
        for head in range(2):
            lanes = pl.ds(head * HD, HD)
            part = gqk_s[index, :, lanes]
            turned = part * cos_s[...] - pltpu.roll(part, HD // 2, 1) * sin_s[...]
            if index == 0:
                turned = turned * (HD**-0.5)
            gqk_s[index, :, lanes] = turned
        weighted = gqk_s[index] * hat_s[index]
        gain_s[row, index : index + 1, :] = jnp.sum(weighted, axis=0, keepdims=True)
        inners.append(weighted * qk_gain[index])
    for half in HALVES:
        part = slice(half * HT, (half + 1) * HT)
        scal_send(4, half, inners[0][part], inners[1][part])
    gain_base = counter.take(3)
    for slot, device in enumerate((dev_x, dev_y, dev_d)):
        send(gain_base + slot, gain_s.at[row], gain_s.at[row], device)
    for head in range(2):
        lanes = pl.ds(head * HD, HD)
        out_lanes = pl.ds(2 * DC + head * HD, HD)
        gqkv_s[early, out_lanes] = dot_tn(
            probs_s[head, :, early].astype(BF), ga_s[:, lanes]
        ).astype(BF)
        gqkv_s[last, out_lanes] = dot_tn(
            probs_s[head, last, last].astype(BF), ga_s[last, lanes]
        ).astype(BF)
    v_grad = AttnGrad(1, BY_BOTH, x_full, lambda: gqkv_s[:, 2 * DC :], 2 * DC, DC)
    v_grad.start()
    for half in HALVES:
        rows = tokens(half)
        totals = scal_get(4, half)
        for index in range(2):
            scale = wide(work_s[0, rows, index * 128 : (index + 1) * 128])
            gqkv_s[rows, pl.ds(index * DC, DC)] = (
                scale
                * (
                    gqk_s[index, rows, :] * qk_gain[index]
                    - hat_s[index, rows, :] * wide(totals[index] / D)
                )
            ).astype(BF)
    in_sums = [
        Reduce(
            lambda rows, start: dot_nt(gqkv_s[rows, :], wqkv[pl.ds(start, DC), :]), False, half
        )
        for half in HALVES
    ]
    for half in HALVES:
        in_sums[half].start()
    o_grad.relay()
    qk_grad = AttnGrad(2, BY_BOTH, x_full, lambda: gqkv_s[:, : 2 * DC], 0, 2 * DC)
    qk_grad.start()
    v_grad.relay()
    grad_piece(3, 0)
    grad_piece(3, 1)
    late.append(local(stage_gu.at[3], land_mlp.at[0, :, pl.ds(0, 2 * FH)]))
    for half in HALVES:
        rows = tokens(half)
        work_s[1, rows, :] = middle_s[rows, :] + in_sums[half].finish()
    late.append(local(work_s.at[1], grad_in))
    late.append(lo_copy)
    qk_grad.relay()

    for slot, owner in enumerate((row_x, row_y, row_d)):
        arrived(gain_base + slot, gain_s.at[owner])
    gains_out[...] = gain_s[0] + gain_s[1] + gain_s[2] + gain_s[3]
    for slot in (1, 2):
        for part in range(3):
            arrived(grad_base + 3 * slot + part, land_mlp.at[slot, :, grad_lanes(part)])
    for grad in (o_grad, v_grad, qk_grad):
        grad.finish()
    for copy in late:
        copy.wait()
    for copy in list(pending):
        sent(copy)
    assert counter.used <= send_sem.shape[0], counter.used


def total_kernel(
    lo_ref, gin_ref, gains_ref, mlp_ref, attn_ref, lo_out, gin_out, *outs
):
    y_at = lax.div(lax.axis_index("row"), 2)
    lo_out[...] = lo_ref[...]
    gin_out[...] = gin_ref[...]
    attn = attn_ref[0].astype(F32) + attn_ref[1].astype(F32) + attn_ref[2].astype(F32)
    for index in range(4):
        outs[index][...] = attn[:, index * DC : (index + 1) * DC]
    mine = mlp_ref[0].astype(F32) + mlp_ref[1].astype(F32)
    other = mlp_ref[2].astype(F32)
    for index in range(3):
        lanes = slice(index * FH, (index + 1) * FH)
        outs[4 + index][:, aligned(y_at * FH, FH)] = mine[:, lanes]
        outs[4 + index][:, aligned((1 - y_at) * FH, FH)] = other[:, lanes]
    for index in range(4):
        outs[7 + index][...] = gains_ref[index : index + 1, :]


MIB = 1 << 20


def on_device_kernel(
    inputs,
    query_weight,
    key_weight,
    value_weight,
    output_weight,
    gate_weight,
    up_weight,
    down_weight,
    query_gain,
    key_gain,
    attn_gain,
    mlp_gain,
    positions,
    segments,
    cotangent,
):
    hbm = pl.BlockSpec(memory_space=pl.ANY)
    vmem = pl.BlockSpec(memory_space=pltpu.VMEM)
    sds = jax.ShapeDtypeStruct
    copies = 150
    landed = pl.pallas_call(
        block_kernel,
        out_shape=[
            sds((T, DC), BF),
            sds((T, DC), F32),
            sds((8, DC), F32),
            sds((3, DR, 3 * FH), BF),
            sds((3, DR, 4 * DC), BF),
        ],
        in_specs=[hbm] * 14,
        out_specs=[hbm, hbm, vmem, hbm, hbm],
        scratch_shapes=[
            pltpu.VMEM((D, 3 * DC), BF),
            pltpu.VMEM((D, DC), BF),
            pltpu.VMEM((D, 2 * FH), BF),
            pltpu.VMEM((D, FH), BF),
            pltpu.VMEM((T, D), BF),
            pltpu.VMEM((2 * T, D), BF),
            pltpu.VMEM((2 * T, D), BF),
            pltpu.VMEM((T, D), BF),
            pltpu.VMEM((2 * T, 2 * FH), BF),
            pltpu.VMEM((2 * T, FH), BF),
            pltpu.VMEM((2, T, T), F32),
            pltpu.VMEM((2, T, DC), F32),
            pltpu.VMEM((3, T, DC), BF),
            pltpu.VMEM((T, HD), F32),
            pltpu.VMEM((T, HD), F32),
            pltpu.VMEM((T, HD), jnp.int32),
            pltpu.VMEM((4, T, DC), BF),
            pltpu.VMEM((4, T, DC), BF),
            pltpu.VMEM((4, T, DC), BF),
            pltpu.VMEM((T, DC), F32),
            pltpu.VMEM((T, DC), F32),
            pltpu.VMEM((3, T, DC), F32),
            pltpu.VMEM((T, HD), F32),
            pltpu.VMEM((T, DC), BF),
            pltpu.VMEM((T, DC), BF),
            pltpu.VMEM((T, 3 * DC), BF),
            pltpu.VMEM((2, T, T), BF),
            pltpu.VMEM((2, T, DC), F32),
            pltpu.VMEM((4, 2 * T, DC), F32),
            pltpu.VMEM((4, 2 * T, DC), BF),
            pltpu.VMEM((4, 2 * T, DC), BF),
            pltpu.VMEM((4, T, DC), BF),
            pltpu.VMEM((4, T, DC), BF),
            pltpu.VMEM((3, T, DC), BF),
            pltpu.VMEM((3, T, DC), BF),
            pltpu.VMEM((T, DC), BF),
            pltpu.VMEM((LAYER_STAGES, 2, 8, 8, HT), F32),
            pltpu.VMEM((4, 8, DC), F32),
            pltpu.VMEM((4, DR, FH), BF),
            pltpu.VMEM((4, DR, 2 * FH), BF),
            pltpu.VMEM((DR, 3 * FH), BF),
            pltpu.VMEM((DR, 4 * DC), BF),
            pltpu.VMEM((T, DC), BF),
            pltpu.VMEM((1, D), F32),
            pltpu.VMEM((1, D), F32),
            pltpu.VMEM((1, D), F32),
            pltpu.VMEM((1, D), F32),
            pltpu.VMEM((1, T), jnp.int32),
            pltpu.SemaphoreType.DMA((copies,)),
            pltpu.SemaphoreType.DMA((copies,)),
            pltpu.SemaphoreType.DMA((24,)),
        ],
        compiler_params=pltpu.CompilerParams(
            collective_id=0, has_side_effects=True, vmem_limit_bytes=64 * MIB
        ),
        cost_estimate=pl.CostEstimate(
            flops=26_800_000_000, bytes_accessed=16_000_000, transcendentals=2_000_000
        ),
    )(
        inputs,
        query_weight,
        key_weight,
        value_weight,
        output_weight,
        gate_weight,
        up_weight,
        down_weight,
        cotangent,
        query_gain[None, :],
        key_gain[None, :],
        attn_gain[None, :],
        mlp_gain[None, :],
        positions[None, :],
    )
    step = 256

    def rows_of(width):
        return pl.BlockSpec((step, width), lambda at: (at, 0))

    gain_spec = pl.BlockSpec((1, DC), lambda at: (0, 0))
    results = pl.pallas_call(
        total_kernel,
        grid=(DR // step,),
        out_shape=[sds((T, DC), BF), sds((T, DC), F32)]
        + [sds((DR, DC), F32)] * 4
        + [sds((DR, 2 * FH), F32)] * 3
        + [sds((1, DC), F32)] * 4,
        in_specs=[
            rows_of(DC),
            rows_of(DC),
            pl.BlockSpec((8, DC), lambda at: (0, 0)),
            pl.BlockSpec((3, step, 3 * FH), lambda at: (0, at, 0)),
            pl.BlockSpec((3, step, 4 * DC), lambda at: (0, at, 0)),
        ],
        out_specs=[rows_of(DC)] * 6 + [rows_of(2 * FH)] * 3 + [gain_spec] * 4,
        compiler_params=pltpu.CompilerParams(vmem_limit_bytes=64 * MIB),
    )(*landed)
    return (*results[:9], *[gain[0] for gain in results[9:]])


def solution(mesh):
    in_specs = (
        P("row", "col"),
        P("row", "col"),
        P("row", "col"),
        P("row", "col"),
        P("row", "col"),
        P("row", "col"),
        P("row", "col"),
        P("row", "col"),
        P(),
        P(),
        P(),
        P(),
        P("row"),
        P("row"),
        P("row", "col"),
    )
    out_specs = (
        P("row", "col"),
        P("row", "col"),
        P("row", "col"),
        P("row", "col"),
        P("row", "col"),
        P("row", "col"),
        P("row", "col"),
        P("row", "col"),
        P("row", "col"),
        P("col"),
        P("col"),
        P("col"),
        P("col"),
    )
    sizes = (mesh.shape["row"], mesh.shape["col"])
    body = on_device_kernel if sizes == (4, 8) else on_device
    return jax.shard_map(
        body, mesh=mesh, in_specs=in_specs, out_specs=out_specs, check_vma=False
    )
```

```python
import math

import jax
import jax.numpy as jnp
from jax import lax
from jax.experimental import pallas as pl
from jax.experimental.pallas import tpu as pltpu
from jax.sharding import PartitionSpec as P

HD = 128
LENGTH = 512


EPS = 1e-06
THETA = 500000.0
MASKED = -1e30


def rope_tables(positions, head_size):
    halfway = head_size // 2
    frequency = jnp.exp(
        jnp.arange(halfway, dtype=jnp.float32) * (-2.0 * math.log(THETA) / head_size)
    )
    angles = positions.astype(jnp.float32)[:, None] * frequency[None, :]
    return (jnp.cos(angles)[:, None, :], jnp.sin(angles)[:, None, :])


def rotate(values, cosine, sine):
    halfway = values.shape[-1] // 2
    first_half = values[..., :halfway]
    second_half = values[..., halfway:]
    return jnp.concatenate(
        [first_half * cosine - second_half * sine, second_half * cosine + first_half * sine],
        axis=-1,
    )


def matmul(left, right):
    return jnp.dot(left, right, preferred_element_type=jnp.float32)


def cross_rows(left, right):
    return lax.dot_general(
        left, right, (((0,), (0,)), ((), ())), preferred_element_type=jnp.float32
    )


def cross_cols(left, right):
    return lax.dot_general(
        left, right, (((1,), (1,)), ((), ())), preferred_element_type=jnp.float32
    )


def visible_pairs(segment_part):
    places = jnp.arange(segment_part.shape[0])
    return (segment_part[:, None] == segment_part[None, :]) & (places[:, None] >= places[None, :])


def on_device(
    inputs,
    query_weight,
    key_weight,
    value_weight,
    output_weight,
    gate_weight,
    up_weight,
    down_weight,
    query_gain,
    key_gain,
    attn_gain,
    mlp_gain,
    positions,
    segments,
    cotangent,
):
    bfloat = jnp.bfloat16
    floats = jnp.float32
    rows = inputs.shape[0]
    local_width = inputs.shape[1]
    width = local_width * lax.axis_size("col")
    offset = lax.axis_index("col") * local_width
    head_size = HD
    heads_here = local_width // head_size
    sequences = rows // LENGTH
    scale = head_size ** (-0.5)
    shape_seq = (sequences, LENGTH, heads_here, head_size)

    def mine(values):
        return lax.dynamic_slice_in_dim(values, offset, local_width, values.ndim - 1)

    query_gain_here = mine(query_gain)
    key_gain_here = mine(key_gain)
    cot_here = cotangent.astype(floats)
    gathered = (
        lax.all_gather(query_weight, "row", axis=0, tiled=True),
        lax.all_gather(key_weight, "row", axis=0, tiled=True),
        lax.all_gather(value_weight, "row", axis=0, tiled=True),
        lax.all_gather(gate_weight, "row", axis=0, tiled=True),
        lax.all_gather(up_weight, "row", axis=0, tiled=True),
        lax.all_gather(output_weight, "row", axis=0, tiled=True),
        lax.all_gather(down_weight, "row", axis=0, tiled=True),
    )
    query_full, key_full, value_full, gate_full, up_full, output_full, down_full = gathered
    whole_in = lax.all_gather(inputs, "col", axis=1, tiled=True)
    query_raw = matmul(whole_in, query_full)
    key_raw = matmul(whole_in, key_full)
    value_raw = matmul(whole_in, value_full)
    query_total, key_total = lax.psum(
        (jnp.sum(query_raw * query_raw, axis=1), jnp.sum(key_raw * key_raw, axis=1)), "col"
    )
    query_scale = lax.rsqrt(query_total / width + EPS)[:, None]
    key_scale = lax.rsqrt(key_total / width + EPS)[:, None]
    query_hat = query_raw * query_scale
    key_hat = key_raw * key_scale
    cosine, sine = rope_tables(positions, head_size)
    query_low = (
        rotate((query_hat * query_gain_here).reshape(rows, heads_here, head_size), cosine, sine)
        * scale
    ).astype(bfloat)
    key_low = rotate(
        (key_hat * key_gain_here).reshape(rows, heads_here, head_size), cosine, sine
    ).astype(bfloat)
    value_low = value_raw.astype(bfloat).reshape(rows, heads_here, head_size)
    query_blocks = query_low.reshape(shape_seq)
    key_blocks = key_low.reshape(shape_seq)
    value_blocks = value_low.reshape(shape_seq)
    segment_blocks = segments.reshape(sequences, LENGTH)

    def attend(block):
        queries, keys_part, values_part, segment_part = block
        scores = jnp.einsum("qhd,khd->hqk", queries, keys_part, preferred_element_type=floats)
        scores = jnp.where(visible_pairs(segment_part)[None], scores, MASKED)
        largest = jnp.max(scores, axis=-1, keepdims=True)
        exponent = jnp.exp(scores - largest)
        totals = jnp.sum(exponent, axis=-1, keepdims=True)
        weights_low = (exponent / totals).astype(bfloat)
        attended_part = jnp.einsum(
            "hqk,khd->qhd", weights_low, values_part, preferred_element_type=floats
        )
        return (attended_part, (largest + jnp.log(totals))[..., 0])

    attended, log_totals = lax.map(attend, (query_blocks, key_blocks, value_blocks, segment_blocks))
    attended_low = attended.reshape(rows, local_width).astype(bfloat)
    branch = lax.psum(cross_cols(attended_low, output_full), "col")
    branch_scale = lax.rsqrt(jnp.mean(branch * branch, axis=1, keepdims=True) + EPS)
    branch_hat = branch * branch_scale
    middle = whole_in.astype(floats) + branch_hat * attn_gain
    middle_low = middle.astype(bfloat)
    middle_here = mine(middle)
    branch_hat_here = mine(branch_hat)
    gate_pre = matmul(middle_low, gate_full)
    up_pre = matmul(middle_low, up_full)
    sigma = jax.nn.sigmoid(gate_pre)
    silu_gate = gate_pre * sigma
    mixed_low = (silu_gate * up_pre).astype(bfloat)
    ffn = lax.psum(cross_cols(mixed_low, down_full), "col")
    ffn_scale = lax.rsqrt(jnp.mean(ffn * ffn, axis=1, keepdims=True) + EPS)
    ffn_hat = ffn * ffn_scale
    ffn_hat_here = mine(ffn_hat)
    grad_top = lax.all_gather(cotangent, "col", axis=1, tiled=True).astype(floats)
    normed_top = grad_top * mlp_gain
    inner_top = jnp.sum(normed_top * ffn_hat, axis=1, keepdims=True)
    grad_ffn_low = (ffn_scale * (normed_top - ffn_hat * inner_top / width)).astype(bfloat)
    layer_out = (middle_here + ffn_hat_here * mine(mlp_gain)).astype(bfloat)
    grad_mlp_gain = jnp.sum(cot_here * ffn_hat_here, axis=0)
    grad_down = cross_rows(grad_ffn_low, mixed_low)
    grad_mixed = matmul(grad_ffn_low, down_full)
    grad_gate_low = (grad_mixed * up_pre * sigma * (1.0 + gate_pre * (1.0 - sigma))).astype(bfloat)
    grad_up_low = (grad_mixed * silu_gate).astype(bfloat)
    grad_middle_part = cross_cols(grad_gate_low, gate_full) + cross_cols(grad_up_low, up_full)
    grad_gate = cross_rows(middle_low, grad_gate_low)
    grad_up = cross_rows(middle_low, grad_up_low)
    grad_middle = grad_top + lax.psum(grad_middle_part, "col")
    grad_middle_here = mine(grad_middle)
    grad_attn_gain = jnp.sum(grad_middle_here * branch_hat_here, axis=0)
    normed_mid = grad_middle * attn_gain
    inner_mid = jnp.sum(normed_mid * branch_hat, axis=1, keepdims=True)
    grad_branch_low = (branch_scale * (normed_mid - branch_hat * inner_mid / width)).astype(bfloat)
    grad_output = cross_rows(grad_branch_low, attended_low)
    grad_attended_low = matmul(grad_branch_low, output_full).astype(bfloat)

    def attend_back(block):
        queries, keys_part, values_part, segment_part, log_part, grad_part = block
        scores = jnp.einsum("qhd,khd->hqk", queries, keys_part, preferred_element_type=floats)
        scores = jnp.where(visible_pairs(segment_part)[None], scores, MASKED)
        probs = jnp.exp(scores - log_part[..., None])
        grad_values = jnp.einsum(
            "hqk,qhd->khd", probs.astype(bfloat), grad_part, preferred_element_type=floats
        )
        grad_probs = jnp.einsum(
            "qhd,khd->hqk", grad_part, values_part, preferred_element_type=floats
        )
        grad_scores = probs * (grad_probs - jnp.sum(probs * grad_probs, axis=-1, keepdims=True))
        scores_low = grad_scores.astype(bfloat)
        grad_queries = jnp.einsum(
            "hqk,khd->qhd", scores_low, keys_part, preferred_element_type=floats
        )
        grad_keys = jnp.einsum("hqk,qhd->khd", scores_low, queries, preferred_element_type=floats)
        return (grad_queries, grad_keys, grad_values.astype(bfloat))

    grad_queries, grad_keys, grad_values = lax.map(
        attend_back,
        (
            query_blocks,
            key_blocks,
            value_blocks,
            segment_blocks,
            log_totals,
            grad_attended_low.reshape(shape_seq),
        ),
    )
    grad_query_norm = rotate(
        grad_queries.reshape(rows, heads_here, head_size) * scale, cosine, -sine
    ).reshape(rows, local_width)
    grad_key_norm = rotate(grad_keys.reshape(rows, heads_here, head_size), cosine, -sine).reshape(
        rows, local_width
    )
    grad_query_gain = jnp.sum(grad_query_norm * query_hat, axis=0)
    grad_key_gain = jnp.sum(grad_key_norm * key_hat, axis=0)
    normed_query = grad_query_norm * query_gain_here
    normed_key = grad_key_norm * key_gain_here
    inner_query, inner_key = lax.psum(
        (jnp.sum(normed_query * query_hat, axis=1), jnp.sum(normed_key * key_hat, axis=1)), "col"
    )
    grad_query_low = (
        query_scale * (normed_query - query_hat * inner_query[:, None] / width)
    ).astype(bfloat)
    grad_key_low = (key_scale * (normed_key - key_hat * inner_key[:, None] / width)).astype(bfloat)
    grad_value_low = grad_values.reshape(rows, local_width)
    grad_in_part = (
        cross_cols(grad_query_low, query_full)
        + cross_cols(grad_key_low, key_full)
        + cross_cols(grad_value_low, value_full)
    )
    grad_inputs = grad_middle_here + lax.psum_scatter(
        grad_in_part, "col", scatter_dimension=1, tiled=True
    )
    grad_query = cross_rows(whole_in, grad_query_low)
    grad_key = cross_rows(whole_in, grad_key_low)
    grad_value = cross_rows(whole_in, grad_value_low)
    summed = (
        lax.psum_scatter(grad_query, "row", scatter_dimension=0, tiled=True),
        lax.psum_scatter(grad_key, "row", scatter_dimension=0, tiled=True),
        lax.psum_scatter(grad_value, "row", scatter_dimension=0, tiled=True),
        lax.psum_scatter(grad_output, "row", scatter_dimension=0, tiled=True),
        lax.psum_scatter(grad_gate, "row", scatter_dimension=0, tiled=True),
        lax.psum_scatter(grad_up, "row", scatter_dimension=0, tiled=True),
        lax.psum_scatter(grad_down, "row", scatter_dimension=0, tiled=True),
    )
    gains = lax.psum((grad_query_gain, grad_key_gain, grad_attn_gain, grad_mlp_gain), "row")
    return (
        layer_out,
        grad_inputs,
        summed[0],
        summed[1],
        summed[2],
        summed[3],
        summed[4],
        summed[5],
        summed[6],
        gains[0],
        gains[1],
        gains[2],
        gains[3],
    )


BF = jnp.bfloat16
F32 = jnp.float32
MESH_ID = pl.DeviceIdType.MESH
T = 512
DC = 256
DR = 512
D = 2048
FH = 512
HT = 256
LAYER_STAGES = 5
EXACT = lax.Precision.HIGHEST


def dot_nn(a, b):
    return jnp.dot(a, b, preferred_element_type=F32)


def dot_nt(a, b, precision=None):
    return lax.dot_general(
        a, b, (((1,), (1,)), ((), ())), precision=precision, preferred_element_type=F32
    )


def dot_tn(a, b, precision=None):
    return lax.dot_general(
        a, b, (((0,), (0,)), ((), ())), precision=precision, preferred_element_type=F32
    )


def aligned(start, size):
    return pl.ds(pl.multiple_of(start, size), size)


class Counter:
    def __init__(self):
        self.used = 0

    def take(self, count=1):
        first = self.used
        self.used += count
        return first


def block_kernel(
    x_hbm,
    wq_hbm,
    wk_hbm,
    wv_hbm,
    wo_hbm,
    wg_hbm,
    wu_hbm,
    wd_hbm,
    cot_hbm,
    query_gain_hbm,
    key_gain_hbm,
    attn_gain_hbm,
    mlp_gain_hbm,
    pos_hbm,
    layer_out,
    grad_in,
    gains_out,
    land_mlp,
    land_attn,
    wqkv,
    wo,
    wgu,
    wd,
    x_full,
    mid_full,
    gf_full,
    gb_full,
    gu_s,
    mixed_s,
    probs_s,
    hat_s,
    low_s,
    cos_s,
    sin_s,
    pos_s,
    cot_z,
    braw_s,
    raw_s,
    middle_s,
    bhat_s,
    work_s,
    inner_s,
    att_s,
    ga_s,
    gqkv_s,
    gs_s,
    gqk_s,
    own_s,
    stage_c,
    land_c,
    stage_y,
    land_y,
    stage_z,
    land_z,
    land_r,
    scal_s,
    gain_s,
    stage_down,
    stage_gu,
    rel_mlp,
    rel_attn,
    out_lo,
    query_gain_ref,
    key_gain_ref,
    attn_gain_ref,
    mlp_gain_ref,
    pos_ref,
    send_sem,
    recv_sem,
    local_sem,
):
    row = lax.axis_index("row")
    col = lax.axis_index("col")
    x_at = lax.rem(row, 2)
    y_at = lax.div(row, 2)
    core = lax.rem(col, 2)
    z_at = lax.div(col, 2)
    row_x = row + 1 - 2 * x_at
    row_y = lax.rem(row + 2, 4)
    row_d = row_y + 1 - 2 * x_at
    sib = col + 1 - 2 * core
    dev_x = (row_x, col)
    dev_y = (row_y, col)
    dev_d = (row_d, col)
    dev_c = (row, sib)
    z_pair = {
        0: z_at,
        1: z_at + 1 - 2 * lax.rem(z_at, 2),
        2: lax.rem(z_at + 2, 4),
        3: 3 - z_at,
    }
    middle = (z_at == 1) | (z_at == 2)
    at_end = (z_at == 0) | (z_at == 3)
    dev_z = {pair: (row, 2 * z_pair[pair] + core) for pair in (1, 2, 3)}

    counter = Counter()
    locals_used = Counter()
    pending = []

    def copy_of(index, src, dst, device, send_index=None):
        return pltpu.make_async_remote_copy(
            src_ref=src,
            dst_ref=dst,
            send_sem=send_sem.at[index if send_index is None else send_index],
            recv_sem=recv_sem.at[index],
            device_id=device,
            device_id_type=MESH_ID,
        )

    def send(index, src, dst, device, send_index=None, when=None):
        copy = copy_of(index, src, dst, device, send_index)
        if when is None:
            copy.start()
        else:
            pl.when(when)(copy.start)
        pending.append((copy, when))
        return copy, when

    def arrived(index, dst, when=None):
        copy = copy_of(index, dst, dst, dev_c)
        if when is None:
            copy.wait_recv()
        else:
            pl.when(when)(copy.wait_recv)

    def sent(started):
        copy, when = started
        if when is None:
            copy.wait_send()
        else:
            pl.when(when)(copy.wait_send)
        pending[:] = [other for other in pending if other[0] is not copy]

    def local(src, dst):
        copy = pltpu.make_async_copy(src, dst, local_sem.at[locals_used.take()])
        copy.start()
        return copy

    barrier = pltpu.get_barrier_semaphore()
    partners = [dev_x, dev_y, dev_d] + [(row, lax.rem(col + step, 8)) for step in range(1, 8)]
    for device in partners:
        pl.semaphore_signal(barrier, inc=1, device_id=device, device_id_type=MESH_ID)

    @pl.when(at_end)
    def _():
        land_r[...] = jnp.zeros_like(land_r)
        land_z[0] = jnp.zeros_like(land_z[0])

    small_copies = [
        local(query_gain_hbm, query_gain_ref),
        local(key_gain_hbm, key_gain_ref),
        local(attn_gain_hbm, attn_gain_ref),
        local(mlp_gain_hbm, mlp_gain_ref),
    ]
    pos_copy = local(pos_hbm, pos_ref)
    half_mine = aligned(y_at * FH, FH)
    half_other = aligned((1 - y_at) * FH, FH)
    rows_mine = aligned(row * DR, DR)
    local_copies = [local(x_hbm, x_full.at[:, aligned(col * DC, DC)]), local(cot_hbm, cot_z.at[z_at])]
    for index, ref in enumerate((wq_hbm, wk_hbm, wv_hbm)):
        local_copies.append(local(ref, wqkv.at[rows_mine, pl.ds(index * DC, DC)]))
    local_copies.append(local(wo_hbm, wo.at[rows_mine, :]))
    local_copies.append(local(wg_hbm.at[:, half_mine], wgu.at[rows_mine, pl.ds(0, FH)]))
    local_copies.append(local(wu_hbm.at[:, half_mine], wgu.at[rows_mine, pl.ds(FH, FH)]))
    local_copies.append(local(wd_hbm.at[:, half_mine], wd.at[rows_mine, :]))
    pl.semaphore_wait(barrier, len(partners))

    def own_rows(half, plane):
        if plane:
            return aligned(half * 2 * HT + y_at * HT, HT)
        return pl.ds(half * HT, HT)

    def other_rows(half):
        return aligned(half * 2 * HT + (1 - y_at) * HT, HT)

    def half_rows(half, plane):
        count = 2 * HT if plane else HT
        return pl.ds(half * count, count)

    def tokens(half):
        return pl.ds(half * HT, HT)

    gather_base = counter.take(2 * 16)
    gather_sends = ([], [])

    class Gather:
        def __init__(self, buf, plane, raw, process, half):
            self.buf = buf
            self.plane = plane
            self.raw = raw
            self.process = process
            self.half = half
            self.base_z = gather_base + 16 * half
            self.relay = self.base_z + 3
            self.base_c = self.base_z + 4
            self.base_y = self.base_z + 8
            self.base_cy = self.base_z + 12
            self.rows = own_rows(half, plane)
            if plane:
                self.rows_other = other_rows(half)

        def block(self, rows, place, parity=None):
            at = 2 * place + (core if parity is None else parity)
            return rows, aligned(at * DC, DC)

        def start(self):
            self.finish_sends()
            own = self.raw.at[z_at, tokens(self.half)]
            for pair in (2, 3, 1):
                when = middle if pair == 3 else None
                self.send(self.base_z + pair - 1, own, own, dev_z[pair], None, when)

        def send(self, *copy):
            gather_sends[self.half].append(send(*copy))

        def pass_on(self, *pairs):
            for pair in pairs:
                place = z_pair[pair]
                if pair:
                    raw = self.raw.at[place, tokens(self.half)]
                    arrived(self.base_z + pair - 1, raw)
                if pair == 2:
                    self.send(self.base_z + 2, raw, raw, dev_z[1], self.relay, middle)
                where = self.block(self.rows, place)
                self.buf[where] = self.process(pair, place, self.half)
                block = self.buf.at[where]
                if self.plane:
                    self.send(self.base_y + pair, block, block, dev_y)
                self.send(self.base_c + pair, block, block, dev_c)

        def finish_own(self):
            for pair in range(4):
                arrived(
                    self.base_c + pair, self.buf.at[self.block(self.rows, z_pair[pair], 1 - core)]
                )

        def finish_sends(self):
            for copy in gather_sends[self.half]:
                sent(copy)
            gather_sends[self.half].clear()

        def finish_other(self):
            for pair in range(4):
                block = self.buf.at[self.block(self.rows_other, z_pair[pair])]
                arrived(self.base_y + pair, block)
                self.send(self.base_cy + pair, block, block, dev_c)
            for pair in range(4):
                arrived(
                    self.base_cy + pair,
                    self.buf.at[self.block(self.rows_other, z_pair[pair], 1 - core)],
                )

    reduce_base = counter.take(2 * 12)
    stage_sends = ([], [])

    class Reduce:
        ORDER = (3, 1, 2, 0)

        def __init__(self, partial, plane, half):
            self.partial = partial
            self.plane = plane
            self.half = half
            self.base_c = reduce_base + 12 * half
            self.base_z = self.base_c + 4
            self.relay = self.base_c + 7
            self.base_y = self.base_c + 8
            self.left = half_rows(half, plane)
            self.all_rows = pl.ds(half * 2 * HT, 2 * HT if plane else HT)
            self.rows = own_rows(half, True) if plane else self.all_rows
            self.tokens = tokens(half)
            if plane:
                self.rows_other = other_rows(half)

        def start(self):
            for copy in stage_sends[self.half]:
                sent(copy)
            stage_sends[self.half].clear()
            rows = self.all_rows
            for slot, pair in enumerate(self.ORDER):
                target = z_pair[pair]
                start = pl.multiple_of((2 * target + 1 - core) * DC, DC)
                stage_c[slot, rows, :] = self.partial(self.left, start).astype(BF)
                self.send(
                    self.base_c + slot, stage_c.at[slot, rows, :], land_c.at[slot, rows, :], dev_c
                )
                start = pl.multiple_of((2 * target + core) * DC, DC)
                own_s[slot, rows, :] = self.partial(self.left, start)
                if slot:
                    self.cores(slot - 1)
            self.cores(3)

        def send(self, *copy):
            stage_sends[self.half].append(send(*copy))

        def cores(self, slot):
            arrived(self.base_c + slot, land_c.at[slot, self.all_rows, :])
            if self.plane:
                rows = self.rows_other
                stage_y[slot, self.tokens, :] = (
                    own_s[slot, rows, :] + land_c[slot, rows, :].astype(F32)
                ).astype(BF)
                self.send(
                    self.base_y + slot,
                    stage_y.at[slot, self.tokens],
                    land_y.at[slot, self.tokens],
                    dev_y,
                )
                rows = self.rows
                own_s[slot, rows, :] = own_s[slot, rows, :] + land_c[slot, rows, :].astype(F32)
            else:
                self.pass_on(slot, land_c.at[slot, self.rows, :])

        def pass_on(self, slot, landed):
            pair = self.ORDER[slot]
            total = own_s[slot, self.rows, :] + landed[...].astype(F32)
            if pair == 0:
                own_s[slot, self.rows, :] = total
                return
            if pair == 2:
                arrived(self.relay, land_r.at[self.tokens], middle)
                total = total + land_r[self.tokens, :].astype(F32)
            stage_z[slot, self.tokens, :] = total.astype(BF)
            stage, land = stage_z.at[slot, self.tokens], land_z.at[slot, self.tokens]
            if pair == 3:
                index = self.base_z + slot
                self.send(index, stage, land, dev_z[3], None, middle)
                self.send(self.relay, stage, land_r.at[self.tokens], dev_z[1], None, at_end)
            else:
                self.send(self.base_z + slot, stage, land, dev_z[pair])

        def planes(self, *slots):
            for slot in slots:
                landed = land_y.at[slot, self.tokens]
                arrived(self.base_y + slot, landed)
                self.pass_on(slot, landed)

        def finish(self):
            for slot in range(3):
                when = middle if self.ORDER[slot] == 3 else None
                arrived(self.base_z + slot, land_z.at[slot, self.tokens], when)
            total = own_s[3, self.rows, :]
            for slot in range(3):
                total = total + land_z[slot, self.tokens, :].astype(F32)
            return total

    pick = lax.broadcasted_iota(jnp.int32, (8, DC), 0)
    lane = lax.broadcasted_iota(jnp.int32, (8, DC), 1)
    first_row = (pick == 0).astype(F32)
    second_row = (pick == 1).astype(F32)
    spread = ((pick == 0) & (lane < 128)).astype(F32) + ((pick == 1) & (lane >= 128)).astype(F32)
    scal_base = counter.take(4 * 7)
    scal_sends = ([], [], [], [])

    def scal_send(stage, half, first, second=None):
        mine = dot_nt(first_row, first, EXACT)
        if second is not None:
            mine = mine + dot_nt(second_row, second, EXACT)
        place = scal_s.at[stage, half, col]
        place[...] = mine
        turn = 2 * half + stage % 2
        for copy in scal_sends[turn]:
            sent(copy)
        scal_sends[turn].clear()
        for step in range(1, 8):
            index = scal_base + 7 * turn + step - 1
            scal_sends[turn].append(send(index, place, place, (row, lax.rem(col + step, 8))))

    def scal_get(stage, half):
        for step in range(1, 8):
            index = scal_base + 7 * (2 * half + stage % 2) + step - 1
            arrived(index, scal_s.at[stage, half, lax.rem(col + 8 - step, 8)])
        total = scal_s[stage, half, 0]
        for index in range(1, 8):
            total = total + scal_s[stage, half, index]
        both = dot_tn(total, spread, EXACT)
        return both[:, :128], both[:, 128:]

    HALVES = (0, 1)

    def wide(values):
        return jnp.concatenate([values, values], axis=1)

    attn_base = counter.take(16)
    weight_sends = []
    attn_hbm = (wq_hbm, wk_hbm, wv_hbm, wo_hbm)

    def attn_place(index, owner, part=None):
        if part is None:
            rows = aligned(owner * DR, DR)
        else:
            rows = aligned(owner * DR + part * (DR // 2), DR // 2)
        if index < 3:
            return wqkv.at[rows, pl.ds(index * DC, DC)]
        return wo.at[rows, :]

    def weight_send(*copy):
        weight_sends.append(send(*copy))

    def attn_send(index):
        weight_send(attn_base + index, attn_hbm[index], attn_place(index, row), dev_x)
        weight_send(attn_base + 4 + index, attn_hbm[index], attn_place(index, row), dev_y)

    def attn_relay(index):
        arrived(attn_base + index, attn_place(index, row_x))
        part = attn_place(index, row_x, 0 if index < 2 else None)
        weight_send(attn_base + 8 + index, part, part, dev_y)
        arrived(attn_base + 4 + index, attn_place(index, row_y))
        if index < 2:
            part = attn_place(index, row_y, 1)
            weight_send(attn_base + 12 + index, part, part, dev_x)

    def attn_ready(index):
        arrived(attn_base + 8 + index, attn_place(index, row_d, 0 if index < 2 else None))
        if index < 2:
            arrived(attn_base + 12 + index, attn_place(index, row_d, 1))

    mlp_base = counter.take(9)
    mlp_hbm = (wg_hbm, wu_hbm, wd_hbm)

    def mlp_place(index, owner):
        rows = aligned(owner * DR, DR)
        if index < 2:
            return wgu.at[rows, pl.ds(index * FH, FH)]
        return wd.at[rows, :]

    def mlp_send(index):
        weight_send(mlp_base + index, mlp_hbm[index].at[:, half_mine], mlp_place(index, row), dev_x)
        weight_send(mlp_base + 3 + index, mlp_hbm[index].at[:, half_other], mlp_place(index, row), dev_y)

    def mlp_relay(index):
        place = mlp_place(index, row_y)
        arrived(mlp_base + 3 + index, place)
        weight_send(mlp_base + 6 + index, place, place, dev_x)

    def mlp_ready(index):
        arrived(mlp_base + index, mlp_place(index, row_x))
        arrived(mlp_base + 6 + index, mlp_place(index, row_d))

    for index in range(2):
        attn_send(index)

    x_base = counter.take(7)
    cot_base = counter.take(3)

    def x_block(place, parity):
        return x_full.at[:, aligned((2 * place + parity) * DC, DC)]

    for pair in (2, 3, 1):
        send(x_base + pair - 1, x_hbm, x_block(z_at, core), dev_z[pair])
    send(x_base + 3, x_hbm, x_block(z_at, core), dev_c)

    pos_copy.wait()
    position_rows = jnp.broadcast_to(pos_ref[...].astype(F32), (8, T))
    position = dot_tn(position_rows, first_row[:, :HD], EXACT)
    pos_s[...] = position.astype(jnp.int32)
    lane_at = lax.broadcasted_iota(jnp.int32, (1, HD), 1)
    within = lax.rem(lane_at, HD // 2).astype(F32)
    frequency = jnp.exp(within * (-2.0 * math.log(THETA) / HD))
    angles = position * frequency
    cos_s[...] = jnp.cos(angles)
    sine = jnp.sin(angles)
    sin_s[...] = jnp.where(lane_at < HD // 2, -sine, sine)

    for index in range(2):
        attn_relay(index)
    attn_send(2)
    attn_send(3)
    for pair in (2, 1, 3):
        block = x_block(z_pair[pair], core)
        arrived(x_base + pair - 1, block)
        send(x_base + 3 + pair, block, block, dev_c)
    for copy in local_copies + small_copies:
        copy.wait()
    for pair in range(4):
        arrived(x_base + 3 + pair, x_block(z_pair[pair], 1 - core))
    attn_ready(0)
    attn_ready(1)

    def gain_at(ref, at):
        return ref[:, aligned(at * DC, DC)]

    qk_gain = (gain_at(query_gain_ref, col), gain_at(key_gain_ref, col))
    for index in range(2):
        hat_s[index] = dot_nn(x_full[...], wqkv[:, pl.ds(index * DC, DC)])
    for half in HALVES:
        query, key = hat_s[0, tokens(half), :], hat_s[1, tokens(half), :]
        scal_send(0, half, query * query, key * key)
    attn_relay(2)
    attn_relay(3)
    for index in range(3):
        mlp_send(index)
    attn_ready(2)
    low_s[2] = dot_nn(x_full[...], wqkv[:, pl.ds(2 * DC, DC)]).astype(BF)
    for half in HALVES:
        scales = [lax.rsqrt(total / D + EPS) for total in scal_get(0, half)]
        rows = tokens(half)
        work_s[0, rows, :] = jnp.concatenate(scales, axis=1)
        for index in range(2):
            hat = hat_s[index, rows, :] * wide(scales[index])
            hat_s[index, rows, :] = hat
            normed = hat * qk_gain[index]
            for head in range(2):
                part = normed[:, head * HD : (head + 1) * HD]
                turned = part * cos_s[rows, :] + pltpu.roll(part, HD // 2, 1) * sin_s[rows, :]
                if index == 0:
                    turned = turned * (HD**-0.5)
                low_s[index, rows, pl.ds(head * HD, HD)] = turned.astype(BF)

    chunk = 128

    def attend(half):
        count = (half + 1) * HT
        keys = pl.ds(0, count)

        def attend_chunk(at, carry):
            rows = aligned(at * chunk, chunk)
            query = at * chunk + lax.broadcasted_iota(jnp.int32, (chunk, count), 0)
            key = lax.broadcasted_iota(jnp.int32, (chunk, count), 1)
            oldest = query - pos_s[rows, :1]
            allowed = (key <= query) & (key >= oldest)
            for head in range(2):
                lanes = pl.ds(head * HD, HD)
                scores = dot_nt(low_s[0, rows, lanes], low_s[1, keys, lanes])
                scores = jnp.where(allowed, scores, MASKED)
                exponent = jnp.exp(scores - jnp.max(scores, axis=1, keepdims=True))
                probs = exponent / jnp.sum(exponent, axis=1, keepdims=True)
                probs_s[head, rows, keys] = probs
                att_s[rows, lanes] = dot_nn(probs.astype(BF), low_s[2, keys, lanes]).astype(BF)
            return carry

        first = half * (HT // chunk)
        lax.fori_loop(first, first + HT // chunk, attend_chunk, 0)

    branch_sums = [
        Reduce(
            lambda rows, start: dot_nt(att_s[rows, :], wo[pl.ds(start, DC), :]), False, half
        )
        for half in HALVES
    ]

    def middle_block(pair, place, half):
        rows = tokens(half)
        at = 2 * place + core
        raw = work_s[1, rows, :] if pair == 0 else braw_s[place, rows, :].astype(F32)
        hat = raw * wide(work_s[2, rows, :128])
        inputs = x_full[rows, aligned(at * DC, DC)].astype(F32)
        middle = inputs + hat * gain_at(attn_gain_ref, at)
        if pair == 0:
            bhat_s[rows, :] = hat
            middle_s[rows, :] = middle
        return middle.astype(BF)

    mid_gathers = [Gather(mid_full, True, braw_s, middle_block, half) for half in HALVES]

    def branch_done(half):
        rows = tokens(half)
        branch = branch_sums[half].finish()
        scal_send(1, half, branch * branch)
        work_s[1, rows, :] = branch
        braw_s[z_at, rows, :] = branch.astype(BF)
        mid_gathers[half].start()

    def branch_scaled(half):
        total, _ = scal_get(1, half)
        work_s[2, tokens(half), :128] = lax.rsqrt(total / D + EPS)

    attend(0)
    attn_ready(3)
    branch_sums[0].start()
    attend(1)
    branch_sums[1].start()
    mlp_relay(0)
    branch_done(0)
    mlp_relay(1)
    branch_scaled(0)
    mid_gathers[0].pass_on(0)
    branch_done(1)
    mlp_relay(2)
    mid_gathers[0].pass_on(2, 1, 3)
    branch_scaled(1)
    mid_gathers[1].pass_on(0)
    mid_gathers[1].pass_on(2, 1, 3)
    for pair in (2, 3, 1):
        weight_send(cot_base + pair - 1, cot_z.at[z_at], cot_z.at[z_at], dev_z[pair])
    mid_gathers[0].finish_own()
    mid_gathers[0].finish_other()
    mlp_ready(0)
    mlp_ready(1)

    tile = 256

    def forward_tiles(half):
        rows = half_rows(half, True)

        def forward_tile(at, carry):
            lanes = aligned(at * tile, tile)
            lanes_up = aligned(at * tile + FH, tile)
            gate = dot_nn(mid_full[rows, :], wgu[:, lanes])
            up = dot_nn(mid_full[rows, :], wgu[:, lanes_up])
            gu_s[rows, lanes] = gate.astype(BF)
            gu_s[rows, lanes_up] = up.astype(BF)
            mixed_s[rows, lanes] = (gate * jax.nn.sigmoid(gate) * up).astype(BF)
            return carry

        lax.fori_loop(0, FH // tile, forward_tile, 0)

    ffn_sums = [
        Reduce(
            lambda rows, start: dot_nt(mixed_s[rows, :], wd[pl.ds(start, DC), :]), True, half
        )
        for half in HALVES
    ]
    mlp_gain = gain_at(mlp_gain_ref, col)

    def grad_ffn_block(pair, place, half):
        rows = tokens(half)
        at = 2 * place + core
        raw = work_s[1, rows, :] if pair == 0 else raw_s[place, rows, :].astype(F32)
        scale = wide(work_s[2, rows, 128:])
        grad = cot_z[place, rows, :].astype(F32) * gain_at(mlp_gain_ref, at)
        return (scale * (grad - raw * scale * wide(inner_s[rows, :]))).astype(BF)

    gf_gathers = [Gather(gf_full, True, raw_s, grad_ffn_block, half) for half in HALVES]

    def ffn_done(half):
        rows = tokens(half)
        ffn = ffn_sums[half].finish()
        cot = cot_z[z_at, rows, :].astype(F32)
        scal_send(2, half, ffn * ffn, cot * mlp_gain * ffn)
        work_s[1, rows, :] = ffn
        raw_s[z_at, rows, :] = ffn.astype(BF)
        gf_gathers[half].start()

    def ffn_scaled(half):
        rows = tokens(half)
        total, inner = scal_get(2, half)
        scale = lax.rsqrt(total / D + EPS)
        work_s[2, rows, 128:] = scale
        inner_s[rows, :] = inner * scale / D
        ffn_hat = work_s[1, rows, :] * wide(scale)
        out_lo[rows, :] = (middle_s[rows, :] + ffn_hat * mlp_gain).astype(BF)
        cot = cot_z[z_at, rows, :].astype(F32)
        return jnp.sum(cot * ffn_hat, axis=0, keepdims=True)

    forward_tiles(0)
    mlp_ready(2)
    ffn_sums[0].start()
    mid_gathers[1].finish_own()
    mid_gathers[1].finish_other()
    forward_tiles(1)
    ffn_sums[1].start()
    ffn_sums[0].planes(0, 1, 2, 3)
    ffn_sums[1].planes(0, 1)
    for pair in (1, 2, 3):
        arrived(cot_base + pair - 1, cot_z.at[z_pair[pair]])
    ffn_done(0)
    ffn_sums[1].planes(2, 3)
    mlp_gain_part = ffn_scaled(0)
    gf_gathers[0].pass_on(0)
    ffn_done(1)
    gf_gathers[0].pass_on(2, 1, 3)
    gain_s[row, 3:4, :] = mlp_gain_part + ffn_scaled(1)
    gf_gathers[1].pass_on(0, 2, 1, 3)
    lo_copy = local(out_lo, layer_out)
    gf_gathers[0].finish_own()
    gf_gathers[0].finish_other()

    def backward_tiles(half):
        rows = half_rows(half, True)

        def backward_tile(at, carry):
            lanes = aligned(at * tile, tile)
            lanes_up = aligned(at * tile + FH, tile)
            grad_mixed = dot_nn(gf_full[rows, :], wd[:, lanes])
            gate = gu_s[rows, lanes].astype(F32)
            up = gu_s[rows, lanes_up].astype(F32)
            sigma = jax.nn.sigmoid(gate)
            gu_s[rows, lanes] = (grad_mixed * up * sigma * (1.0 + gate * (1.0 - sigma))).astype(BF)
            gu_s[rows, lanes_up] = (grad_mixed * gate * sigma).astype(BF)
            return carry

        lax.fori_loop(0, FH // tile, backward_tile, 0)

    def lanes_of(owner):
        return aligned(owner * DR, DR)

    def down_piece(owner):
        return dot_tn(gf_full[:, lanes_of(owner)], mixed_s[...])

    def gu_piece(owner, part):
        return dot_tn(mid_full[:, lanes_of(owner)], gu_s[:, pl.ds(part * FH, FH)])

    grad_base = counter.take(9)
    grad_sends = {}

    def grad_lanes(part):
        return pl.ds(part * FH, FH)

    def grad_stage(slot, part):
        if part == 2:
            return stage_down.at[slot]
        return stage_gu.at[slot, :, grad_lanes(part)]

    def grad_piece(slot, part, more=None):
        owner = (row_d, row_x, row_y, row)[slot]
        total = down_piece(owner) if part == 2 else gu_piece(owner, part)
        if more is not None:
            total = total + more
        grad_stage(slot, part)[...] = total.astype(BF)

    def grad_send(slot, part, landing, device):
        index = grad_base + 3 * slot + part
        grad_sends[slot, part] = send(index, grad_stage(slot, part), landing, device)

    def grad_diagonal(part):
        grad_piece(0, part)
        grad_send(0, part, rel_mlp.at[:, grad_lanes(part)], dev_x)

    def grad_near(part):
        grad_piece(1, part)
        grad_send(1, part, land_mlp.at[1, :, grad_lanes(part)], dev_x)

    def grad_relay(part):
        arrived(grad_base + part, rel_mlp.at[:, grad_lanes(part)])
        grad_piece(2, part, rel_mlp[:, grad_lanes(part)].astype(F32))
        grad_send(2, part, land_mlp.at[2, :, grad_lanes(part)], dev_y)

    mid_sums = [
        Reduce(lambda rows, start: dot_nt(gu_s[rows, :], wgu[pl.ds(start, DC), :]), True, half)
        for half in HALVES
    ]
    attn_gain = gain_at(attn_gain_ref, col)

    def grad_branch_block(pair, place, half):
        rows = tokens(half)
        at = 2 * place + core
        scale = wide(work_s[2, rows, :128])
        raw = middle_s[rows, :] if pair == 0 else raw_s[place, rows, :].astype(F32)
        hat = bhat_s[rows, :] if pair == 0 else braw_s[place, rows, :].astype(F32) * scale
        inner = wide(inner_s[rows, :])
        return (scale * (raw * gain_at(attn_gain_ref, at) - hat * inner)).astype(BF)

    gb_gathers = [Gather(gb_full, False, raw_s, grad_branch_block, half) for half in HALVES]

    def mid_done(half):
        rows = tokens(half)
        grad_middle = cot_z[z_at, rows, :].astype(F32) + mid_sums[half].finish()
        scal_send(3, half, grad_middle * attn_gain * bhat_s[rows, :])
        middle_s[rows, :] = grad_middle
        raw_s[z_at, rows, :] = grad_middle.astype(BF)
        gb_gathers[half].start()

    def mid_scaled(half):
        inner, _ = scal_get(3, half)
        inner_s[tokens(half), :] = inner / D

    backward_tiles(0)
    gf_gathers[0].finish_sends()
    mid_sums[0].start()
    gf_gathers[1].finish_own()
    gf_gathers[1].finish_other()
    grad_diagonal(2)
    backward_tiles(1)
    gf_gathers[1].finish_sends()
    mid_sums[1].start()
    grad_diagonal(0)
    grad_diagonal(1)
    mid_sums[0].planes(0, 1, 2, 3)
    grad_relay(2)
    mid_sums[1].planes(0, 1)
    mid_done(0)
    mid_sums[1].planes(2, 3)
    grad_relay(0)
    grad_near(2)
    mid_scaled(0)
    gb_gathers[0].pass_on(0)
    mid_done(1)
    grad_relay(1)
    grad_near(0)
    gb_gathers[0].pass_on(2, 1, 3)
    mid_scaled(1)
    gb_gathers[1].pass_on(0)
    grad_near(1)
    late = []
    gb_gathers[1].pass_on(2, 1, 3)
    gain_s[row, 2:3, :] = jnp.sum(middle_s[...] * bhat_s[...], axis=0, keepdims=True)
    gb_gathers[0].finish_own()
    gb_gathers[1].finish_own()

    ga_s[...] = dot_nn(gb_full[...], wo[...]).astype(BF)

    whole = pl.ds(0, DR)
    upper = pl.ds(0, DR // 2)
    lower = pl.ds(DR // 2, DR // 2)
    BY_Y = ((whole, 2),)
    BY_BOTH = ((upper, 1), (lower, 2))
    neighbours = {1: dev_x, 2: dev_y}
    attn_grad_base = counter.take(3 * 6)

    class AttnGrad:
        def __init__(self, order, routes, left, right, start, size):
            self.base = attn_grad_base + 6 * order
            self.routes = routes
            self.left, self.right = left, right
            self.start_lane, self.size = start, size
            self.lanes = pl.ds(start, size)

        def at(self, slot, rows):
            rows = pl.ds(slot // 2 * DR + rows.start, rows.size)
            return gf_full.at[rows, pl.ds(slot % 2 * 4 * DC + self.start_lane, self.size)]

        def piece(self, slot):
            owner = (row_d, row_x, row_y, row)[slot]
            piece = dot_tn(self.left[:, lanes_of(owner)], self.right())
            self.at(slot, whole)[...] = piece.astype(BF)

        def diagonal(self):
            self.piece(0)
            for step, (rows, first) in enumerate(self.routes):
                landing = rel_attn.at[rows, self.lanes]
                send(self.base + step, self.at(0, rows), landing, neighbours[first])

        def near(self):
            self.piece(1)
            self.piece(2)
            for step, (rows, first) in enumerate(self.routes):
                landing = land_attn.at[first, rows, self.lanes]
                send(self.base + 2 + step, self.at(first, rows), landing, neighbours[first])

        def own(self):
            self.piece(3)
            late.append(local(self.at(3, whole), land_attn.at[0, :, self.lanes]))

        def relay(self):
            for step, (rows, first) in enumerate(self.routes):
                slot = 3 - first
                arrived(self.base + step, rel_attn.at[rows, self.lanes])
                stage = self.at(slot, rows)
                stage[...] = (
                    stage[...].astype(F32) + rel_attn[rows, self.lanes].astype(F32)
                ).astype(BF)
                landing = land_attn.at[slot, rows, self.lanes]
                send(self.base + 4 + step, stage, landing, neighbours[slot])

        def finish(self):
            for step, (rows, first) in enumerate(self.routes):
                arrived(self.base + 2 + step, land_attn.at[first, rows, self.lanes])
                arrived(self.base + 4 + step, land_attn.at[3 - first, rows, self.lanes])

    grad_piece(3, 2)
    late.append(local(stage_down.at[3], land_mlp.at[0, :, grad_lanes(2)]))
    for gather in gf_gathers:
        gather.finish_sends()
    o_grad = AttnGrad(0, BY_BOTH, gb_full, lambda: att_s[...], 3 * DC, DC)
    o_grad.diagonal()
    o_grad.near()

    def attend_back(half):
        count = (half + 1) * HT
        keys = pl.ds(0, count)

        def attend_back_chunk(at, carry):
            rows = aligned(at * chunk, chunk)
            for head in range(2):
                lanes = pl.ds(head * HD, HD)
                grad_probs = dot_nt(ga_s[rows, lanes], low_s[2, keys, lanes])
                probs = probs_s[head, rows, keys]
                inner = jnp.sum(probs * grad_probs, axis=1, keepdims=True)
                grad_scores = (probs * (grad_probs - inner)).astype(BF)
                gs_s[head, rows, keys] = grad_scores
                gqk_s[0, rows, lanes] = dot_nn(grad_scores, low_s[1, keys, lanes])
            return carry

        first = half * (HT // chunk)
        lax.fori_loop(first, first + HT // chunk, attend_back_chunk, 0)

    for half in HALVES:
        attend_back(half)
    early, last = pl.ds(0, HT), pl.ds(HT, HT)
    for head in range(2):
        lanes = pl.ds(head * HD, HD)
        gqk_s[1, early, lanes] = dot_tn(gs_s[head, :, early], low_s[0, :, lanes])
        gqk_s[1, last, lanes] = dot_tn(gs_s[head, last, last], low_s[0, last, lanes])
    inners = []
    for index in range(2):
        for head in range(2):
            lanes = pl.ds(head * HD, HD)
            part = gqk_s[index, :, lanes]
            turned = part * cos_s[...] - pltpu.roll(part, HD // 2, 1) * sin_s[...]
            if index == 0:
                turned = turned * (HD**-0.5)
            gqk_s[index, :, lanes] = turned
        weighted = gqk_s[index] * hat_s[index]
        gain_s[row, index : index + 1, :] = jnp.sum(weighted, axis=0, keepdims=True)
        inners.append(weighted * qk_gain[index])
    for half in HALVES:
        part = slice(half * HT, (half + 1) * HT)
        scal_send(4, half, inners[0][part], inners[1][part])
    gain_base = counter.take(3)
    for slot, device in enumerate((dev_x, dev_y, dev_d)):
        send(gain_base + slot, gain_s.at[row], gain_s.at[row], device)
    for head in range(2):
        lanes = pl.ds(head * HD, HD)
        out_lanes = pl.ds(2 * DC + head * HD, HD)
        gqkv_s[early, out_lanes] = dot_tn(
            probs_s[head, :, early].astype(BF), ga_s[:, lanes]
        ).astype(BF)
        gqkv_s[last, out_lanes] = dot_tn(
            probs_s[head, last, last].astype(BF), ga_s[last, lanes]
        ).astype(BF)
    v_grad = AttnGrad(1, BY_BOTH, x_full, lambda: gqkv_s[:, 2 * DC :], 2 * DC, DC)
    v_grad.diagonal()
    v_grad.near()
    for half in HALVES:
        rows = tokens(half)
        totals = scal_get(4, half)
        for index in range(2):
            scale = wide(work_s[0, rows, index * 128 : (index + 1) * 128])
            gqkv_s[rows, pl.ds(index * DC, DC)] = (
                scale
                * (
                    gqk_s[index, rows, :] * qk_gain[index]
                    - hat_s[index, rows, :] * wide(totals[index] / D)
                )
            ).astype(BF)
    in_sums = [
        Reduce(
            lambda rows, start: dot_nt(gqkv_s[rows, :], wqkv[pl.ds(start, DC), :]), False, half
        )
        for half in HALVES
    ]
    qk_grad = AttnGrad(2, BY_BOTH, x_full, lambda: gqkv_s[:, : 2 * DC], 0, 2 * DC)
    qk_grad.diagonal()
    in_sums[0].start()
    qk_grad.near()
    in_sums[1].start()
    o_grad.relay()
    v_grad.relay()
    qk_grad.relay()
    for grad in (o_grad, v_grad, qk_grad):
        grad.own()
    grad_piece(3, 0)
    grad_piece(3, 1)
    late.append(local(stage_gu.at[3], land_mlp.at[0, :, pl.ds(0, 2 * FH)]))
    for half in HALVES:
        rows = tokens(half)
        work_s[1, rows, :] = middle_s[rows, :] + in_sums[half].finish()
    late.append(local(work_s.at[1], grad_in))
    late.append(lo_copy)

    for slot, owner in enumerate((row_x, row_y, row_d)):
        arrived(gain_base + slot, gain_s.at[owner])
    gains_out[...] = gain_s[0] + gain_s[1] + gain_s[2] + gain_s[3]
    for slot in (1, 2):
        for part in range(3):
            arrived(grad_base + 3 * slot + part, land_mlp.at[slot, :, grad_lanes(part)])
    for grad in (o_grad, v_grad, qk_grad):
        grad.finish()
    for copy in late:
        copy.wait()
    for copy in list(pending):
        sent(copy)
    assert counter.used <= send_sem.shape[0], counter.used


def total_kernel(
    lo_ref, gin_ref, gains_ref, mlp_ref, attn_ref, lo_out, gin_out, *outs
):
    y_at = lax.div(lax.axis_index("row"), 2)
    lo_out[...] = lo_ref[...]
    gin_out[...] = gin_ref[...]
    attn = attn_ref[0].astype(F32) + attn_ref[1].astype(F32) + attn_ref[2].astype(F32)
    for index in range(4):
        outs[index][...] = attn[:, index * DC : (index + 1) * DC]
    mine = mlp_ref[0].astype(F32) + mlp_ref[1].astype(F32)
    other = mlp_ref[2].astype(F32)
    for index in range(3):
        lanes = slice(index * FH, (index + 1) * FH)
        outs[4 + index][:, aligned(y_at * FH, FH)] = mine[:, lanes]
        outs[4 + index][:, aligned((1 - y_at) * FH, FH)] = other[:, lanes]
    for index in range(4):
        outs[7 + index][...] = gains_ref[index : index + 1, :]


MIB = 1 << 20


def on_device_kernel(
    inputs,
    query_weight,
    key_weight,
    value_weight,
    output_weight,
    gate_weight,
    up_weight,
    down_weight,
    query_gain,
    key_gain,
    attn_gain,
    mlp_gain,
    positions,
    segments,
    cotangent,
):
    hbm = pl.BlockSpec(memory_space=pl.ANY)
    vmem = pl.BlockSpec(memory_space=pltpu.VMEM)
    sds = jax.ShapeDtypeStruct
    copies = 150
    landed = pl.pallas_call(
        block_kernel,
        out_shape=[
            sds((T, DC), BF),
            sds((T, DC), F32),
            sds((8, DC), F32),
            sds((3, DR, 3 * FH), BF),
            sds((3, DR, 4 * DC), BF),
        ],
        in_specs=[hbm] * 14,
        out_specs=[hbm, hbm, vmem, hbm, hbm],
        scratch_shapes=[
            pltpu.VMEM((D, 3 * DC), BF),
            pltpu.VMEM((D, DC), BF),
            pltpu.VMEM((D, 2 * FH), BF),
            pltpu.VMEM((D, FH), BF),
            pltpu.VMEM((T, D), BF),
            pltpu.VMEM((2 * T, D), BF),
            pltpu.VMEM((2 * T, D), BF),
            pltpu.VMEM((T, D), BF),
            pltpu.VMEM((2 * T, 2 * FH), BF),
            pltpu.VMEM((2 * T, FH), BF),
            pltpu.VMEM((2, T, T), F32),
            pltpu.VMEM((2, T, DC), F32),
            pltpu.VMEM((3, T, DC), BF),
            pltpu.VMEM((T, HD), F32),
            pltpu.VMEM((T, HD), F32),
            pltpu.VMEM((T, HD), jnp.int32),
            pltpu.VMEM((4, T, DC), BF),
            pltpu.VMEM((4, T, DC), BF),
            pltpu.VMEM((4, T, DC), BF),
            pltpu.VMEM((T, DC), F32),
            pltpu.VMEM((T, DC), F32),
            pltpu.VMEM((3, T, DC), F32),
            pltpu.VMEM((T, HD), F32),
            pltpu.VMEM((T, DC), BF),
            pltpu.VMEM((T, DC), BF),
            pltpu.VMEM((T, 3 * DC), BF),
            pltpu.VMEM((2, T, T), BF),
            pltpu.VMEM((2, T, DC), F32),
            pltpu.VMEM((4, 2 * T, DC), F32),
            pltpu.VMEM((4, 2 * T, DC), BF),
            pltpu.VMEM((4, 2 * T, DC), BF),
            pltpu.VMEM((4, T, DC), BF),
            pltpu.VMEM((4, T, DC), BF),
            pltpu.VMEM((3, T, DC), BF),
            pltpu.VMEM((3, T, DC), BF),
            pltpu.VMEM((T, DC), BF),
            pltpu.VMEM((LAYER_STAGES, 2, 8, 8, HT), F32),
            pltpu.VMEM((4, 8, DC), F32),
            pltpu.VMEM((4, DR, FH), BF),
            pltpu.VMEM((4, DR, 2 * FH), BF),
            pltpu.VMEM((DR, 3 * FH), BF),
            pltpu.VMEM((DR, 4 * DC), BF),
            pltpu.VMEM((T, DC), BF),
            pltpu.VMEM((1, D), F32),
            pltpu.VMEM((1, D), F32),
            pltpu.VMEM((1, D), F32),
            pltpu.VMEM((1, D), F32),
            pltpu.VMEM((1, T), jnp.int32),
            pltpu.SemaphoreType.DMA((copies,)),
            pltpu.SemaphoreType.DMA((copies,)),
            pltpu.SemaphoreType.DMA((24,)),
        ],
        compiler_params=pltpu.CompilerParams(
            collective_id=0, has_side_effects=True, vmem_limit_bytes=64 * MIB
        ),
        cost_estimate=pl.CostEstimate(
            flops=26_800_000_000, bytes_accessed=16_000_000, transcendentals=2_000_000
        ),
    )(
        inputs,
        query_weight,
        key_weight,
        value_weight,
        output_weight,
        gate_weight,
        up_weight,
        down_weight,
        cotangent,
        query_gain[None, :],
        key_gain[None, :],
        attn_gain[None, :],
        mlp_gain[None, :],
        positions[None, :],
    )
    step = 256

    def rows_of(width):
        return pl.BlockSpec((step, width), lambda at: (at, 0))

    gain_spec = pl.BlockSpec((1, DC), lambda at: (0, 0))
    results = pl.pallas_call(
        total_kernel,
        grid=(DR // step,),
        out_shape=[sds((T, DC), BF), sds((T, DC), F32)]
        + [sds((DR, DC), F32)] * 4
        + [sds((DR, 2 * FH), F32)] * 3
        + [sds((1, DC), F32)] * 4,
        in_specs=[
            rows_of(DC),
            rows_of(DC),
            pl.BlockSpec((8, DC), lambda at: (0, 0)),
            pl.BlockSpec((3, step, 3 * FH), lambda at: (0, at, 0)),
            pl.BlockSpec((3, step, 4 * DC), lambda at: (0, at, 0)),
        ],
        out_specs=[rows_of(DC)] * 6 + [rows_of(2 * FH)] * 3 + [gain_spec] * 4,
        compiler_params=pltpu.CompilerParams(vmem_limit_bytes=64 * MIB),
    )(*landed)
    return (*results[:9], *[gain[0] for gain in results[9:]])


def solution(mesh):
    in_specs = (
        P("row", "col"),
        P("row", "col"),
        P("row", "col"),
        P("row", "col"),
        P("row", "col"),
        P("row", "col"),
        P("row", "col"),
        P("row", "col"),
        P(),
        P(),
        P(),
        P(),
        P("row"),
        P("row"),
        P("row", "col"),
    )
    out_specs = (
        P("row", "col"),
        P("row", "col"),
        P("row", "col"),
        P("row", "col"),
        P("row", "col"),
        P("row", "col"),
        P("row", "col"),
        P("row", "col"),
        P("row", "col"),
        P("col"),
        P("col"),
        P("col"),
        P("col"),
    )
    sizes = (mesh.shape["row"], mesh.shape["col"])
    body = on_device_kernel if sizes == (4, 8) else on_device
    return jax.shard_map(
        body, mesh=mesh, in_specs=in_specs, out_specs=out_specs, check_vma=False
    )
```

```python
import math

import jax
import jax.numpy as jnp
from jax import lax
from jax.experimental import pallas as pl
from jax.experimental.pallas import tpu as pltpu
from jax.sharding import PartitionSpec as P

HD = 128
LENGTH = 512


EPS = 1e-06
THETA = 500000.0
MASKED = -1e30


def rope_tables(positions, head_size):
    halfway = head_size // 2
    frequency = jnp.exp(
        jnp.arange(halfway, dtype=jnp.float32) * (-2.0 * math.log(THETA) / head_size)
    )
    angles = positions.astype(jnp.float32)[:, None] * frequency[None, :]
    return (jnp.cos(angles)[:, None, :], jnp.sin(angles)[:, None, :])


def rotate(values, cosine, sine):
    halfway = values.shape[-1] // 2
    first_half = values[..., :halfway]
    second_half = values[..., halfway:]
    return jnp.concatenate(
        [first_half * cosine - second_half * sine, second_half * cosine + first_half * sine],
        axis=-1,
    )


def matmul(left, right):
    return jnp.dot(left, right, preferred_element_type=jnp.float32)


def cross_rows(left, right):
    return lax.dot_general(
        left, right, (((0,), (0,)), ((), ())), preferred_element_type=jnp.float32
    )


def cross_cols(left, right):
    return lax.dot_general(
        left, right, (((1,), (1,)), ((), ())), preferred_element_type=jnp.float32
    )


def visible_pairs(segment_part):
    places = jnp.arange(segment_part.shape[0])
    return (segment_part[:, None] == segment_part[None, :]) & (places[:, None] >= places[None, :])


def on_device(
    inputs,
    query_weight,
    key_weight,
    value_weight,
    output_weight,
    gate_weight,
    up_weight,
    down_weight,
    query_gain,
    key_gain,
    attn_gain,
    mlp_gain,
    positions,
    segments,
    cotangent,
):
    bfloat = jnp.bfloat16
    floats = jnp.float32
    rows = inputs.shape[0]
    local_width = inputs.shape[1]
    width = local_width * lax.axis_size("col")
    offset = lax.axis_index("col") * local_width
    head_size = HD
    heads_here = local_width // head_size
    sequences = rows // LENGTH
    scale = head_size ** (-0.5)
    shape_seq = (sequences, LENGTH, heads_here, head_size)

    def mine(values):
        return lax.dynamic_slice_in_dim(values, offset, local_width, values.ndim - 1)

    query_gain_here = mine(query_gain)
    key_gain_here = mine(key_gain)
    cot_here = cotangent.astype(floats)
    gathered = (
        lax.all_gather(query_weight, "row", axis=0, tiled=True),
        lax.all_gather(key_weight, "row", axis=0, tiled=True),
        lax.all_gather(value_weight, "row", axis=0, tiled=True),
        lax.all_gather(gate_weight, "row", axis=0, tiled=True),
        lax.all_gather(up_weight, "row", axis=0, tiled=True),
        lax.all_gather(output_weight, "row", axis=0, tiled=True),
        lax.all_gather(down_weight, "row", axis=0, tiled=True),
    )
    query_full, key_full, value_full, gate_full, up_full, output_full, down_full = gathered
    whole_in = lax.all_gather(inputs, "col", axis=1, tiled=True)
    query_raw = matmul(whole_in, query_full)
    key_raw = matmul(whole_in, key_full)
    value_raw = matmul(whole_in, value_full)
    query_total, key_total = lax.psum(
        (jnp.sum(query_raw * query_raw, axis=1), jnp.sum(key_raw * key_raw, axis=1)), "col"
    )
    query_scale = lax.rsqrt(query_total / width + EPS)[:, None]
    key_scale = lax.rsqrt(key_total / width + EPS)[:, None]
    query_hat = query_raw * query_scale
    key_hat = key_raw * key_scale
    cosine, sine = rope_tables(positions, head_size)
    query_low = (
        rotate((query_hat * query_gain_here).reshape(rows, heads_here, head_size), cosine, sine)
        * scale
    ).astype(bfloat)
    key_low = rotate(
        (key_hat * key_gain_here).reshape(rows, heads_here, head_size), cosine, sine
    ).astype(bfloat)
    value_low = value_raw.astype(bfloat).reshape(rows, heads_here, head_size)
    query_blocks = query_low.reshape(shape_seq)
    key_blocks = key_low.reshape(shape_seq)
    value_blocks = value_low.reshape(shape_seq)
    segment_blocks = segments.reshape(sequences, LENGTH)

    def attend(block):
        queries, keys_part, values_part, segment_part = block
        scores = jnp.einsum("qhd,khd->hqk", queries, keys_part, preferred_element_type=floats)
        scores = jnp.where(visible_pairs(segment_part)[None], scores, MASKED)
        largest = jnp.max(scores, axis=-1, keepdims=True)
        exponent = jnp.exp(scores - largest)
        totals = jnp.sum(exponent, axis=-1, keepdims=True)
        weights_low = (exponent / totals).astype(bfloat)
        attended_part = jnp.einsum(
            "hqk,khd->qhd", weights_low, values_part, preferred_element_type=floats
        )
        return (attended_part, (largest + jnp.log(totals))[..., 0])

    attended, log_totals = lax.map(attend, (query_blocks, key_blocks, value_blocks, segment_blocks))
    attended_low = attended.reshape(rows, local_width).astype(bfloat)
    branch = lax.psum(cross_cols(attended_low, output_full), "col")
    branch_scale = lax.rsqrt(jnp.mean(branch * branch, axis=1, keepdims=True) + EPS)
    branch_hat = branch * branch_scale
    middle = whole_in.astype(floats) + branch_hat * attn_gain
    middle_low = middle.astype(bfloat)
    middle_here = mine(middle)
    branch_hat_here = mine(branch_hat)
    gate_pre = matmul(middle_low, gate_full)
    up_pre = matmul(middle_low, up_full)
    sigma = jax.nn.sigmoid(gate_pre)
    silu_gate = gate_pre * sigma
    mixed_low = (silu_gate * up_pre).astype(bfloat)
    ffn = lax.psum(cross_cols(mixed_low, down_full), "col")
    ffn_scale = lax.rsqrt(jnp.mean(ffn * ffn, axis=1, keepdims=True) + EPS)
    ffn_hat = ffn * ffn_scale
    ffn_hat_here = mine(ffn_hat)
    grad_top = lax.all_gather(cotangent, "col", axis=1, tiled=True).astype(floats)
    normed_top = grad_top * mlp_gain
    inner_top = jnp.sum(normed_top * ffn_hat, axis=1, keepdims=True)
    grad_ffn_low = (ffn_scale * (normed_top - ffn_hat * inner_top / width)).astype(bfloat)
    layer_out = (middle_here + ffn_hat_here * mine(mlp_gain)).astype(bfloat)
    grad_mlp_gain = jnp.sum(cot_here * ffn_hat_here, axis=0)
    grad_down = cross_rows(grad_ffn_low, mixed_low)
    grad_mixed = matmul(grad_ffn_low, down_full)
    grad_gate_low = (grad_mixed * up_pre * sigma * (1.0 + gate_pre * (1.0 - sigma))).astype(bfloat)
    grad_up_low = (grad_mixed * silu_gate).astype(bfloat)
    grad_middle_part = cross_cols(grad_gate_low, gate_full) + cross_cols(grad_up_low, up_full)
    grad_gate = cross_rows(middle_low, grad_gate_low)
    grad_up = cross_rows(middle_low, grad_up_low)
    grad_middle = grad_top + lax.psum(grad_middle_part, "col")
    grad_middle_here = mine(grad_middle)
    grad_attn_gain = jnp.sum(grad_middle_here * branch_hat_here, axis=0)
    normed_mid = grad_middle * attn_gain
    inner_mid = jnp.sum(normed_mid * branch_hat, axis=1, keepdims=True)
    grad_branch_low = (branch_scale * (normed_mid - branch_hat * inner_mid / width)).astype(bfloat)
    grad_output = cross_rows(grad_branch_low, attended_low)
    grad_attended_low = matmul(grad_branch_low, output_full).astype(bfloat)

    def attend_back(block):
        queries, keys_part, values_part, segment_part, log_part, grad_part = block
        scores = jnp.einsum("qhd,khd->hqk", queries, keys_part, preferred_element_type=floats)
        scores = jnp.where(visible_pairs(segment_part)[None], scores, MASKED)
        probs = jnp.exp(scores - log_part[..., None])
        grad_values = jnp.einsum(
            "hqk,qhd->khd", probs.astype(bfloat), grad_part, preferred_element_type=floats
        )
        grad_probs = jnp.einsum(
            "qhd,khd->hqk", grad_part, values_part, preferred_element_type=floats
        )
        grad_scores = probs * (grad_probs - jnp.sum(probs * grad_probs, axis=-1, keepdims=True))
        scores_low = grad_scores.astype(bfloat)
        grad_queries = jnp.einsum(
            "hqk,khd->qhd", scores_low, keys_part, preferred_element_type=floats
        )
        grad_keys = jnp.einsum("hqk,qhd->khd", scores_low, queries, preferred_element_type=floats)
        return (grad_queries, grad_keys, grad_values.astype(bfloat))

    grad_queries, grad_keys, grad_values = lax.map(
        attend_back,
        (
            query_blocks,
            key_blocks,
            value_blocks,
            segment_blocks,
            log_totals,
            grad_attended_low.reshape(shape_seq),
        ),
    )
    grad_query_norm = rotate(
        grad_queries.reshape(rows, heads_here, head_size) * scale, cosine, -sine
    ).reshape(rows, local_width)
    grad_key_norm = rotate(grad_keys.reshape(rows, heads_here, head_size), cosine, -sine).reshape(
        rows, local_width
    )
    grad_query_gain = jnp.sum(grad_query_norm * query_hat, axis=0)
    grad_key_gain = jnp.sum(grad_key_norm * key_hat, axis=0)
    normed_query = grad_query_norm * query_gain_here
    normed_key = grad_key_norm * key_gain_here
    inner_query, inner_key = lax.psum(
        (jnp.sum(normed_query * query_hat, axis=1), jnp.sum(normed_key * key_hat, axis=1)), "col"
    )
    grad_query_low = (
        query_scale * (normed_query - query_hat * inner_query[:, None] / width)
    ).astype(bfloat)
    grad_key_low = (key_scale * (normed_key - key_hat * inner_key[:, None] / width)).astype(bfloat)
    grad_value_low = grad_values.reshape(rows, local_width)
    grad_in_part = (
        cross_cols(grad_query_low, query_full)
        + cross_cols(grad_key_low, key_full)
        + cross_cols(grad_value_low, value_full)
    )
    grad_inputs = grad_middle_here + lax.psum_scatter(
        grad_in_part, "col", scatter_dimension=1, tiled=True
    )
    grad_query = cross_rows(whole_in, grad_query_low)
    grad_key = cross_rows(whole_in, grad_key_low)
    grad_value = cross_rows(whole_in, grad_value_low)
    summed = (
        lax.psum_scatter(grad_query, "row", scatter_dimension=0, tiled=True),
        lax.psum_scatter(grad_key, "row", scatter_dimension=0, tiled=True),
        lax.psum_scatter(grad_value, "row", scatter_dimension=0, tiled=True),
        lax.psum_scatter(grad_output, "row", scatter_dimension=0, tiled=True),
        lax.psum_scatter(grad_gate, "row", scatter_dimension=0, tiled=True),
        lax.psum_scatter(grad_up, "row", scatter_dimension=0, tiled=True),
        lax.psum_scatter(grad_down, "row", scatter_dimension=0, tiled=True),
    )
    gains = lax.psum((grad_query_gain, grad_key_gain, grad_attn_gain, grad_mlp_gain), "row")
    return (
        layer_out,
        grad_inputs,
        summed[0],
        summed[1],
        summed[2],
        summed[3],
        summed[4],
        summed[5],
        summed[6],
        gains[0],
        gains[1],
        gains[2],
        gains[3],
    )


BF = jnp.bfloat16
F32 = jnp.float32
MESH_ID = pl.DeviceIdType.MESH
T = 512
DC = 256
DR = 512
D = 2048
FH = 512
HT = 256
LAYER_STAGES = 5
EXACT = lax.Precision.HIGHEST


def dot_nn(a, b):
    return jnp.dot(a, b, preferred_element_type=F32)


def dot_nt(a, b, precision=None):
    return lax.dot_general(
        a, b, (((1,), (1,)), ((), ())), precision=precision, preferred_element_type=F32
    )


def dot_tn(a, b, precision=None):
    return lax.dot_general(
        a, b, (((0,), (0,)), ((), ())), precision=precision, preferred_element_type=F32
    )


def aligned(start, size):
    return pl.ds(pl.multiple_of(start, size), size)


class Counter:
    def __init__(self):
        self.used = 0

    def take(self, count=1):
        first = self.used
        self.used += count
        return first


def block_kernel(
    x_hbm,
    wq_hbm,
    wk_hbm,
    wv_hbm,
    wo_hbm,
    wg_hbm,
    wu_hbm,
    wd_hbm,
    cot_hbm,
    query_gain_hbm,
    key_gain_hbm,
    attn_gain_hbm,
    mlp_gain_hbm,
    pos_hbm,
    layer_out,
    grad_in,
    gains_out,
    land_mlp,
    land_attn,
    wqkv,
    wo,
    wgu,
    wd,
    x_full,
    mid_full,
    gf_full,
    gb_full,
    gu_s,
    mixed_s,
    probs_s,
    hat_s,
    low_s,
    cos_s,
    sin_s,
    pos_s,
    cot_z,
    braw_s,
    raw_s,
    middle_s,
    bhat_s,
    work_s,
    inner_s,
    att_s,
    ga_s,
    gqkv_s,
    gs_s,
    gqk_s,
    own_s,
    stage_c,
    land_c,
    stage_y,
    land_y,
    stage_z,
    land_z,
    land_r,
    scal_s,
    gain_s,
    stage_down,
    stage_gu,
    rel_mlp,
    rel_attn,
    out_lo,
    query_gain_ref,
    key_gain_ref,
    attn_gain_ref,
    mlp_gain_ref,
    pos_ref,
    send_sem,
    recv_sem,
    local_sem,
):
    row = lax.axis_index("row")
    col = lax.axis_index("col")
    x_at = lax.rem(row, 2)
    y_at = lax.div(row, 2)
    core = lax.rem(col, 2)
    z_at = lax.div(col, 2)
    row_x = row + 1 - 2 * x_at
    row_y = lax.rem(row + 2, 4)
    row_d = row_y + 1 - 2 * x_at
    sib = col + 1 - 2 * core
    dev_x = (row_x, col)
    dev_y = (row_y, col)
    dev_d = (row_d, col)
    dev_c = (row, sib)
    z_pair = {
        0: z_at,
        1: z_at + 1 - 2 * lax.rem(z_at, 2),
        2: lax.rem(z_at + 2, 4),
        3: 3 - z_at,
    }
    middle = (z_at == 1) | (z_at == 2)
    at_end = (z_at == 0) | (z_at == 3)
    dev_z = {pair: (row, 2 * z_pair[pair] + core) for pair in (1, 2, 3)}

    counter = Counter()
    locals_used = Counter()
    pending = []

    def copy_of(index, src, dst, device, send_index=None):
        return pltpu.make_async_remote_copy(
            src_ref=src,
            dst_ref=dst,
            send_sem=send_sem.at[index if send_index is None else send_index],
            recv_sem=recv_sem.at[index],
            device_id=device,
            device_id_type=MESH_ID,
        )

    def send(index, src, dst, device, send_index=None, when=None):
        copy = copy_of(index, src, dst, device, send_index)
        if when is None:
            copy.start()
        else:
            pl.when(when)(copy.start)
        pending.append((copy, when))
        return copy, when

    def arrived(index, dst, when=None):
        copy = copy_of(index, dst, dst, dev_c)
        if when is None:
            copy.wait_recv()
        else:
            pl.when(when)(copy.wait_recv)

    def sent(started):
        copy, when = started
        if when is None:
            copy.wait_send()
        else:
            pl.when(when)(copy.wait_send)
        pending[:] = [other for other in pending if other[0] is not copy]

    def local(src, dst):
        copy = pltpu.make_async_copy(src, dst, local_sem.at[locals_used.take()])
        copy.start()
        return copy

    barrier = pltpu.get_barrier_semaphore()
    partners = [dev_x, dev_y, dev_d] + [(row, lax.rem(col + step, 8)) for step in range(1, 8)]
    for device in partners:
        pl.semaphore_signal(barrier, inc=1, device_id=device, device_id_type=MESH_ID)

    @pl.when(at_end)
    def _():
        land_r[...] = jnp.zeros_like(land_r)
        land_z[0] = jnp.zeros_like(land_z[0])

    small_copies = [
        local(query_gain_hbm, query_gain_ref),
        local(key_gain_hbm, key_gain_ref),
        local(attn_gain_hbm, attn_gain_ref),
        local(mlp_gain_hbm, mlp_gain_ref),
    ]
    pos_copy = local(pos_hbm, pos_ref)
    half_mine = aligned(y_at * FH, FH)
    half_other = aligned((1 - y_at) * FH, FH)
    rows_mine = aligned(row * DR, DR)
    local_copies = [local(x_hbm, x_full.at[:, aligned(col * DC, DC)]), local(cot_hbm, cot_z.at[z_at])]
    for index, ref in enumerate((wq_hbm, wk_hbm, wv_hbm)):
        local_copies.append(local(ref, wqkv.at[rows_mine, pl.ds(index * DC, DC)]))
    local_copies.append(local(wo_hbm, wo.at[rows_mine, :]))
    local_copies.append(local(wg_hbm.at[:, half_mine], wgu.at[rows_mine, pl.ds(0, FH)]))
    local_copies.append(local(wu_hbm.at[:, half_mine], wgu.at[rows_mine, pl.ds(FH, FH)]))
    local_copies.append(local(wd_hbm.at[:, half_mine], wd.at[rows_mine, :]))
    pl.semaphore_wait(barrier, len(partners))

    def own_rows(half, plane):
        if plane:
            return aligned(half * 2 * HT + y_at * HT, HT)
        return pl.ds(half * HT, HT)

    def other_rows(half):
        return aligned(half * 2 * HT + (1 - y_at) * HT, HT)

    def half_rows(half, plane):
        count = 2 * HT if plane else HT
        return pl.ds(half * count, count)

    def tokens(half):
        return pl.ds(half * HT, HT)

    gather_base = counter.take(2 * 16)
    gather_sends = ([], [])

    class Gather:
        def __init__(self, buf, plane, raw, process, half):
            self.buf = buf
            self.plane = plane
            self.raw = raw
            self.process = process
            self.half = half
            self.base_z = gather_base + 16 * half
            self.relay = self.base_z + 3
            self.base_c = self.base_z + 4
            self.base_y = self.base_z + 8
            self.base_cy = self.base_z + 12
            self.rows = own_rows(half, plane)
            if plane:
                self.rows_other = other_rows(half)

        def block(self, rows, place, parity=None):
            at = 2 * place + (core if parity is None else parity)
            return rows, aligned(at * DC, DC)

        def start(self):
            self.finish_sends()
            own = self.raw.at[z_at, tokens(self.half)]
            for pair in (2, 3, 1):
                when = middle if pair == 3 else None
                self.send(self.base_z + pair - 1, own, own, dev_z[pair], None, when)

        def send(self, *copy):
            gather_sends[self.half].append(send(*copy))

        def pass_on(self, *pairs):
            for pair in pairs:
                place = z_pair[pair]
                if pair:
                    raw = self.raw.at[place, tokens(self.half)]
                    arrived(self.base_z + pair - 1, raw)
                if pair == 2:
                    self.send(self.base_z + 2, raw, raw, dev_z[1], self.relay, middle)
                where = self.block(self.rows, place)
                self.buf[where] = self.process(pair, place, self.half)
                block = self.buf.at[where]
                if self.plane:
                    self.send(self.base_y + pair, block, block, dev_y)
                self.send(self.base_c + pair, block, block, dev_c)

        def finish_own(self):
            for pair in range(4):
                arrived(
                    self.base_c + pair, self.buf.at[self.block(self.rows, z_pair[pair], 1 - core)]
                )

        def finish_sends(self):
            for copy in gather_sends[self.half]:
                sent(copy)
            gather_sends[self.half].clear()

        def finish_other(self):
            for pair in range(4):
                block = self.buf.at[self.block(self.rows_other, z_pair[pair])]
                arrived(self.base_y + pair, block)
                self.send(self.base_cy + pair, block, block, dev_c)
            for pair in range(4):
                arrived(
                    self.base_cy + pair,
                    self.buf.at[self.block(self.rows_other, z_pair[pair], 1 - core)],
                )

    reduce_base = counter.take(2 * 12)
    stage_sends = ([], [])

    class Reduce:
        ORDER = (3, 1, 2, 0)

        def __init__(self, partial, plane, half):
            self.partial = partial
            self.plane = plane
            self.half = half
            self.base_c = reduce_base + 12 * half
            self.base_z = self.base_c + 4
            self.relay = self.base_c + 7
            self.base_y = self.base_c + 8
            self.left = half_rows(half, plane)
            self.all_rows = pl.ds(half * 2 * HT, 2 * HT if plane else HT)
            self.rows = own_rows(half, True) if plane else self.all_rows
            self.tokens = tokens(half)
            if plane:
                self.rows_other = other_rows(half)

        def start(self):
            for copy in stage_sends[self.half]:
                sent(copy)
            stage_sends[self.half].clear()
            rows = self.all_rows
            for slot, pair in enumerate(self.ORDER):
                target = z_pair[pair]
                start = pl.multiple_of((2 * target + 1 - core) * DC, DC)
                stage_c[slot, rows, :] = self.partial(self.left, start).astype(BF)
                self.send(
                    self.base_c + slot, stage_c.at[slot, rows, :], land_c.at[slot, rows, :], dev_c
                )
                start = pl.multiple_of((2 * target + core) * DC, DC)
                own_s[slot, rows, :] = self.partial(self.left, start)
                if slot:
                    self.cores(slot - 1)
            self.cores(3)

        def send(self, *copy):
            stage_sends[self.half].append(send(*copy))

        def cores(self, slot):
            arrived(self.base_c + slot, land_c.at[slot, self.all_rows, :])
            if self.plane:
                rows = self.rows_other
                stage_y[slot, self.tokens, :] = (
                    own_s[slot, rows, :] + land_c[slot, rows, :].astype(F32)
                ).astype(BF)
                self.send(
                    self.base_y + slot,
                    stage_y.at[slot, self.tokens],
                    land_y.at[slot, self.tokens],
                    dev_y,
                )
                rows = self.rows
                own_s[slot, rows, :] = own_s[slot, rows, :] + land_c[slot, rows, :].astype(F32)
            else:
                self.pass_on(slot, land_c.at[slot, self.rows, :])

        def pass_on(self, slot, landed):
            pair = self.ORDER[slot]
            total = own_s[slot, self.rows, :] + landed[...].astype(F32)
            if pair == 0:
                own_s[slot, self.rows, :] = total
                return
            if pair == 2:
                arrived(self.relay, land_r.at[self.tokens], middle)
                total = total + land_r[self.tokens, :].astype(F32)
            stage_z[slot, self.tokens, :] = total.astype(BF)
            stage, land = stage_z.at[slot, self.tokens], land_z.at[slot, self.tokens]
            if pair == 3:
                index = self.base_z + slot
                self.send(index, stage, land, dev_z[3], None, middle)
                self.send(self.relay, stage, land_r.at[self.tokens], dev_z[1], None, at_end)
            else:
                self.send(self.base_z + slot, stage, land, dev_z[pair])

        def planes(self, *slots):
            for slot in slots:
                landed = land_y.at[slot, self.tokens]
                arrived(self.base_y + slot, landed)
                self.pass_on(slot, landed)

        def finish(self):
            for slot in range(3):
                when = middle if self.ORDER[slot] == 3 else None
                arrived(self.base_z + slot, land_z.at[slot, self.tokens], when)
            total = own_s[3, self.rows, :]
            for slot in range(3):
                total = total + land_z[slot, self.tokens, :].astype(F32)
            return total

    pick = lax.broadcasted_iota(jnp.int32, (8, DC), 0)
    lane = lax.broadcasted_iota(jnp.int32, (8, DC), 1)
    first_row = (pick == 0).astype(F32)
    second_row = (pick == 1).astype(F32)
    spread = ((pick == 0) & (lane < 128)).astype(F32) + ((pick == 1) & (lane >= 128)).astype(F32)
    scal_base = counter.take(4 * 7)
    scal_sends = ([], [], [], [])

    def scal_send(stage, half, first, second=None):
        mine = dot_nt(first_row, first, EXACT)
        if second is not None:
            mine = mine + dot_nt(second_row, second, EXACT)
        place = scal_s.at[stage, half, col]
        place[...] = mine
        turn = 2 * half + stage % 2
        for copy in scal_sends[turn]:
            sent(copy)
        scal_sends[turn].clear()
        for step in range(1, 8):
            index = scal_base + 7 * turn + step - 1
            scal_sends[turn].append(send(index, place, place, (row, lax.rem(col + step, 8))))

    def scal_get(stage, half):
        for step in range(1, 8):
            index = scal_base + 7 * (2 * half + stage % 2) + step - 1
            arrived(index, scal_s.at[stage, half, lax.rem(col + 8 - step, 8)])
        total = scal_s[stage, half, 0]
        for index in range(1, 8):
            total = total + scal_s[stage, half, index]
        both = dot_tn(total, spread, EXACT)
        return both[:, :128], both[:, 128:]

    HALVES = (0, 1)

    def wide(values):
        return jnp.concatenate([values, values], axis=1)

    attn_base = counter.take(16)
    weight_sends = []
    attn_hbm = (wq_hbm, wk_hbm, wv_hbm, wo_hbm)

    def attn_place(index, owner, part=None):
        if part is None:
            rows = aligned(owner * DR, DR)
        else:
            rows = aligned(owner * DR + part * (DR // 2), DR // 2)
        if index < 3:
            return wqkv.at[rows, pl.ds(index * DC, DC)]
        return wo.at[rows, :]

    def weight_send(*copy):
        weight_sends.append(send(*copy))

    def attn_send(index):
        weight_send(attn_base + index, attn_hbm[index], attn_place(index, row), dev_x)
        weight_send(attn_base + 4 + index, attn_hbm[index], attn_place(index, row), dev_y)

    def attn_relay(index):
        arrived(attn_base + index, attn_place(index, row_x))
        part = attn_place(index, row_x, 0 if index < 2 else None)
        weight_send(attn_base + 8 + index, part, part, dev_y)
        arrived(attn_base + 4 + index, attn_place(index, row_y))
        if index < 2:
            part = attn_place(index, row_y, 1)
            weight_send(attn_base + 12 + index, part, part, dev_x)

    def attn_ready(index):
        arrived(attn_base + 8 + index, attn_place(index, row_d, 0 if index < 2 else None))
        if index < 2:
            arrived(attn_base + 12 + index, attn_place(index, row_d, 1))

    mlp_base = counter.take(9)
    mlp_hbm = (wg_hbm, wu_hbm, wd_hbm)

    def mlp_place(index, owner):
        rows = aligned(owner * DR, DR)
        if index < 2:
            return wgu.at[rows, pl.ds(index * FH, FH)]
        return wd.at[rows, :]

    def mlp_send(index):
        weight_send(mlp_base + index, mlp_hbm[index].at[:, half_mine], mlp_place(index, row), dev_x)
        weight_send(mlp_base + 3 + index, mlp_hbm[index].at[:, half_other], mlp_place(index, row), dev_y)

    def mlp_relay(index):
        place = mlp_place(index, row_y)
        arrived(mlp_base + 3 + index, place)
        weight_send(mlp_base + 6 + index, place, place, dev_x)

    def mlp_ready(index):
        arrived(mlp_base + index, mlp_place(index, row_x))
        arrived(mlp_base + 6 + index, mlp_place(index, row_d))

    for index in range(2):
        attn_send(index)

    x_base = counter.take(7)
    cot_base = counter.take(3)

    def x_block(place, parity):
        return x_full.at[:, aligned((2 * place + parity) * DC, DC)]

    for pair in (2, 3, 1):
        send(x_base + pair - 1, x_hbm, x_block(z_at, core), dev_z[pair])
    send(x_base + 3, x_hbm, x_block(z_at, core), dev_c)

    pos_copy.wait()
    position_rows = jnp.broadcast_to(pos_ref[...].astype(F32), (8, T))
    position = dot_tn(position_rows, first_row[:, :HD], EXACT)
    pos_s[...] = position.astype(jnp.int32)
    lane_at = lax.broadcasted_iota(jnp.int32, (1, HD), 1)
    within = lax.rem(lane_at, HD // 2).astype(F32)
    frequency = jnp.exp(within * (-2.0 * math.log(THETA) / HD))
    angles = position * frequency
    cos_s[...] = jnp.cos(angles)
    sine = jnp.sin(angles)
    sin_s[...] = jnp.where(lane_at < HD // 2, -sine, sine)

    for index in range(2):
        attn_relay(index)
    attn_send(2)
    attn_send(3)
    for pair in (2, 1, 3):
        block = x_block(z_pair[pair], core)
        arrived(x_base + pair - 1, block)
        send(x_base + 3 + pair, block, block, dev_c)
    for copy in local_copies + small_copies:
        copy.wait()
    for pair in range(4):
        arrived(x_base + 3 + pair, x_block(z_pair[pair], 1 - core))
    attn_ready(0)
    attn_ready(1)

    def gain_at(ref, at):
        return ref[:, aligned(at * DC, DC)]

    qk_gain = (gain_at(query_gain_ref, col), gain_at(key_gain_ref, col))
    for index in range(2):
        hat_s[index] = dot_nn(x_full[...], wqkv[:, pl.ds(index * DC, DC)])
    for half in HALVES:
        query, key = hat_s[0, tokens(half), :], hat_s[1, tokens(half), :]
        scal_send(0, half, query * query, key * key)
    attn_relay(2)
    attn_relay(3)
    for index in range(3):
        mlp_send(index)
    attn_ready(2)
    low_s[2] = dot_nn(x_full[...], wqkv[:, pl.ds(2 * DC, DC)]).astype(BF)
    for half in HALVES:
        scales = [lax.rsqrt(total / D + EPS) for total in scal_get(0, half)]
        rows = tokens(half)
        work_s[0, rows, :] = jnp.concatenate(scales, axis=1)
        for index in range(2):
            hat = hat_s[index, rows, :] * wide(scales[index])
            hat_s[index, rows, :] = hat
            normed = hat * qk_gain[index]
            for head in range(2):
                part = normed[:, head * HD : (head + 1) * HD]
                turned = part * cos_s[rows, :] + pltpu.roll(part, HD // 2, 1) * sin_s[rows, :]
                if index == 0:
                    turned = turned * (HD**-0.5)
                low_s[index, rows, pl.ds(head * HD, HD)] = turned.astype(BF)

    chunk = 128

    def attend(half):
        count = (half + 1) * HT
        keys = pl.ds(0, count)

        def attend_chunk(at, carry):
            rows = aligned(at * chunk, chunk)
            query = at * chunk + lax.broadcasted_iota(jnp.int32, (chunk, count), 0)
            key = lax.broadcasted_iota(jnp.int32, (chunk, count), 1)
            oldest = query - pos_s[rows, :1]
            allowed = (key <= query) & (key >= oldest)
            for head in range(2):
                lanes = pl.ds(head * HD, HD)
                scores = dot_nt(low_s[0, rows, lanes], low_s[1, keys, lanes])
                scores = jnp.where(allowed, scores, MASKED)
                exponent = jnp.exp(scores - jnp.max(scores, axis=1, keepdims=True))
                probs = exponent / jnp.sum(exponent, axis=1, keepdims=True)
                probs_s[head, rows, keys] = probs
                att_s[rows, lanes] = dot_nn(probs.astype(BF), low_s[2, keys, lanes]).astype(BF)
            return carry

        first = half * (HT // chunk)
        lax.fori_loop(first, first + HT // chunk, attend_chunk, 0)

    branch_sums = [
        Reduce(
            lambda rows, start: dot_nt(att_s[rows, :], wo[pl.ds(start, DC), :]), False, half
        )
        for half in HALVES
    ]

    def middle_block(pair, place, half):
        rows = tokens(half)
        at = 2 * place + core
        raw = work_s[1, rows, :] if pair == 0 else braw_s[place, rows, :].astype(F32)
        hat = raw * wide(work_s[2, rows, :128])
        inputs = x_full[rows, aligned(at * DC, DC)].astype(F32)
        middle = inputs + hat * gain_at(attn_gain_ref, at)
        if pair == 0:
            bhat_s[rows, :] = hat
            middle_s[rows, :] = middle
        return middle.astype(BF)

    mid_gathers = [Gather(mid_full, True, braw_s, middle_block, half) for half in HALVES]

    def branch_done(half):
        rows = tokens(half)
        branch = branch_sums[half].finish()
        scal_send(1, half, branch * branch)
        work_s[1, rows, :] = branch
        braw_s[z_at, rows, :] = branch.astype(BF)
        mid_gathers[half].start()

    def branch_scaled(half):
        total, _ = scal_get(1, half)
        work_s[2, tokens(half), :128] = lax.rsqrt(total / D + EPS)

    attend(0)
    attn_ready(3)
    branch_sums[0].start()
    attend(1)
    branch_sums[1].start()
    mlp_relay(0)
    branch_done(0)
    mlp_relay(1)
    branch_scaled(0)
    mid_gathers[0].pass_on(0)
    branch_done(1)
    mlp_relay(2)
    mid_gathers[0].pass_on(2, 1, 3)
    branch_scaled(1)
    mid_gathers[1].pass_on(0)
    mid_gathers[1].pass_on(2, 1, 3)
    for pair in (2, 3, 1):
        weight_send(cot_base + pair - 1, cot_z.at[z_at], cot_z.at[z_at], dev_z[pair])
    mid_gathers[0].finish_own()
    mid_gathers[0].finish_other()
    mlp_ready(0)
    mlp_ready(1)

    tile = 256

    def forward_tiles(half):
        rows = half_rows(half, True)

        def forward_tile(at, carry):
            lanes = aligned(at * tile, tile)
            lanes_up = aligned(at * tile + FH, tile)
            gate = dot_nn(mid_full[rows, :], wgu[:, lanes])
            up = dot_nn(mid_full[rows, :], wgu[:, lanes_up])
            gu_s[rows, lanes] = gate.astype(BF)
            gu_s[rows, lanes_up] = up.astype(BF)
            mixed_s[rows, lanes] = (gate * jax.nn.sigmoid(gate) * up).astype(BF)
            return carry

        lax.fori_loop(0, FH // tile, forward_tile, 0)

    ffn_sums = [
        Reduce(
            lambda rows, start: dot_nt(mixed_s[rows, :], wd[pl.ds(start, DC), :]), True, half
        )
        for half in HALVES
    ]
    mlp_gain = gain_at(mlp_gain_ref, col)

    def grad_ffn_block(pair, place, half):
        rows = tokens(half)
        at = 2 * place + core
        raw = work_s[1, rows, :] if pair == 0 else raw_s[place, rows, :].astype(F32)
        scale = wide(work_s[2, rows, 128:])
        grad = cot_z[place, rows, :].astype(F32) * gain_at(mlp_gain_ref, at)
        return (scale * (grad - raw * scale * wide(inner_s[rows, :]))).astype(BF)

    gf_gathers = [Gather(gf_full, True, raw_s, grad_ffn_block, half) for half in HALVES]

    def ffn_done(half):
        rows = tokens(half)
        ffn = ffn_sums[half].finish()
        cot = cot_z[z_at, rows, :].astype(F32)
        scal_send(2, half, ffn * ffn, cot * mlp_gain * ffn)
        work_s[1, rows, :] = ffn
        raw_s[z_at, rows, :] = ffn.astype(BF)
        gf_gathers[half].start()

    def ffn_scaled(half):
        rows = tokens(half)
        total, inner = scal_get(2, half)
        scale = lax.rsqrt(total / D + EPS)
        work_s[2, rows, 128:] = scale
        inner_s[rows, :] = inner * scale / D

    forward_tiles(0)
    mlp_ready(2)
    ffn_sums[0].start()
    mid_gathers[1].finish_own()
    mid_gathers[1].finish_other()
    forward_tiles(1)
    ffn_sums[0].planes(0, 1)
    ffn_sums[1].start()
    ffn_sums[0].planes(2, 3)
    ffn_sums[1].planes(0, 1)
    for pair in (1, 2, 3):
        arrived(cot_base + pair - 1, cot_z.at[z_pair[pair]])
    ffn_done(0)
    ffn_sums[1].planes(2, 3)
    ffn_scaled(0)
    gf_gathers[0].pass_on(0)
    ffn_done(1)
    gf_gathers[0].pass_on(2, 1, 3)
    ffn_scaled(1)
    gf_gathers[1].pass_on(0, 2, 1, 3)
    ffn_hat = work_s[1] * wide(work_s[2, :, 128:])
    out_lo[...] = (middle_s[...] + ffn_hat * mlp_gain).astype(BF)
    gain_s[row, 3:4, :] = jnp.sum(cot_z[z_at].astype(F32) * ffn_hat, axis=0, keepdims=True)
    lo_copy = local(out_lo, layer_out)
    gf_gathers[0].finish_own()
    gf_gathers[0].finish_other()

    def backward_tiles(half):
        rows = half_rows(half, True)

        def backward_tile(at, carry):
            lanes = aligned(at * tile, tile)
            lanes_up = aligned(at * tile + FH, tile)
            grad_mixed = dot_nn(gf_full[rows, :], wd[:, lanes])
            gate = gu_s[rows, lanes].astype(F32)
            up = gu_s[rows, lanes_up].astype(F32)
            sigma = jax.nn.sigmoid(gate)
            gu_s[rows, lanes] = (grad_mixed * up * sigma * (1.0 + gate * (1.0 - sigma))).astype(BF)
            gu_s[rows, lanes_up] = (grad_mixed * gate * sigma).astype(BF)
            return carry

        lax.fori_loop(0, FH // tile, backward_tile, 0)

    def lanes_of(owner):
        return aligned(owner * DR, DR)

    def down_piece(owner):
        return dot_tn(gf_full[:, lanes_of(owner)], mixed_s[...])

    def gu_piece(owner, part):
        return dot_tn(mid_full[:, lanes_of(owner)], gu_s[:, pl.ds(part * FH, FH)])

    grad_base = counter.take(9)
    grad_sends = {}

    def grad_lanes(part):
        return pl.ds(part * FH, FH)

    def grad_stage(slot, part):
        if part == 2:
            return stage_down.at[slot]
        return stage_gu.at[slot, :, grad_lanes(part)]

    def grad_piece(slot, part, more=None):
        owner = (row_d, row_x, row_y, row)[slot]
        total = down_piece(owner) if part == 2 else gu_piece(owner, part)
        if more is not None:
            total = total + more
        grad_stage(slot, part)[...] = total.astype(BF)

    def grad_send(slot, part, landing, device):
        index = grad_base + 3 * slot + part
        grad_sends[slot, part] = send(index, grad_stage(slot, part), landing, device)

    def grad_diagonal(part):
        grad_piece(0, part)
        grad_send(0, part, rel_mlp.at[:, grad_lanes(part)], dev_x)

    def grad_near(part):
        grad_piece(1, part)
        grad_send(1, part, land_mlp.at[1, :, grad_lanes(part)], dev_x)

    def grad_relay(part):
        arrived(grad_base + part, rel_mlp.at[:, grad_lanes(part)])
        grad_piece(2, part, rel_mlp[:, grad_lanes(part)].astype(F32))
        grad_send(2, part, land_mlp.at[2, :, grad_lanes(part)], dev_y)

    mid_sums = [
        Reduce(lambda rows, start: dot_nt(gu_s[rows, :], wgu[pl.ds(start, DC), :]), True, half)
        for half in HALVES
    ]
    attn_gain = gain_at(attn_gain_ref, col)

    def grad_branch_block(pair, place, half):
        rows = tokens(half)
        at = 2 * place + core
        scale = wide(work_s[2, rows, :128])
        raw = middle_s[rows, :] if pair == 0 else raw_s[place, rows, :].astype(F32)
        hat = bhat_s[rows, :] if pair == 0 else braw_s[place, rows, :].astype(F32) * scale
        inner = wide(inner_s[rows, :])
        return (scale * (raw * gain_at(attn_gain_ref, at) - hat * inner)).astype(BF)

    gb_gathers = [Gather(gb_full, False, raw_s, grad_branch_block, half) for half in HALVES]

    def mid_done(half):
        rows = tokens(half)
        grad_middle = cot_z[z_at, rows, :].astype(F32) + mid_sums[half].finish()
        scal_send(3, half, grad_middle * attn_gain * bhat_s[rows, :])
        middle_s[rows, :] = grad_middle
        raw_s[z_at, rows, :] = grad_middle.astype(BF)
        gb_gathers[half].start()

    def mid_scaled(half):
        inner, _ = scal_get(3, half)
        inner_s[tokens(half), :] = inner / D

    def attend_back(half):
        count = (half + 1) * HT
        keys = pl.ds(0, count)

        def attend_back_chunk(at, carry):
            rows = aligned(at * chunk, chunk)
            for head in range(2):
                lanes = pl.ds(head * HD, HD)
                grad_probs = dot_nt(ga_s[rows, lanes], low_s[2, keys, lanes])
                probs = probs_s[head, rows, keys]
                inner = jnp.sum(probs * grad_probs, axis=1, keepdims=True)
                grad_scores = (probs * (grad_probs - inner)).astype(BF)
                gs_s[head, rows, keys] = grad_scores
                gqk_s[0, rows, lanes] = dot_nn(grad_scores, low_s[1, keys, lanes])
            return carry

        first = half * (HT // chunk)
        lax.fori_loop(first, first + HT // chunk, attend_back_chunk, 0)

    backward_tiles(0)
    gf_gathers[0].finish_sends()
    mid_sums[0].start()
    gf_gathers[1].finish_own()
    gf_gathers[1].finish_other()
    grad_diagonal(2)
    backward_tiles(1)
    gf_gathers[1].finish_sends()
    mid_sums[1].start()
    grad_diagonal(0)
    grad_diagonal(1)
    mid_sums[0].planes(0, 1, 2, 3)
    grad_relay(2)
    mid_sums[1].planes(0, 1)
    mid_done(0)
    mid_sums[1].planes(2, 3)
    grad_relay(0)
    grad_near(2)
    mid_scaled(0)
    gb_gathers[0].pass_on(0)
    mid_done(1)
    grad_relay(1)
    grad_near(0)
    gb_gathers[0].pass_on(2, 1, 3)
    mid_scaled(1)
    gb_gathers[1].pass_on(0)
    grad_near(1)
    late = []
    gb_gathers[0].finish_own()
    ga_s[tokens(0), :] = dot_nn(gb_full[tokens(0), :], wo[...]).astype(BF)
    gb_gathers[1].pass_on(2, 1, 3)
    attend_back(0)
    gain_s[row, 2:3, :] = jnp.sum(middle_s[...] * bhat_s[...], axis=0, keepdims=True)
    gb_gathers[1].finish_own()

    ga_s[tokens(1), :] = dot_nn(gb_full[tokens(1), :], wo[...]).astype(BF)

    whole = pl.ds(0, DR)
    upper = pl.ds(0, DR // 2)
    lower = pl.ds(DR // 2, DR // 2)
    BY_Y = ((whole, 2),)
    BY_BOTH = ((upper, 1), (lower, 2))
    neighbours = {1: dev_x, 2: dev_y}
    attn_grad_base = counter.take(3 * 6)

    class AttnGrad:
        def __init__(self, order, routes, left, right, start, size):
            self.base = attn_grad_base + 6 * order
            self.routes = routes
            self.left, self.right = left, right
            self.start_lane, self.size = start, size
            self.lanes = pl.ds(start, size)

        def at(self, slot, rows):
            rows = pl.ds(slot // 2 * DR + rows.start, rows.size)
            return gf_full.at[rows, pl.ds(slot % 2 * 4 * DC + self.start_lane, self.size)]

        def piece(self, slot):
            owner = (row_d, row_x, row_y, row)[slot]
            piece = dot_tn(self.left[:, lanes_of(owner)], self.right())
            self.at(slot, whole)[...] = piece.astype(BF)

        def diagonal(self):
            self.piece(0)
            for step, (rows, first) in enumerate(self.routes):
                landing = rel_attn.at[rows, self.lanes]
                send(self.base + step, self.at(0, rows), landing, neighbours[first])

        def near(self):
            self.piece(1)
            self.piece(2)
            for step, (rows, first) in enumerate(self.routes):
                landing = land_attn.at[first, rows, self.lanes]
                send(self.base + 2 + step, self.at(first, rows), landing, neighbours[first])

        def own(self):
            self.piece(3)
            late.append(local(self.at(3, whole), land_attn.at[0, :, self.lanes]))

        def relay(self):
            for step, (rows, first) in enumerate(self.routes):
                slot = 3 - first
                arrived(self.base + step, rel_attn.at[rows, self.lanes])
                stage = self.at(slot, rows)
                stage[...] = (
                    stage[...].astype(F32) + rel_attn[rows, self.lanes].astype(F32)
                ).astype(BF)
                landing = land_attn.at[slot, rows, self.lanes]
                send(self.base + 4 + step, stage, landing, neighbours[slot])

        def finish(self):
            for step, (rows, first) in enumerate(self.routes):
                arrived(self.base + 2 + step, land_attn.at[first, rows, self.lanes])
                arrived(self.base + 4 + step, land_attn.at[3 - first, rows, self.lanes])

    grad_piece(3, 2)
    late.append(local(stage_down.at[3], land_mlp.at[0, :, grad_lanes(2)]))
    for gather in gf_gathers:
        gather.finish_sends()
    o_grad = AttnGrad(0, BY_BOTH, gb_full, lambda: att_s[...], 3 * DC, DC)
    o_grad.diagonal()
    o_grad.near()

    attend_back(1)
    early, last = pl.ds(0, HT), pl.ds(HT, HT)
    for head in range(2):
        lanes = pl.ds(head * HD, HD)
        gqk_s[1, early, lanes] = dot_tn(gs_s[head, :, early], low_s[0, :, lanes])
        gqk_s[1, last, lanes] = dot_tn(gs_s[head, last, last], low_s[0, last, lanes])
    inners = []
    for index in range(2):
        for head in range(2):
            lanes = pl.ds(head * HD, HD)
            part = gqk_s[index, :, lanes]
            turned = part * cos_s[...] - pltpu.roll(part, HD // 2, 1) * sin_s[...]
            if index == 0:
                turned = turned * (HD**-0.5)
            gqk_s[index, :, lanes] = turned
        weighted = gqk_s[index] * hat_s[index]
        gain_s[row, index : index + 1, :] = jnp.sum(weighted, axis=0, keepdims=True)
        inners.append(weighted * qk_gain[index])
    for half in HALVES:
        part = slice(half * HT, (half + 1) * HT)
        scal_send(4, half, inners[0][part], inners[1][part])
    gain_base = counter.take(3)
    for slot, device in enumerate((dev_x, dev_y, dev_d)):
        send(gain_base + slot, gain_s.at[row], gain_s.at[row], device)
    for head in range(2):
        lanes = pl.ds(head * HD, HD)
        out_lanes = pl.ds(2 * DC + head * HD, HD)
        gqkv_s[early, out_lanes] = dot_tn(
            probs_s[head, :, early].astype(BF), ga_s[:, lanes]
        ).astype(BF)
        gqkv_s[last, out_lanes] = dot_tn(
            probs_s[head, last, last].astype(BF), ga_s[last, lanes]
        ).astype(BF)
    v_grad = AttnGrad(1, BY_BOTH, x_full, lambda: gqkv_s[:, 2 * DC :], 2 * DC, DC)
    v_grad.diagonal()
    v_grad.near()
    for half in HALVES:
        rows = tokens(half)
        totals = scal_get(4, half)
        for index in range(2):
            scale = wide(work_s[0, rows, index * 128 : (index + 1) * 128])
            gqkv_s[rows, pl.ds(index * DC, DC)] = (
                scale
                * (
                    gqk_s[index, rows, :] * qk_gain[index]
                    - hat_s[index, rows, :] * wide(totals[index] / D)
                )
            ).astype(BF)
    in_sums = [
        Reduce(
            lambda rows, start: dot_nt(gqkv_s[rows, :], wqkv[pl.ds(start, DC), :]), False, half
        )
        for half in HALVES
    ]
    qk_grad = AttnGrad(2, BY_BOTH, x_full, lambda: gqkv_s[:, : 2 * DC], 0, 2 * DC)
    qk_grad.diagonal()
    in_sums[0].start()
    qk_grad.near()
    in_sums[1].start()
    o_grad.relay()
    v_grad.relay()
    qk_grad.relay()
    for grad in (o_grad, v_grad, qk_grad):
        grad.own()
    grad_piece(3, 0)
    grad_piece(3, 1)
    late.append(local(stage_gu.at[3], land_mlp.at[0, :, pl.ds(0, 2 * FH)]))
    for half in HALVES:
        rows = tokens(half)
        work_s[1, rows, :] = middle_s[rows, :] + in_sums[half].finish()
    late.append(local(work_s.at[1], grad_in))
    late.append(lo_copy)

    for slot, owner in enumerate((row_x, row_y, row_d)):
        arrived(gain_base + slot, gain_s.at[owner])
    gains_out[...] = gain_s[0] + gain_s[1] + gain_s[2] + gain_s[3]
    for slot in (1, 2):
        for part in range(3):
            arrived(grad_base + 3 * slot + part, land_mlp.at[slot, :, grad_lanes(part)])
    for grad in (o_grad, v_grad, qk_grad):
        grad.finish()
    for copy in late:
        copy.wait()
    for copy in list(pending):
        sent(copy)
    assert counter.used <= send_sem.shape[0], counter.used


def total_kernel(
    lo_ref, gin_ref, gains_ref, mlp_ref, attn_ref, lo_out, gin_out, *outs
):
    y_at = lax.div(lax.axis_index("row"), 2)
    lo_out[...] = lo_ref[...]
    gin_out[...] = gin_ref[...]
    attn = attn_ref[0].astype(F32) + attn_ref[1].astype(F32) + attn_ref[2].astype(F32)
    for index in range(4):
        outs[index][...] = attn[:, index * DC : (index + 1) * DC]
    mine = mlp_ref[0].astype(F32) + mlp_ref[1].astype(F32)
    other = mlp_ref[2].astype(F32)
    for index in range(3):
        lanes = slice(index * FH, (index + 1) * FH)
        outs[4 + index][:, aligned(y_at * FH, FH)] = mine[:, lanes]
        outs[4 + index][:, aligned((1 - y_at) * FH, FH)] = other[:, lanes]
    for index in range(4):
        outs[7 + index][...] = gains_ref[index : index + 1, :]


MIB = 1 << 20


def on_device_kernel(
    inputs,
    query_weight,
    key_weight,
    value_weight,
    output_weight,
    gate_weight,
    up_weight,
    down_weight,
    query_gain,
    key_gain,
    attn_gain,
    mlp_gain,
    positions,
    segments,
    cotangent,
):
    hbm = pl.BlockSpec(memory_space=pl.ANY)
    vmem = pl.BlockSpec(memory_space=pltpu.VMEM)
    sds = jax.ShapeDtypeStruct
    copies = 150
    landed = pl.pallas_call(
        block_kernel,
        out_shape=[
            sds((T, DC), BF),
            sds((T, DC), F32),
            sds((8, DC), F32),
            sds((3, DR, 3 * FH), BF),
            sds((3, DR, 4 * DC), BF),
        ],
        in_specs=[hbm] * 14,
        out_specs=[hbm, hbm, vmem, hbm, hbm],
        scratch_shapes=[
            pltpu.VMEM((D, 3 * DC), BF),
            pltpu.VMEM((D, DC), BF),
            pltpu.VMEM((D, 2 * FH), BF),
            pltpu.VMEM((D, FH), BF),
            pltpu.VMEM((T, D), BF),
            pltpu.VMEM((2 * T, D), BF),
            pltpu.VMEM((2 * T, D), BF),
            pltpu.VMEM((T, D), BF),
            pltpu.VMEM((2 * T, 2 * FH), BF),
            pltpu.VMEM((2 * T, FH), BF),
            pltpu.VMEM((2, T, T), F32),
            pltpu.VMEM((2, T, DC), F32),
            pltpu.VMEM((3, T, DC), BF),
            pltpu.VMEM((T, HD), F32),
            pltpu.VMEM((T, HD), F32),
            pltpu.VMEM((T, HD), jnp.int32),
            pltpu.VMEM((4, T, DC), BF),
            pltpu.VMEM((4, T, DC), BF),
            pltpu.VMEM((4, T, DC), BF),
            pltpu.VMEM((T, DC), F32),
            pltpu.VMEM((T, DC), F32),
            pltpu.VMEM((3, T, DC), F32),
            pltpu.VMEM((T, HD), F32),
            pltpu.VMEM((T, DC), BF),
            pltpu.VMEM((T, DC), BF),
            pltpu.VMEM((T, 3 * DC), BF),
            pltpu.VMEM((2, T, T), BF),
            pltpu.VMEM((2, T, DC), F32),
            pltpu.VMEM((4, 2 * T, DC), F32),
            pltpu.VMEM((4, 2 * T, DC), BF),
            pltpu.VMEM((4, 2 * T, DC), BF),
            pltpu.VMEM((4, T, DC), BF),
            pltpu.VMEM((4, T, DC), BF),
            pltpu.VMEM((3, T, DC), BF),
            pltpu.VMEM((3, T, DC), BF),
            pltpu.VMEM((T, DC), BF),
            pltpu.VMEM((LAYER_STAGES, 2, 8, 8, HT), F32),
            pltpu.VMEM((4, 8, DC), F32),
            pltpu.VMEM((4, DR, FH), BF),
            pltpu.VMEM((4, DR, 2 * FH), BF),
            pltpu.VMEM((DR, 3 * FH), BF),
            pltpu.VMEM((DR, 4 * DC), BF),
            pltpu.VMEM((T, DC), BF),
            pltpu.VMEM((1, D), F32),
            pltpu.VMEM((1, D), F32),
            pltpu.VMEM((1, D), F32),
            pltpu.VMEM((1, D), F32),
            pltpu.VMEM((1, T), jnp.int32),
            pltpu.SemaphoreType.DMA((copies,)),
            pltpu.SemaphoreType.DMA((copies,)),
            pltpu.SemaphoreType.DMA((24,)),
        ],
        compiler_params=pltpu.CompilerParams(
            collective_id=0, has_side_effects=True, vmem_limit_bytes=64 * MIB
        ),
        cost_estimate=pl.CostEstimate(
            flops=26_800_000_000, bytes_accessed=16_000_000, transcendentals=2_000_000
        ),
    )(
        inputs,
        query_weight,
        key_weight,
        value_weight,
        output_weight,
        gate_weight,
        up_weight,
        down_weight,
        cotangent,
        query_gain[None, :],
        key_gain[None, :],
        attn_gain[None, :],
        mlp_gain[None, :],
        positions[None, :],
    )
    step = 256

    def rows_of(width):
        return pl.BlockSpec((step, width), lambda at: (at, 0))

    gain_spec = pl.BlockSpec((1, DC), lambda at: (0, 0))
    results = pl.pallas_call(
        total_kernel,
        grid=(DR // step,),
        out_shape=[sds((T, DC), BF), sds((T, DC), F32)]
        + [sds((DR, DC), F32)] * 4
        + [sds((DR, 2 * FH), F32)] * 3
        + [sds((1, DC), F32)] * 4,
        in_specs=[
            rows_of(DC),
            rows_of(DC),
            pl.BlockSpec((8, DC), lambda at: (0, 0)),
            pl.BlockSpec((3, step, 3 * FH), lambda at: (0, at, 0)),
            pl.BlockSpec((3, step, 4 * DC), lambda at: (0, at, 0)),
        ],
        out_specs=[rows_of(DC)] * 6 + [rows_of(2 * FH)] * 3 + [gain_spec] * 4,
        compiler_params=pltpu.CompilerParams(vmem_limit_bytes=64 * MIB),
    )(*landed)
    return (*results[:9], *[gain[0] for gain in results[9:]])


def solution(mesh):
    in_specs = (
        P("row", "col"),
        P("row", "col"),
        P("row", "col"),
        P("row", "col"),
        P("row", "col"),
        P("row", "col"),
        P("row", "col"),
        P("row", "col"),
        P(),
        P(),
        P(),
        P(),
        P("row"),
        P("row"),
        P("row", "col"),
    )
    out_specs = (
        P("row", "col"),
        P("row", "col"),
        P("row", "col"),
        P("row", "col"),
        P("row", "col"),
        P("row", "col"),
        P("row", "col"),
        P("row", "col"),
        P("row", "col"),
        P("col"),
        P("col"),
        P("col"),
        P("col"),
    )
    sizes = (mesh.shape["row"], mesh.shape["col"])
    body = on_device_kernel if sizes == (4, 8) else on_device
    return jax.shard_map(
        body, mesh=mesh, in_specs=in_specs, out_specs=out_specs, check_vma=False
    )
```

```python
import math

import jax
import jax.numpy as jnp
from jax import lax
from jax.experimental import pallas as pl
from jax.experimental.pallas import tpu as pltpu
from jax.sharding import PartitionSpec as P

HD = 128
LENGTH = 512


EPS = 1e-06
THETA = 500000.0
MASKED = -1e30


def rope_tables(positions, head_size):
    halfway = head_size // 2
    frequency = jnp.exp(
        jnp.arange(halfway, dtype=jnp.float32) * (-2.0 * math.log(THETA) / head_size)
    )
    angles = positions.astype(jnp.float32)[:, None] * frequency[None, :]
    return (jnp.cos(angles)[:, None, :], jnp.sin(angles)[:, None, :])


def rotate(values, cosine, sine):
    halfway = values.shape[-1] // 2
    first_half = values[..., :halfway]
    second_half = values[..., halfway:]
    return jnp.concatenate(
        [first_half * cosine - second_half * sine, second_half * cosine + first_half * sine],
        axis=-1,
    )


def matmul(left, right):
    return jnp.dot(left, right, preferred_element_type=jnp.float32)


def cross_rows(left, right):
    return lax.dot_general(
        left, right, (((0,), (0,)), ((), ())), preferred_element_type=jnp.float32
    )


def cross_cols(left, right):
    return lax.dot_general(
        left, right, (((1,), (1,)), ((), ())), preferred_element_type=jnp.float32
    )


def visible_pairs(segment_part):
    places = jnp.arange(segment_part.shape[0])
    return (segment_part[:, None] == segment_part[None, :]) & (places[:, None] >= places[None, :])


def on_device(
    inputs,
    query_weight,
    key_weight,
    value_weight,
    output_weight,
    gate_weight,
    up_weight,
    down_weight,
    query_gain,
    key_gain,
    attn_gain,
    mlp_gain,
    positions,
    segments,
    cotangent,
):
    bfloat = jnp.bfloat16
    floats = jnp.float32
    rows = inputs.shape[0]
    local_width = inputs.shape[1]
    width = local_width * lax.axis_size("col")
    offset = lax.axis_index("col") * local_width
    head_size = HD
    heads_here = local_width // head_size
    sequences = rows // LENGTH
    scale = head_size ** (-0.5)
    shape_seq = (sequences, LENGTH, heads_here, head_size)

    def mine(values):
        return lax.dynamic_slice_in_dim(values, offset, local_width, values.ndim - 1)

    query_gain_here = mine(query_gain)
    key_gain_here = mine(key_gain)
    cot_here = cotangent.astype(floats)
    gathered = (
        lax.all_gather(query_weight, "row", axis=0, tiled=True),
        lax.all_gather(key_weight, "row", axis=0, tiled=True),
        lax.all_gather(value_weight, "row", axis=0, tiled=True),
        lax.all_gather(gate_weight, "row", axis=0, tiled=True),
        lax.all_gather(up_weight, "row", axis=0, tiled=True),
        lax.all_gather(output_weight, "row", axis=0, tiled=True),
        lax.all_gather(down_weight, "row", axis=0, tiled=True),
    )
    query_full, key_full, value_full, gate_full, up_full, output_full, down_full = gathered
    whole_in = lax.all_gather(inputs, "col", axis=1, tiled=True)
    query_raw = matmul(whole_in, query_full)
    key_raw = matmul(whole_in, key_full)
    value_raw = matmul(whole_in, value_full)
    query_total, key_total = lax.psum(
        (jnp.sum(query_raw * query_raw, axis=1), jnp.sum(key_raw * key_raw, axis=1)), "col"
    )
    query_scale = lax.rsqrt(query_total / width + EPS)[:, None]
    key_scale = lax.rsqrt(key_total / width + EPS)[:, None]
    query_hat = query_raw * query_scale
    key_hat = key_raw * key_scale
    cosine, sine = rope_tables(positions, head_size)
    query_low = (
        rotate((query_hat * query_gain_here).reshape(rows, heads_here, head_size), cosine, sine)
        * scale
    ).astype(bfloat)
    key_low = rotate(
        (key_hat * key_gain_here).reshape(rows, heads_here, head_size), cosine, sine
    ).astype(bfloat)
    value_low = value_raw.astype(bfloat).reshape(rows, heads_here, head_size)
    query_blocks = query_low.reshape(shape_seq)
    key_blocks = key_low.reshape(shape_seq)
    value_blocks = value_low.reshape(shape_seq)
    segment_blocks = segments.reshape(sequences, LENGTH)

    def attend(block):
        queries, keys_part, values_part, segment_part = block
        scores = jnp.einsum("qhd,khd->hqk", queries, keys_part, preferred_element_type=floats)
        scores = jnp.where(visible_pairs(segment_part)[None], scores, MASKED)
        largest = jnp.max(scores, axis=-1, keepdims=True)
        exponent = jnp.exp(scores - largest)
        totals = jnp.sum(exponent, axis=-1, keepdims=True)
        weights_low = (exponent / totals).astype(bfloat)
        attended_part = jnp.einsum(
            "hqk,khd->qhd", weights_low, values_part, preferred_element_type=floats
        )
        return (attended_part, (largest + jnp.log(totals))[..., 0])

    attended, log_totals = lax.map(attend, (query_blocks, key_blocks, value_blocks, segment_blocks))
    attended_low = attended.reshape(rows, local_width).astype(bfloat)
    branch = lax.psum(cross_cols(attended_low, output_full), "col")
    branch_scale = lax.rsqrt(jnp.mean(branch * branch, axis=1, keepdims=True) + EPS)
    branch_hat = branch * branch_scale
    middle = whole_in.astype(floats) + branch_hat * attn_gain
    middle_low = middle.astype(bfloat)
    middle_here = mine(middle)
    branch_hat_here = mine(branch_hat)
    gate_pre = matmul(middle_low, gate_full)
    up_pre = matmul(middle_low, up_full)
    sigma = jax.nn.sigmoid(gate_pre)
    silu_gate = gate_pre * sigma
    mixed_low = (silu_gate * up_pre).astype(bfloat)
    ffn = lax.psum(cross_cols(mixed_low, down_full), "col")
    ffn_scale = lax.rsqrt(jnp.mean(ffn * ffn, axis=1, keepdims=True) + EPS)
    ffn_hat = ffn * ffn_scale
    ffn_hat_here = mine(ffn_hat)
    grad_top = lax.all_gather(cotangent, "col", axis=1, tiled=True).astype(floats)
    normed_top = grad_top * mlp_gain
    inner_top = jnp.sum(normed_top * ffn_hat, axis=1, keepdims=True)
    grad_ffn_low = (ffn_scale * (normed_top - ffn_hat * inner_top / width)).astype(bfloat)
    layer_out = (middle_here + ffn_hat_here * mine(mlp_gain)).astype(bfloat)
    grad_mlp_gain = jnp.sum(cot_here * ffn_hat_here, axis=0)
    grad_down = cross_rows(grad_ffn_low, mixed_low)
    grad_mixed = matmul(grad_ffn_low, down_full)
    grad_gate_low = (grad_mixed * up_pre * sigma * (1.0 + gate_pre * (1.0 - sigma))).astype(bfloat)
    grad_up_low = (grad_mixed * silu_gate).astype(bfloat)
    grad_middle_part = cross_cols(grad_gate_low, gate_full) + cross_cols(grad_up_low, up_full)
    grad_gate = cross_rows(middle_low, grad_gate_low)
    grad_up = cross_rows(middle_low, grad_up_low)
    grad_middle = grad_top + lax.psum(grad_middle_part, "col")
    grad_middle_here = mine(grad_middle)
    grad_attn_gain = jnp.sum(grad_middle_here * branch_hat_here, axis=0)
    normed_mid = grad_middle * attn_gain
    inner_mid = jnp.sum(normed_mid * branch_hat, axis=1, keepdims=True)
    grad_branch_low = (branch_scale * (normed_mid - branch_hat * inner_mid / width)).astype(bfloat)
    grad_output = cross_rows(grad_branch_low, attended_low)
    grad_attended_low = matmul(grad_branch_low, output_full).astype(bfloat)

    def attend_back(block):
        queries, keys_part, values_part, segment_part, log_part, grad_part = block
        scores = jnp.einsum("qhd,khd->hqk", queries, keys_part, preferred_element_type=floats)
        scores = jnp.where(visible_pairs(segment_part)[None], scores, MASKED)
        probs = jnp.exp(scores - log_part[..., None])
        grad_values = jnp.einsum(
            "hqk,qhd->khd", probs.astype(bfloat), grad_part, preferred_element_type=floats
        )
        grad_probs = jnp.einsum(
            "qhd,khd->hqk", grad_part, values_part, preferred_element_type=floats
        )
        grad_scores = probs * (grad_probs - jnp.sum(probs * grad_probs, axis=-1, keepdims=True))
        scores_low = grad_scores.astype(bfloat)
        grad_queries = jnp.einsum(
            "hqk,khd->qhd", scores_low, keys_part, preferred_element_type=floats
        )
        grad_keys = jnp.einsum("hqk,qhd->khd", scores_low, queries, preferred_element_type=floats)
        return (grad_queries, grad_keys, grad_values.astype(bfloat))

    grad_queries, grad_keys, grad_values = lax.map(
        attend_back,
        (
            query_blocks,
            key_blocks,
            value_blocks,
            segment_blocks,
            log_totals,
            grad_attended_low.reshape(shape_seq),
        ),
    )
    grad_query_norm = rotate(
        grad_queries.reshape(rows, heads_here, head_size) * scale, cosine, -sine
    ).reshape(rows, local_width)
    grad_key_norm = rotate(grad_keys.reshape(rows, heads_here, head_size), cosine, -sine).reshape(
        rows, local_width
    )
    grad_query_gain = jnp.sum(grad_query_norm * query_hat, axis=0)
    grad_key_gain = jnp.sum(grad_key_norm * key_hat, axis=0)
    normed_query = grad_query_norm * query_gain_here
    normed_key = grad_key_norm * key_gain_here
    inner_query, inner_key = lax.psum(
        (jnp.sum(normed_query * query_hat, axis=1), jnp.sum(normed_key * key_hat, axis=1)), "col"
    )
    grad_query_low = (
        query_scale * (normed_query - query_hat * inner_query[:, None] / width)
    ).astype(bfloat)
    grad_key_low = (key_scale * (normed_key - key_hat * inner_key[:, None] / width)).astype(bfloat)
    grad_value_low = grad_values.reshape(rows, local_width)
    grad_in_part = (
        cross_cols(grad_query_low, query_full)
        + cross_cols(grad_key_low, key_full)
        + cross_cols(grad_value_low, value_full)
    )
    grad_inputs = grad_middle_here + lax.psum_scatter(
        grad_in_part, "col", scatter_dimension=1, tiled=True
    )
    grad_query = cross_rows(whole_in, grad_query_low)
    grad_key = cross_rows(whole_in, grad_key_low)
    grad_value = cross_rows(whole_in, grad_value_low)
    summed = (
        lax.psum_scatter(grad_query, "row", scatter_dimension=0, tiled=True),
        lax.psum_scatter(grad_key, "row", scatter_dimension=0, tiled=True),
        lax.psum_scatter(grad_value, "row", scatter_dimension=0, tiled=True),
        lax.psum_scatter(grad_output, "row", scatter_dimension=0, tiled=True),
        lax.psum_scatter(grad_gate, "row", scatter_dimension=0, tiled=True),
        lax.psum_scatter(grad_up, "row", scatter_dimension=0, tiled=True),
        lax.psum_scatter(grad_down, "row", scatter_dimension=0, tiled=True),
    )
    gains = lax.psum((grad_query_gain, grad_key_gain, grad_attn_gain, grad_mlp_gain), "row")
    return (
        layer_out,
        grad_inputs,
        summed[0],
        summed[1],
        summed[2],
        summed[3],
        summed[4],
        summed[5],
        summed[6],
        gains[0],
        gains[1],
        gains[2],
        gains[3],
    )


BF = jnp.bfloat16
F32 = jnp.float32
MESH_ID = pl.DeviceIdType.MESH
T = 512
DC = 256
DR = 512
D = 2048
FH = 512
HT = 256
LAYER_STAGES = 5
EXACT = lax.Precision.HIGHEST


def dot_nn(a, b):
    return jnp.dot(a, b, preferred_element_type=F32)


def dot_nt(a, b, precision=None):
    return lax.dot_general(
        a, b, (((1,), (1,)), ((), ())), precision=precision, preferred_element_type=F32
    )


def dot_tn(a, b, precision=None):
    return lax.dot_general(
        a, b, (((0,), (0,)), ((), ())), precision=precision, preferred_element_type=F32
    )


def aligned(start, size):
    return pl.ds(pl.multiple_of(start, size), size)


class Counter:
    def __init__(self):
        self.used = 0

    def take(self, count=1):
        first = self.used
        self.used += count
        return first


def block_kernel(
    x_hbm,
    wq_hbm,
    wk_hbm,
    wv_hbm,
    wo_hbm,
    wg_hbm,
    wu_hbm,
    wd_hbm,
    cot_hbm,
    query_gain_hbm,
    key_gain_hbm,
    attn_gain_hbm,
    mlp_gain_hbm,
    pos_hbm,
    layer_out,
    grad_in,
    gains_out,
    land_mlp,
    land_attn,
    wqkv,
    wo,
    wgu,
    wd,
    x_full,
    mid_full,
    gf_full,
    gb_full,
    gu_s,
    mixed_s,
    probs_s,
    hat_s,
    low_s,
    cos_s,
    sin_s,
    pos_s,
    cot_z,
    braw_s,
    raw_s,
    middle_s,
    bhat_s,
    work_s,
    inner_s,
    att_s,
    ga_s,
    gqkv_s,
    gs_s,
    gqk_s,
    own_s,
    stage_c,
    land_c,
    stage_y,
    land_y,
    stage_z,
    land_z,
    land_r,
    scal_s,
    gain_s,
    stage_down,
    stage_gu,
    rel_mlp,
    rel_attn,
    out_lo,
    query_gain_ref,
    key_gain_ref,
    attn_gain_ref,
    mlp_gain_ref,
    pos_ref,
    send_sem,
    recv_sem,
    local_sem,
):
    row = lax.axis_index("row")
    col = lax.axis_index("col")
    x_at = lax.rem(row, 2)
    y_at = lax.div(row, 2)
    core = lax.rem(col, 2)
    z_at = lax.div(col, 2)
    row_x = row + 1 - 2 * x_at
    row_y = lax.rem(row + 2, 4)
    row_d = row_y + 1 - 2 * x_at
    sib = col + 1 - 2 * core
    dev_x = (row_x, col)
    dev_y = (row_y, col)
    dev_d = (row_d, col)
    dev_c = (row, sib)
    z_pair = {
        0: z_at,
        1: z_at + 1 - 2 * lax.rem(z_at, 2),
        2: lax.rem(z_at + 2, 4),
        3: 3 - z_at,
    }
    middle = (z_at == 1) | (z_at == 2)
    at_end = (z_at == 0) | (z_at == 3)
    dev_z = {pair: (row, 2 * z_pair[pair] + core) for pair in (1, 2, 3)}

    counter = Counter()
    locals_used = Counter()
    pending = []

    def copy_of(index, src, dst, device, send_index=None):
        return pltpu.make_async_remote_copy(
            src_ref=src,
            dst_ref=dst,
            send_sem=send_sem.at[index if send_index is None else send_index],
            recv_sem=recv_sem.at[index],
            device_id=device,
            device_id_type=MESH_ID,
        )

    def send(index, src, dst, device, send_index=None, when=None):
        copy = copy_of(index, src, dst, device, send_index)
        if when is None:
            copy.start()
        else:
            pl.when(when)(copy.start)
        pending.append((copy, when))
        return copy, when

    def arrived(index, dst, when=None):
        copy = copy_of(index, dst, dst, dev_c)
        if when is None:
            copy.wait_recv()
        else:
            pl.when(when)(copy.wait_recv)

    def sent(started):
        copy, when = started
        if when is None:
            copy.wait_send()
        else:
            pl.when(when)(copy.wait_send)
        pending[:] = [other for other in pending if other[0] is not copy]

    def local(src, dst):
        copy = pltpu.make_async_copy(src, dst, local_sem.at[locals_used.take()])
        copy.start()
        return copy

    barrier = pltpu.get_barrier_semaphore()
    partners = [dev_x, dev_y, dev_d] + [(row, lax.rem(col + step, 8)) for step in range(1, 8)]
    for device in partners:
        pl.semaphore_signal(barrier, inc=1, device_id=device, device_id_type=MESH_ID)

    @pl.when(at_end)
    def _():
        land_r[...] = jnp.zeros_like(land_r)
        land_z[0] = jnp.zeros_like(land_z[0])

    small_copies = [
        local(query_gain_hbm, query_gain_ref),
        local(key_gain_hbm, key_gain_ref),
        local(attn_gain_hbm, attn_gain_ref),
        local(mlp_gain_hbm, mlp_gain_ref),
    ]
    pos_copy = local(pos_hbm, pos_ref)
    half_mine = aligned(y_at * FH, FH)
    half_other = aligned((1 - y_at) * FH, FH)
    rows_mine = aligned(row * DR, DR)
    local_copies = [local(x_hbm, x_full.at[:, aligned(col * DC, DC)]), local(cot_hbm, cot_z.at[z_at])]
    for index, ref in enumerate((wq_hbm, wk_hbm, wv_hbm)):
        local_copies.append(local(ref, wqkv.at[rows_mine, pl.ds(index * DC, DC)]))
    local_copies.append(local(wo_hbm, wo.at[rows_mine, :]))
    local_copies.append(local(wg_hbm.at[:, half_mine], wgu.at[rows_mine, pl.ds(0, FH)]))
    local_copies.append(local(wu_hbm.at[:, half_mine], wgu.at[rows_mine, pl.ds(FH, FH)]))
    local_copies.append(local(wd_hbm.at[:, half_mine], wd.at[rows_mine, :]))
    pl.semaphore_wait(barrier, len(partners))

    def own_rows(half, plane):
        if plane:
            return aligned(half * 2 * HT + y_at * HT, HT)
        return pl.ds(half * HT, HT)

    def other_rows(half):
        return aligned(half * 2 * HT + (1 - y_at) * HT, HT)

    def half_rows(half, plane):
        count = 2 * HT if plane else HT
        return pl.ds(half * count, count)

    def tokens(half):
        return pl.ds(half * HT, HT)

    gather_base = counter.take(2 * 16)
    gather_sends = ([], [])

    class Gather:
        def __init__(self, buf, plane, raw, process, half):
            self.buf = buf
            self.plane = plane
            self.raw = raw
            self.process = process
            self.half = half
            self.base_z = gather_base + 16 * half
            self.relay = self.base_z + 3
            self.base_c = self.base_z + 4
            self.base_y = self.base_z + 8
            self.base_cy = self.base_z + 12
            self.rows = own_rows(half, plane)
            if plane:
                self.rows_other = other_rows(half)

        def block(self, rows, place, parity=None):
            at = 2 * place + (core if parity is None else parity)
            return rows, aligned(at * DC, DC)

        def start(self):
            self.finish_sends()
            own = self.raw.at[z_at, tokens(self.half)]
            for pair in (2, 3, 1):
                when = middle if pair == 3 else None
                self.send(self.base_z + pair - 1, own, own, dev_z[pair], None, when)

        def send(self, *copy):
            gather_sends[self.half].append(send(*copy))

        def pass_on(self, *pairs):
            for pair in pairs:
                place = z_pair[pair]
                if pair:
                    raw = self.raw.at[place, tokens(self.half)]
                    arrived(self.base_z + pair - 1, raw)
                if pair == 2:
                    self.send(self.base_z + 2, raw, raw, dev_z[1], self.relay, middle)
                where = self.block(self.rows, place)
                self.buf[where] = self.process(pair, place, self.half)
                block = self.buf.at[where]
                if self.plane:
                    self.send(self.base_y + pair, block, block, dev_y)
                self.send(self.base_c + pair, block, block, dev_c)

        def finish_own(self):
            for pair in range(4):
                arrived(
                    self.base_c + pair, self.buf.at[self.block(self.rows, z_pair[pair], 1 - core)]
                )

        def finish_sends(self):
            for copy in gather_sends[self.half]:
                sent(copy)
            gather_sends[self.half].clear()

        def finish_other(self):
            for pair in range(4):
                block = self.buf.at[self.block(self.rows_other, z_pair[pair])]
                arrived(self.base_y + pair, block)
                self.send(self.base_cy + pair, block, block, dev_c)
            for pair in range(4):
                arrived(
                    self.base_cy + pair,
                    self.buf.at[self.block(self.rows_other, z_pair[pair], 1 - core)],
                )

    reduce_base = counter.take(2 * 12)
    stage_sends = ([], [])

    class Reduce:
        ORDER = (3, 1, 2, 0)

        def __init__(self, partial, plane, half):
            self.partial = partial
            self.plane = plane
            self.half = half
            self.base_c = reduce_base + 12 * half
            self.base_z = self.base_c + 4
            self.relay = self.base_c + 7
            self.base_y = self.base_c + 8
            self.left = half_rows(half, plane)
            self.all_rows = pl.ds(half * 2 * HT, 2 * HT if plane else HT)
            self.rows = own_rows(half, True) if plane else self.all_rows
            self.tokens = tokens(half)
            if plane:
                self.rows_other = other_rows(half)

        def start(self):
            for copy in stage_sends[self.half]:
                sent(copy)
            stage_sends[self.half].clear()
            rows = self.all_rows
            for slot, pair in enumerate(self.ORDER):
                target = z_pair[pair]
                start = pl.multiple_of((2 * target + 1 - core) * DC, DC)
                stage_c[slot, rows, :] = self.partial(self.left, start).astype(BF)
                self.send(
                    self.base_c + slot, stage_c.at[slot, rows, :], land_c.at[slot, rows, :], dev_c
                )
                start = pl.multiple_of((2 * target + core) * DC, DC)
                own_s[slot, rows, :] = self.partial(self.left, start)
                if slot:
                    self.cores(slot - 1)
            self.cores(3)

        def send(self, *copy):
            stage_sends[self.half].append(send(*copy))

        def cores(self, slot):
            arrived(self.base_c + slot, land_c.at[slot, self.all_rows, :])
            if self.plane:
                rows = self.rows_other
                stage_y[slot, self.tokens, :] = (
                    own_s[slot, rows, :] + land_c[slot, rows, :].astype(F32)
                ).astype(BF)
                self.send(
                    self.base_y + slot,
                    stage_y.at[slot, self.tokens],
                    land_y.at[slot, self.tokens],
                    dev_y,
                )
                rows = self.rows
                own_s[slot, rows, :] = own_s[slot, rows, :] + land_c[slot, rows, :].astype(F32)
            else:
                self.pass_on(slot, land_c.at[slot, self.rows, :])

        def pass_on(self, slot, landed):
            pair = self.ORDER[slot]
            total = own_s[slot, self.rows, :] + landed[...].astype(F32)
            if pair == 0:
                own_s[slot, self.rows, :] = total
                return
            if pair == 2:
                arrived(self.relay, land_r.at[self.tokens], middle)
                total = total + land_r[self.tokens, :].astype(F32)
            stage_z[slot, self.tokens, :] = total.astype(BF)
            stage, land = stage_z.at[slot, self.tokens], land_z.at[slot, self.tokens]
            if pair == 3:
                index = self.base_z + slot
                self.send(index, stage, land, dev_z[3], None, middle)
                self.send(self.relay, stage, land_r.at[self.tokens], dev_z[1], None, at_end)
            else:
                self.send(self.base_z + slot, stage, land, dev_z[pair])

        def planes(self, *slots):
            for slot in slots:
                landed = land_y.at[slot, self.tokens]
                arrived(self.base_y + slot, landed)
                self.pass_on(slot, landed)

        def finish(self):
            for slot in range(3):
                when = middle if self.ORDER[slot] == 3 else None
                arrived(self.base_z + slot, land_z.at[slot, self.tokens], when)
            total = own_s[3, self.rows, :]
            for slot in range(3):
                total = total + land_z[slot, self.tokens, :].astype(F32)
            return total

    pick = lax.broadcasted_iota(jnp.int32, (8, DC), 0)
    lane = lax.broadcasted_iota(jnp.int32, (8, DC), 1)
    first_row = (pick == 0).astype(F32)
    second_row = (pick == 1).astype(F32)
    spread = ((pick == 0) & (lane < 128)).astype(F32) + ((pick == 1) & (lane >= 128)).astype(F32)
    scal_base = counter.take(4 * 7)
    scal_sends = ([], [], [], [])

    def scal_send(stage, half, first, second=None):
        mine = dot_nt(first_row, first, EXACT)
        if second is not None:
            mine = mine + dot_nt(second_row, second, EXACT)
        place = scal_s.at[stage, half, col]
        place[...] = mine
        turn = 2 * half + stage % 2
        for copy in scal_sends[turn]:
            sent(copy)
        scal_sends[turn].clear()
        for step in range(1, 8):
            index = scal_base + 7 * turn + step - 1
            scal_sends[turn].append(send(index, place, place, (row, lax.rem(col + step, 8))))

    def scal_get(stage, half):
        for step in range(1, 8):
            index = scal_base + 7 * (2 * half + stage % 2) + step - 1
            arrived(index, scal_s.at[stage, half, lax.rem(col + 8 - step, 8)])
        total = scal_s[stage, half, 0]
        for index in range(1, 8):
            total = total + scal_s[stage, half, index]
        both = dot_tn(total, spread, EXACT)
        return both[:, :128], both[:, 128:]

    HALVES = (0, 1)

    def wide(values):
        return jnp.concatenate([values, values], axis=1)

    attn_base = counter.take(16)
    weight_sends = []
    attn_hbm = (wq_hbm, wk_hbm, wv_hbm, wo_hbm)

    def attn_place(index, owner, part=None):
        if part is None:
            rows = aligned(owner * DR, DR)
        else:
            rows = aligned(owner * DR + part * (DR // 2), DR // 2)
        if index < 3:
            return wqkv.at[rows, pl.ds(index * DC, DC)]
        return wo.at[rows, :]

    def weight_send(*copy):
        weight_sends.append(send(*copy))

    def attn_send(index):
        weight_send(attn_base + index, attn_hbm[index], attn_place(index, row), dev_x)
        weight_send(attn_base + 4 + index, attn_hbm[index], attn_place(index, row), dev_y)

    def attn_relay(index):
        arrived(attn_base + index, attn_place(index, row_x))
        part = attn_place(index, row_x, 0 if index < 2 else None)
        weight_send(attn_base + 8 + index, part, part, dev_y)
        arrived(attn_base + 4 + index, attn_place(index, row_y))
        if index < 2:
            part = attn_place(index, row_y, 1)
            weight_send(attn_base + 12 + index, part, part, dev_x)

    def attn_ready(index):
        arrived(attn_base + 8 + index, attn_place(index, row_d, 0 if index < 2 else None))
        if index < 2:
            arrived(attn_base + 12 + index, attn_place(index, row_d, 1))

    mlp_base = counter.take(9)
    mlp_hbm = (wg_hbm, wu_hbm, wd_hbm)

    def mlp_place(index, owner):
        rows = aligned(owner * DR, DR)
        if index < 2:
            return wgu.at[rows, pl.ds(index * FH, FH)]
        return wd.at[rows, :]

    def mlp_send(index):
        weight_send(mlp_base + index, mlp_hbm[index].at[:, half_mine], mlp_place(index, row), dev_x)
        weight_send(mlp_base + 3 + index, mlp_hbm[index].at[:, half_other], mlp_place(index, row), dev_y)

    def mlp_relay(index):
        place = mlp_place(index, row_y)
        arrived(mlp_base + 3 + index, place)
        weight_send(mlp_base + 6 + index, place, place, dev_x)

    def mlp_ready(index):
        arrived(mlp_base + index, mlp_place(index, row_x))
        arrived(mlp_base + 6 + index, mlp_place(index, row_d))

    for index in range(2):
        attn_send(index)

    x_base = counter.take(7)
    cot_base = counter.take(3)

    def x_block(place, parity):
        return x_full.at[:, aligned((2 * place + parity) * DC, DC)]

    for pair in (2, 3, 1):
        send(x_base + pair - 1, x_hbm, x_block(z_at, core), dev_z[pair])
    send(x_base + 3, x_hbm, x_block(z_at, core), dev_c)

    pos_copy.wait()
    position_rows = jnp.broadcast_to(pos_ref[...].astype(F32), (8, T))
    position = dot_tn(position_rows, first_row[:, :HD], EXACT)
    pos_s[...] = position.astype(jnp.int32)
    lane_at = lax.broadcasted_iota(jnp.int32, (1, HD), 1)
    within = lax.rem(lane_at, HD // 2).astype(F32)
    frequency = jnp.exp(within * (-2.0 * math.log(THETA) / HD))
    angles = position * frequency
    cos_s[...] = jnp.cos(angles)
    sine = jnp.sin(angles)
    sin_s[...] = jnp.where(lane_at < HD // 2, -sine, sine)

    for index in range(2):
        attn_relay(index)
    attn_send(2)
    attn_send(3)
    for pair in (2, 1, 3):
        block = x_block(z_pair[pair], core)
        arrived(x_base + pair - 1, block)
        send(x_base + 3 + pair, block, block, dev_c)
    for copy in local_copies + small_copies:
        copy.wait()
    for pair in range(4):
        arrived(x_base + 3 + pair, x_block(z_pair[pair], 1 - core))
    attn_ready(0)
    attn_ready(1)

    def gain_at(ref, at):
        return ref[:, aligned(at * DC, DC)]

    qk_gain = (gain_at(query_gain_ref, col), gain_at(key_gain_ref, col))
    for index in range(2):
        hat_s[index] = dot_nn(x_full[...], wqkv[:, pl.ds(index * DC, DC)])
    for half in HALVES:
        query, key = hat_s[0, tokens(half), :], hat_s[1, tokens(half), :]
        scal_send(0, half, query * query, key * key)
    for pair in (2, 3, 1):
        weight_send(cot_base + pair - 1, cot_z.at[z_at], cot_z.at[z_at], dev_z[pair])
    attn_relay(2)
    attn_relay(3)
    for index in range(3):
        mlp_send(index)
    attn_ready(2)
    low_s[2] = dot_nn(x_full[...], wqkv[:, pl.ds(2 * DC, DC)]).astype(BF)
    for half in HALVES:
        scales = [lax.rsqrt(total / D + EPS) for total in scal_get(0, half)]
        rows = tokens(half)
        work_s[0, rows, :] = jnp.concatenate(scales, axis=1)
        for index in range(2):
            hat = hat_s[index, rows, :] * wide(scales[index])
            hat_s[index, rows, :] = hat
            normed = hat * qk_gain[index]
            for head in range(2):
                part = normed[:, head * HD : (head + 1) * HD]
                turned = part * cos_s[rows, :] + pltpu.roll(part, HD // 2, 1) * sin_s[rows, :]
                if index == 0:
                    turned = turned * (HD**-0.5)
                low_s[index, rows, pl.ds(head * HD, HD)] = turned.astype(BF)

    chunk = 128

    def attend(half):
        count = (half + 1) * HT
        keys = pl.ds(0, count)

        def attend_chunk(at, carry):
            rows = aligned(at * chunk, chunk)
            query = at * chunk + lax.broadcasted_iota(jnp.int32, (chunk, count), 0)
            key = lax.broadcasted_iota(jnp.int32, (chunk, count), 1)
            oldest = query - pos_s[rows, :1]
            allowed = (key <= query) & (key >= oldest)
            for head in range(2):
                lanes = pl.ds(head * HD, HD)
                scores = dot_nt(low_s[0, rows, lanes], low_s[1, keys, lanes])
                scores = jnp.where(allowed, scores, MASKED)
                exponent = jnp.exp(scores - jnp.max(scores, axis=1, keepdims=True))
                probs = exponent / jnp.sum(exponent, axis=1, keepdims=True)
                probs_s[head, rows, keys] = probs
                att_s[rows, lanes] = dot_nn(probs.astype(BF), low_s[2, keys, lanes]).astype(BF)
            return carry

        first = half * (HT // chunk)
        lax.fori_loop(first, first + HT // chunk, attend_chunk, 0)

    branch_sums = [
        Reduce(
            lambda rows, start: dot_nt(att_s[rows, :], wo[pl.ds(start, DC), :]), False, half
        )
        for half in HALVES
    ]

    def middle_block(pair, place, half):
        rows = tokens(half)
        at = 2 * place + core
        raw = work_s[1, rows, :] if pair == 0 else braw_s[place, rows, :].astype(F32)
        hat = raw * wide(work_s[2, rows, :128])
        inputs = x_full[rows, aligned(at * DC, DC)].astype(F32)
        middle = inputs + hat * gain_at(attn_gain_ref, at)
        if pair == 0:
            bhat_s[rows, :] = hat
            middle_s[rows, :] = middle
        return middle.astype(BF)

    mid_gathers = [Gather(mid_full, True, braw_s, middle_block, half) for half in HALVES]

    def branch_done(half):
        rows = tokens(half)
        branch = branch_sums[half].finish()
        scal_send(1, half, branch * branch)
        work_s[1, rows, :] = branch
        braw_s[z_at, rows, :] = branch.astype(BF)
        mid_gathers[half].start()

    def branch_scaled(half):
        total, _ = scal_get(1, half)
        work_s[2, tokens(half), :128] = lax.rsqrt(total / D + EPS)

    attend(0)
    attn_ready(3)
    branch_sums[0].start()
    attend(1)
    branch_sums[1].start()
    mlp_relay(0)
    branch_done(0)
    mlp_relay(1)
    branch_scaled(0)
    mid_gathers[0].pass_on(0)
    branch_done(1)
    mlp_relay(2)
    mid_gathers[0].pass_on(2, 1, 3)
    branch_scaled(1)
    mid_gathers[1].pass_on(0)
    mid_gathers[1].pass_on(2, 1, 3)
    mid_gathers[0].finish_own()
    mid_gathers[0].finish_other()
    mlp_ready(0)
    mlp_ready(1)

    tile = 256

    def forward_tiles(half):
        rows = half_rows(half, True)

        def forward_tile(at, carry):
            lanes = aligned(at * tile, tile)
            lanes_up = aligned(at * tile + FH, tile)
            gate = dot_nn(mid_full[rows, :], wgu[:, lanes])
            up = dot_nn(mid_full[rows, :], wgu[:, lanes_up])
            gu_s[rows, lanes] = gate.astype(BF)
            gu_s[rows, lanes_up] = up.astype(BF)
            mixed_s[rows, lanes] = (gate * jax.nn.sigmoid(gate) * up).astype(BF)
            return carry

        lax.fori_loop(0, FH // tile, forward_tile, 0)

    ffn_sums = [
        Reduce(
            lambda rows, start: dot_nt(mixed_s[rows, :], wd[pl.ds(start, DC), :]), True, half
        )
        for half in HALVES
    ]
    mlp_gain = gain_at(mlp_gain_ref, col)

    def grad_ffn_block(pair, place, half):
        rows = tokens(half)
        at = 2 * place + core
        raw = work_s[1, rows, :] if pair == 0 else raw_s[place, rows, :].astype(F32)
        scale = wide(work_s[2, rows, 128:])
        grad = cot_z[place, rows, :].astype(F32) * gain_at(mlp_gain_ref, at)
        return (scale * (grad - raw * scale * wide(inner_s[rows, :]))).astype(BF)

    gf_gathers = [Gather(gf_full, True, raw_s, grad_ffn_block, half) for half in HALVES]

    def ffn_done(half):
        rows = tokens(half)
        ffn = ffn_sums[half].finish()
        cot = cot_z[z_at, rows, :].astype(F32)
        scal_send(2, half, ffn * ffn, cot * mlp_gain * ffn)
        work_s[1, rows, :] = ffn
        raw_s[z_at, rows, :] = ffn.astype(BF)
        gf_gathers[half].start()

    def ffn_scaled(half):
        rows = tokens(half)
        total, inner = scal_get(2, half)
        scale = lax.rsqrt(total / D + EPS)
        work_s[2, rows, 128:] = scale
        inner_s[rows, :] = inner * scale / D

    forward_tiles(0)
    mlp_ready(2)
    ffn_sums[0].start()
    mid_gathers[1].finish_own()
    mid_gathers[1].finish_other()
    forward_tiles(1)
    ffn_sums[0].planes(0, 1)
    ffn_sums[1].start()
    ffn_sums[0].planes(2, 3)
    ffn_sums[1].planes(0, 1)
    for pair in (1, 2, 3):
        arrived(cot_base + pair - 1, cot_z.at[z_pair[pair]])
    ffn_done(0)
    ffn_sums[1].planes(2, 3)
    ffn_scaled(0)
    gf_gathers[0].pass_on(0)
    ffn_done(1)
    gf_gathers[0].pass_on(2, 1, 3)
    ffn_scaled(1)
    gf_gathers[1].pass_on(0, 2, 1, 3)
    ffn_hat = work_s[1] * wide(work_s[2, :, 128:])
    out_lo[...] = (middle_s[...] + ffn_hat * mlp_gain).astype(BF)
    gain_s[row, 3:4, :] = jnp.sum(cot_z[z_at].astype(F32) * ffn_hat, axis=0, keepdims=True)
    lo_copy = local(out_lo, layer_out)
    gf_gathers[0].finish_own()
    gf_gathers[0].finish_other()

    def backward_tiles(half):
        rows = half_rows(half, True)

        def backward_tile(at, carry):
            lanes = aligned(at * tile, tile)
            lanes_up = aligned(at * tile + FH, tile)
            grad_mixed = dot_nn(gf_full[rows, :], wd[:, lanes])
            gate = gu_s[rows, lanes].astype(F32)
            up = gu_s[rows, lanes_up].astype(F32)
            sigma = jax.nn.sigmoid(gate)
            gu_s[rows, lanes] = (grad_mixed * up * sigma * (1.0 + gate * (1.0 - sigma))).astype(BF)
            gu_s[rows, lanes_up] = (grad_mixed * gate * sigma).astype(BF)
            return carry

        lax.fori_loop(0, FH // tile, backward_tile, 0)

    def lanes_of(owner):
        return aligned(owner * DR, DR)

    def down_piece(owner):
        return dot_tn(gf_full[:, lanes_of(owner)], mixed_s[...])

    def gu_piece(owner, part):
        return dot_tn(mid_full[:, lanes_of(owner)], gu_s[:, pl.ds(part * FH, FH)])

    grad_base = counter.take(9)
    grad_sends = {}

    def grad_lanes(part):
        return pl.ds(part * FH, FH)

    def grad_stage(slot, part):
        if part == 2:
            return stage_down.at[slot]
        return stage_gu.at[slot, :, grad_lanes(part)]

    def grad_piece(slot, part, more=None):
        owner = (row_d, row_x, row_y, row)[slot]
        total = down_piece(owner) if part == 2 else gu_piece(owner, part)
        if more is not None:
            total = total + more
        grad_stage(slot, part)[...] = total.astype(BF)

    def grad_send(slot, part, landing, device):
        index = grad_base + 3 * slot + part
        grad_sends[slot, part] = send(index, grad_stage(slot, part), landing, device)

    def grad_diagonal(part):
        grad_piece(0, part)
        grad_send(0, part, rel_mlp.at[:, grad_lanes(part)], dev_x)

    def grad_near(part):
        grad_piece(1, part)
        grad_send(1, part, land_mlp.at[1, :, grad_lanes(part)], dev_x)

    def grad_relay(part):
        arrived(grad_base + part, rel_mlp.at[:, grad_lanes(part)])
        grad_piece(2, part, rel_mlp[:, grad_lanes(part)].astype(F32))
        grad_send(2, part, land_mlp.at[2, :, grad_lanes(part)], dev_y)

    mid_sums = [
        Reduce(lambda rows, start: dot_nt(gu_s[rows, :], wgu[pl.ds(start, DC), :]), True, half)
        for half in HALVES
    ]
    attn_gain = gain_at(attn_gain_ref, col)

    def grad_branch_block(pair, place, half):
        rows = tokens(half)
        at = 2 * place + core
        scale = wide(work_s[2, rows, :128])
        raw = middle_s[rows, :] if pair == 0 else raw_s[place, rows, :].astype(F32)
        hat = bhat_s[rows, :] if pair == 0 else braw_s[place, rows, :].astype(F32) * scale
        inner = wide(inner_s[rows, :])
        return (scale * (raw * gain_at(attn_gain_ref, at) - hat * inner)).astype(BF)

    gb_gathers = [Gather(gb_full, False, raw_s, grad_branch_block, half) for half in HALVES]

    def mid_done(half):
        rows = tokens(half)
        grad_middle = cot_z[z_at, rows, :].astype(F32) + mid_sums[half].finish()
        scal_send(3, half, grad_middle * attn_gain * bhat_s[rows, :])
        middle_s[rows, :] = grad_middle
        raw_s[z_at, rows, :] = grad_middle.astype(BF)
        gb_gathers[half].start()

    def mid_scaled(half):
        inner, _ = scal_get(3, half)
        inner_s[tokens(half), :] = inner / D

    def attend_back(half):
        count = (half + 1) * HT
        keys = pl.ds(0, count)

        def attend_back_chunk(at, carry):
            rows = aligned(at * chunk, chunk)
            for head in range(2):
                lanes = pl.ds(head * HD, HD)
                grad_probs = dot_nt(ga_s[rows, lanes], low_s[2, keys, lanes])
                probs = probs_s[head, rows, keys]
                inner = jnp.sum(probs * grad_probs, axis=1, keepdims=True)
                grad_scores = (probs * (grad_probs - inner)).astype(BF)
                gs_s[head, rows, keys] = grad_scores
                gqk_s[0, rows, lanes] = dot_nn(grad_scores, low_s[1, keys, lanes])
            return carry

        first = half * (HT // chunk)
        lax.fori_loop(first, first + HT // chunk, attend_back_chunk, 0)

    backward_tiles(0)
    gf_gathers[0].finish_sends()
    mid_sums[0].start()
    gf_gathers[1].finish_own()
    gf_gathers[1].finish_other()
    grad_diagonal(2)
    backward_tiles(1)
    gf_gathers[1].finish_sends()
    mid_sums[1].start()
    grad_diagonal(0)
    grad_diagonal(1)
    mid_sums[0].planes(0, 1, 2, 3)
    grad_relay(2)
    mid_sums[1].planes(0, 1)
    mid_done(0)
    mid_sums[1].planes(2, 3)
    grad_relay(0)
    grad_near(2)
    mid_scaled(0)
    gb_gathers[0].pass_on(0)
    mid_done(1)
    grad_relay(1)
    grad_near(0)
    gb_gathers[0].pass_on(2, 1, 3)
    mid_scaled(1)
    gb_gathers[1].pass_on(0)
    grad_near(1)
    late = []
    gb_gathers[0].finish_own()
    ga_s[tokens(0), :] = dot_nn(gb_full[tokens(0), :], wo[...]).astype(BF)
    gb_gathers[1].pass_on(2, 1, 3)
    attend_back(0)
    gain_s[row, 2:3, :] = jnp.sum(middle_s[...] * bhat_s[...], axis=0, keepdims=True)
    gb_gathers[1].finish_own()

    ga_s[tokens(1), :] = dot_nn(gb_full[tokens(1), :], wo[...]).astype(BF)

    whole = pl.ds(0, DR)
    upper = pl.ds(0, DR // 2)
    lower = pl.ds(DR // 2, DR // 2)
    BY_Y = ((whole, 2),)
    BY_BOTH = ((upper, 1), (lower, 2))
    neighbours = {1: dev_x, 2: dev_y}
    attn_grad_base = counter.take(3 * 6)

    class AttnGrad:
        def __init__(self, order, routes, left, right, start, size):
            self.base = attn_grad_base + 6 * order
            self.routes = routes
            self.left, self.right = left, right
            self.start_lane, self.size = start, size
            self.lanes = pl.ds(start, size)

        def at(self, slot, rows):
            rows = pl.ds(slot // 2 * DR + rows.start, rows.size)
            return gf_full.at[rows, pl.ds(slot % 2 * 4 * DC + self.start_lane, self.size)]

        def piece(self, slot):
            owner = (row_d, row_x, row_y, row)[slot]
            piece = dot_tn(self.left[:, lanes_of(owner)], self.right())
            self.at(slot, whole)[...] = piece.astype(BF)

        def diagonal(self):
            self.piece(0)
            for step, (rows, first) in enumerate(self.routes):
                landing = rel_attn.at[rows, self.lanes]
                send(self.base + step, self.at(0, rows), landing, neighbours[first])

        def near(self):
            self.piece(1)
            self.piece(2)
            for step, (rows, first) in enumerate(self.routes):
                landing = land_attn.at[first, rows, self.lanes]
                send(self.base + 2 + step, self.at(first, rows), landing, neighbours[first])

        def own(self):
            self.piece(3)
            late.append(local(self.at(3, whole), land_attn.at[0, :, self.lanes]))

        def relay(self):
            for step, (rows, first) in enumerate(self.routes):
                slot = 3 - first
                arrived(self.base + step, rel_attn.at[rows, self.lanes])
                stage = self.at(slot, rows)
                stage[...] = (
                    stage[...].astype(F32) + rel_attn[rows, self.lanes].astype(F32)
                ).astype(BF)
                landing = land_attn.at[slot, rows, self.lanes]
                send(self.base + 4 + step, stage, landing, neighbours[slot])

        def finish(self):
            for step, (rows, first) in enumerate(self.routes):
                arrived(self.base + 2 + step, land_attn.at[first, rows, self.lanes])
                arrived(self.base + 4 + step, land_attn.at[3 - first, rows, self.lanes])

    grad_piece(3, 2)
    late.append(local(stage_down.at[3], land_mlp.at[0, :, grad_lanes(2)]))
    for gather in gf_gathers:
        gather.finish_sends()
    o_grad = AttnGrad(0, BY_BOTH, gb_full, lambda: att_s[...], 3 * DC, DC)
    o_grad.diagonal()
    o_grad.near()

    attend_back(1)
    early, last = pl.ds(0, HT), pl.ds(HT, HT)
    for head in range(2):
        lanes = pl.ds(head * HD, HD)
        gqk_s[1, early, lanes] = dot_tn(gs_s[head, :, early], low_s[0, :, lanes])
        gqk_s[1, last, lanes] = dot_tn(gs_s[head, last, last], low_s[0, last, lanes])
    inners = []
    for index in range(2):
        for head in range(2):
            lanes = pl.ds(head * HD, HD)
            part = gqk_s[index, :, lanes]
            turned = part * cos_s[...] - pltpu.roll(part, HD // 2, 1) * sin_s[...]
            if index == 0:
                turned = turned * (HD**-0.5)
            gqk_s[index, :, lanes] = turned
        weighted = gqk_s[index] * hat_s[index]
        gain_s[row, index : index + 1, :] = jnp.sum(weighted, axis=0, keepdims=True)
        inners.append(weighted * qk_gain[index])
    for half in HALVES:
        part = slice(half * HT, (half + 1) * HT)
        scal_send(4, half, inners[0][part], inners[1][part])
    gain_base = counter.take(3)
    for slot, device in enumerate((dev_x, dev_y, dev_d)):
        send(gain_base + slot, gain_s.at[row], gain_s.at[row], device)
    for head in range(2):
        lanes = pl.ds(head * HD, HD)
        out_lanes = pl.ds(2 * DC + head * HD, HD)
        gqkv_s[early, out_lanes] = dot_tn(
            probs_s[head, :, early].astype(BF), ga_s[:, lanes]
        ).astype(BF)
        gqkv_s[last, out_lanes] = dot_tn(
            probs_s[head, last, last].astype(BF), ga_s[last, lanes]
        ).astype(BF)
    v_grad = AttnGrad(1, BY_BOTH, x_full, lambda: gqkv_s[:, 2 * DC :], 2 * DC, DC)
    v_grad.diagonal()
    v_grad.near()
    for half in HALVES:
        rows = tokens(half)
        totals = scal_get(4, half)
        for index in range(2):
            scale = wide(work_s[0, rows, index * 128 : (index + 1) * 128])
            gqkv_s[rows, pl.ds(index * DC, DC)] = (
                scale
                * (
                    gqk_s[index, rows, :] * qk_gain[index]
                    - hat_s[index, rows, :] * wide(totals[index] / D)
                )
            ).astype(BF)
    in_sums = [
        Reduce(
            lambda rows, start: dot_nt(gqkv_s[rows, :], wqkv[pl.ds(start, DC), :]), False, half
        )
        for half in HALVES
    ]
    qk_grad = AttnGrad(2, BY_BOTH, x_full, lambda: gqkv_s[:, : 2 * DC], 0, 2 * DC)
    qk_grad.diagonal()
    in_sums[0].start()
    qk_grad.near()
    in_sums[1].start()
    o_grad.relay()
    v_grad.relay()
    qk_grad.relay()
    for grad in (o_grad, v_grad, qk_grad):
        grad.own()
    grad_piece(3, 0)
    grad_piece(3, 1)
    late.append(local(stage_gu.at[3], land_mlp.at[0, :, pl.ds(0, 2 * FH)]))
    for half in HALVES:
        rows = tokens(half)
        work_s[1, rows, :] = middle_s[rows, :] + in_sums[half].finish()
    late.append(local(work_s.at[1], grad_in))
    late.append(lo_copy)

    for slot, owner in enumerate((row_x, row_y, row_d)):
        arrived(gain_base + slot, gain_s.at[owner])
    gains_out[...] = gain_s[0] + gain_s[1] + gain_s[2] + gain_s[3]
    for slot in (1, 2):
        for part in range(3):
            arrived(grad_base + 3 * slot + part, land_mlp.at[slot, :, grad_lanes(part)])
    for grad in (o_grad, v_grad, qk_grad):
        grad.finish()
    for copy in late:
        copy.wait()
    for copy in list(pending):
        sent(copy)
    assert counter.used <= send_sem.shape[0], counter.used


def total_kernel(
    lo_ref, gin_ref, gains_ref, mlp_ref, attn_ref, lo_out, gin_out, *outs
):
    y_at = lax.div(lax.axis_index("row"), 2)
    lo_out[...] = lo_ref[...]
    gin_out[...] = gin_ref[...]
    attn = attn_ref[0].astype(F32) + attn_ref[1].astype(F32) + attn_ref[2].astype(F32)
    for index in range(4):
        outs[index][...] = attn[:, index * DC : (index + 1) * DC]
    mine = mlp_ref[0].astype(F32) + mlp_ref[1].astype(F32)
    other = mlp_ref[2].astype(F32)
    for index in range(3):
        lanes = slice(index * FH, (index + 1) * FH)
        outs[4 + index][:, aligned(y_at * FH, FH)] = mine[:, lanes]
        outs[4 + index][:, aligned((1 - y_at) * FH, FH)] = other[:, lanes]
    for index in range(4):
        outs[7 + index][...] = gains_ref[index : index + 1, :]


MIB = 1 << 20


def on_device_kernel(
    inputs,
    query_weight,
    key_weight,
    value_weight,
    output_weight,
    gate_weight,
    up_weight,
    down_weight,
    query_gain,
    key_gain,
    attn_gain,
    mlp_gain,
    positions,
    segments,
    cotangent,
):
    hbm = pl.BlockSpec(memory_space=pl.ANY)
    vmem = pl.BlockSpec(memory_space=pltpu.VMEM)
    sds = jax.ShapeDtypeStruct
    copies = 150
    landed = pl.pallas_call(
        block_kernel,
        out_shape=[
            sds((T, DC), BF),
            sds((T, DC), F32),
            sds((8, DC), F32),
            sds((3, DR, 3 * FH), BF),
            sds((3, DR, 4 * DC), BF),
        ],
        in_specs=[hbm] * 14,
        out_specs=[hbm, hbm, vmem, hbm, hbm],
        scratch_shapes=[
            pltpu.VMEM((D, 3 * DC), BF),
            pltpu.VMEM((D, DC), BF),
            pltpu.VMEM((D, 2 * FH), BF),
            pltpu.VMEM((D, FH), BF),
            pltpu.VMEM((T, D), BF),
            pltpu.VMEM((2 * T, D), BF),
            pltpu.VMEM((2 * T, D), BF),
            pltpu.VMEM((T, D), BF),
            pltpu.VMEM((2 * T, 2 * FH), BF),
            pltpu.VMEM((2 * T, FH), BF),
            pltpu.VMEM((2, T, T), F32),
            pltpu.VMEM((2, T, DC), F32),
            pltpu.VMEM((3, T, DC), BF),
            pltpu.VMEM((T, HD), F32),
            pltpu.VMEM((T, HD), F32),
            pltpu.VMEM((T, HD), jnp.int32),
            pltpu.VMEM((4, T, DC), BF),
            pltpu.VMEM((4, T, DC), BF),
            pltpu.VMEM((4, T, DC), BF),
            pltpu.VMEM((T, DC), F32),
            pltpu.VMEM((T, DC), F32),
            pltpu.VMEM((3, T, DC), F32),
            pltpu.VMEM((T, HD), F32),
            pltpu.VMEM((T, DC), BF),
            pltpu.VMEM((T, DC), BF),
            pltpu.VMEM((T, 3 * DC), BF),
            pltpu.VMEM((2, T, T), BF),
            pltpu.VMEM((2, T, DC), F32),
            pltpu.VMEM((4, 2 * T, DC), F32),
            pltpu.VMEM((4, 2 * T, DC), BF),
            pltpu.VMEM((4, 2 * T, DC), BF),
            pltpu.VMEM((4, T, DC), BF),
            pltpu.VMEM((4, T, DC), BF),
            pltpu.VMEM((3, T, DC), BF),
            pltpu.VMEM((3, T, DC), BF),
            pltpu.VMEM((T, DC), BF),
            pltpu.VMEM((LAYER_STAGES, 2, 8, 8, HT), F32),
            pltpu.VMEM((4, 8, DC), F32),
            pltpu.VMEM((4, DR, FH), BF),
            pltpu.VMEM((4, DR, 2 * FH), BF),
            pltpu.VMEM((DR, 3 * FH), BF),
            pltpu.VMEM((DR, 4 * DC), BF),
            pltpu.VMEM((T, DC), BF),
            pltpu.VMEM((1, D), F32),
            pltpu.VMEM((1, D), F32),
            pltpu.VMEM((1, D), F32),
            pltpu.VMEM((1, D), F32),
            pltpu.VMEM((1, T), jnp.int32),
            pltpu.SemaphoreType.DMA((copies,)),
            pltpu.SemaphoreType.DMA((copies,)),
            pltpu.SemaphoreType.DMA((24,)),
        ],
        compiler_params=pltpu.CompilerParams(
            collective_id=0, has_side_effects=True, vmem_limit_bytes=64 * MIB
        ),
        cost_estimate=pl.CostEstimate(
            flops=26_800_000_000, bytes_accessed=16_000_000, transcendentals=2_000_000
        ),
    )(
        inputs,
        query_weight,
        key_weight,
        value_weight,
        output_weight,
        gate_weight,
        up_weight,
        down_weight,
        cotangent,
        query_gain[None, :],
        key_gain[None, :],
        attn_gain[None, :],
        mlp_gain[None, :],
        positions[None, :],
    )
    step = 256

    def rows_of(width):
        return pl.BlockSpec((step, width), lambda at: (at, 0))

    gain_spec = pl.BlockSpec((1, DC), lambda at: (0, 0))
    results = pl.pallas_call(
        total_kernel,
        grid=(DR // step,),
        out_shape=[sds((T, DC), BF), sds((T, DC), F32)]
        + [sds((DR, DC), F32)] * 4
        + [sds((DR, 2 * FH), F32)] * 3
        + [sds((1, DC), F32)] * 4,
        in_specs=[
            rows_of(DC),
            rows_of(DC),
            pl.BlockSpec((8, DC), lambda at: (0, 0)),
            pl.BlockSpec((3, step, 3 * FH), lambda at: (0, at, 0)),
            pl.BlockSpec((3, step, 4 * DC), lambda at: (0, at, 0)),
        ],
        out_specs=[rows_of(DC)] * 6 + [rows_of(2 * FH)] * 3 + [gain_spec] * 4,
        compiler_params=pltpu.CompilerParams(vmem_limit_bytes=64 * MIB),
    )(*landed)
    return (*results[:9], *[gain[0] for gain in results[9:]])


def solution(mesh):
    in_specs = (
        P("row", "col"),
        P("row", "col"),
        P("row", "col"),
        P("row", "col"),
        P("row", "col"),
        P("row", "col"),
        P("row", "col"),
        P("row", "col"),
        P(),
        P(),
        P(),
        P(),
        P("row"),
        P("row"),
        P("row", "col"),
    )
    out_specs = (
        P("row", "col"),
        P("row", "col"),
        P("row", "col"),
        P("row", "col"),
        P("row", "col"),
        P("row", "col"),
        P("row", "col"),
        P("row", "col"),
        P("row", "col"),
        P("col"),
        P("col"),
        P("col"),
        P("col"),
    )
    sizes = (mesh.shape["row"], mesh.shape["col"])
    body = on_device_kernel if sizes == (4, 8) else on_device
    return jax.shard_map(
        body, mesh=mesh, in_specs=in_specs, out_specs=out_specs, check_vma=False
    )
```
